32 devices in a mesh: grid: 8 (over z, y), rep: 4 (over x, core).
Axes of the slice: x: 2, y: 2, z: 4, core: 2. Of those that a mesh axis runs over, the one named last changes fastest.
Arguments:
- amplitudes: bfloat16 [256, 30000], P('grid', 'rep'), may hold values from -6 to 6
- coupling: bfloat16 [30000, 28800], P('rep', 'grid'), may hold values from -0.046875 to 0.046875
- integrals: float32 [256, 60, 480], P('grid', 'rep'), may hold values from -6 to 6
- row_energy: float32 [256], P('grid'), may hold values from -4 to -0.8
- occ_energy: float32 [60], P('rep'), may hold values from -2 to -0.4
- vir_energy: float32 [480], replicated, may hold values from 0.2 to 3
- row_irrep: int32 [256], P('grid'), may hold values from 0 to 7, as said below
- occ_irrep: int32 [60], P('rep'), may hold values from 0 to 7
- vir_irrep: int32 [480], replicated, may hold values from 0 to 7
Outputs:
- updated: float32 [256, 60, 480], P('grid', 'rep')
The draws below stay inside these ranges and needn't reach their ends.
Inputs may be any that keep to these rules, and one draw needn't show every extreme that they name: `row_irrep`: in every draw the 32 rows of some index of grid all carry irrep 0.
All inputs are finite; a program needn't handle non-finite values.
Results may differ from the reference program's by a relative error of at most 0.0003.
Values may be sent and summed in bfloat16 or wider, within the bound.
No kernel may reach another device: no remote copies, remote signals or barrier semaphores. Data moves between devices by JAX's collectives and lax.ppermute only.
A program may use at most 192 MiB of HBM per device.

```python
import jax
import jax.numpy as jnp

NOCC = 60
VWIN = 480
ROWS_DEV = 32
SLAB_ROWS = 256
PAIRS_KC = 30000
PAIRS_JB = 28800


def mostly_symmetric(key, count):
    keys = jax.random.split(key, 3)
    chosen = jax.random.randint(keys[0], (count,), 0, 8)
    spread = jax.random.randint(keys[1], (count,), 1, 8)
    labels = jnp.where(chosen == 0, spread, 0).astype(jnp.int32)
    first_spot = jax.random.randint(keys[2], (), 0, count)
    second_spot = (first_spot + 1) % count
    labels = labels.at[first_spot].set(7)
    labels = labels.at[second_spot].set(0)
    return labels.astype(jnp.int32)


def draw_row_irrep(key, part):
    key = jax.random.fold_in(key, 11)
    keys = jax.random.split(key, 4)
    block_count = SLAB_ROWS // ROWS_DEV
    dense_block = jax.random.randint(keys[0], (), 0, block_count)
    level_blocks = jax.random.randint(keys[1], (block_count,), 0, 9)
    level_blocks = jnp.where(jnp.arange(block_count) == dense_block, 8, level_blocks)
    owner_block = jnp.arange(SLAB_ROWS) // ROWS_DEV
    level_rows = level_blocks[owner_block]
    chosen = jax.random.randint(keys[2], (SLAB_ROWS,), 0, 8)
    spread = jax.random.randint(keys[3], (SLAB_ROWS,), 0, 8)
    labels = jnp.where(chosen < level_rows, 0, spread).astype(jnp.int32)
    other_block = (dense_block + 1) % block_count
    labels = labels.at[other_block * ROWS_DEV].set(7)
    return labels.astype(jnp.int32)


def draw_occ_irrep(key, part):
    key = jax.random.fold_in(key, 23)
    return mostly_symmetric(key, NOCC)


def draw_vir_irrep(key, part):
    key = jax.random.fold_in(key, 37)
    return mostly_symmetric(key, VWIN)


def spiked(drawn, own_key, source, target, shards_of, factor):
    owner, partner = [(jnp.arange(drawn.shape[position]) // (drawn.shape[position] // shards_of)).reshape([-1 if axis == position else 1 for axis in range(drawn.ndim)]) for position in (source, target)]
    chosen = jax.random.permutation(own_key, shards_of)[partner]
    strong = (owner == chosen) | (owner == (partner + shards_of // 2) % shards_of)
    return jnp.where(strong, factor * drawn, drawn)


def block_levels(own_key, dims, cuts, low, largest):
    def one(axis_at, parts):
        draws = jax.random.uniform(jax.random.fold_in(jax.random.fold_in(own_key, 6), axis_at), (parts,), jnp.float32, low / len(cuts), largest / len(cuts))
        return jnp.repeat(jnp.exp(draws), dims[axis_at] // parts).reshape((-1,) + (1,) * (len(dims) - axis_at - 1))

    level = one(*cuts[0])
    for cut in cuts[1:]:
        level = level * one(*cut)
    return level


def noise(stream_key, shape, deviation, bound, cuts=(), kind=jnp.bfloat16):
    entries = deviation * jax.random.normal(stream_key, shape, jnp.float32)
    if cuts:
        entries = entries * block_levels(stream_key, shape, cuts, -0.22, 0.18)
    return jnp.clip(entries, -bound, bound).astype(kind)


def noise_with(rng, shape, scale, most, shards, heavy, kind=jnp.bfloat16):
    entries = scale * jax.random.normal(rng, shape, jnp.float32)
    if shards:
        entries = entries * block_levels(rng, shape, shards, -0.22, 0.18)
    return jnp.clip(spiked(entries, jax.random.fold_in(rng, 3), *heavy), -most, most).astype(kind)


def setup_inputs(seed: int = 0) -> dict:
    arg_keys = jax.random.split(jax.random.key(seed), 10)
    return {
        "amplitudes": noise(arg_keys[0], (SLAB_ROWS, PAIRS_KC), 1.0, 6.0, ((0, 8), (1, 4))),
        "coupling": noise_with(arg_keys[1], (PAIRS_KC, PAIRS_JB), PAIRS_KC ** -0.5, 0.046875, ((0, 4), (1, 8)), (0, 1, 8, 2.0)),
        "integrals": noise(arg_keys[2], (SLAB_ROWS, NOCC, VWIN), 1.0, 6.0, ((0, 8), (1, 4)), jnp.float32),
        "row_energy": jnp.clip(-4.0 + 3.2 * jax.random.uniform(arg_keys[3], (SLAB_ROWS,), jnp.float32) ** block_levels(arg_keys[3], (SLAB_ROWS,), ((0, 8),), -0.2, 0.2), -4.0, -0.8),
        "occ_energy": jnp.clip(-2.0 + 1.6 * jax.random.uniform(arg_keys[4], (NOCC,), jnp.float32) ** block_levels(arg_keys[4], (NOCC,), ((0, 4),), -0.2, 0.2), -2.0, -0.4),
        "vir_energy": jnp.clip(jax.random.uniform(arg_keys[5], (VWIN,), jnp.float32, 0.2, 3.0), 0.2, 3.0),
        "row_irrep": draw_row_irrep(jax.random.fold_in(arg_keys[9], 71), 0),
        "occ_irrep": draw_occ_irrep(jax.random.fold_in(arg_keys[9], 71), 0),
        "vir_irrep": draw_vir_irrep(jax.random.fold_in(arg_keys[9], 71), 0),
    }


def reference(amplitudes, coupling, integrals, row_energy, occ_energy, vir_energy, row_irrep, occ_irrep, vir_irrep):
    cycle_terms = jnp.dot(amplitudes, coupling, preferred_element_type=jnp.float32)
    cycle_terms = jnp.transpose(cycle_terms.reshape(SLAB_ROWS, VWIN, NOCC), (0, 2, 1))
    denominator = row_energy[:, None, None] + occ_energy[None, :, None] - vir_energy[None, None, :]
    labels = jnp.bitwise_xor(jnp.bitwise_xor(row_irrep[:, None, None], occ_irrep[None, :, None]), vir_irrep[None, None, :])
    allowed = labels == 0
    return jnp.where(allowed, (integrals + cycle_terms) / denominator, jnp.float32(0.0))
```

```python
import functools

import jax
import jax.numpy as jnp
import numpy as np
from jax import lax
from jax.experimental import pallas as pl
from jax.experimental.pallas import tpu as pltpu
from jax.sharding import PartitionSpec as P

NOCC = 60
LANES = 128
K_BLOCK = 2048
C_BLOCK = 240
STEPS = 8.0
TOP = 32767.0
VMEM_LIMIT = 48 * 1024 * 1024


def ceil_to(value, unit):
    return -(-value // unit) * unit


def encode(rows, count):
    index = lax.broadcasted_iota(jnp.int32, rows.shape, 0)
    rows = jnp.where(index < count, rows, 0.0)
    largest = jnp.max(jnp.abs(rows), axis=0, keepdims=True)
    level = jnp.ceil(jnp.log2(jnp.maximum(largest, 1e-30)) * STEPS) + 1.0
    coded = jnp.floor(rows * (jnp.exp2(level * (-1.0 / STEPS)) * TOP) + 0.5)
    return jnp.where(index == count, level, coded)


def decode(block, count):
    index = lax.broadcasted_iota(jnp.int32, block.shape, 0)
    scale = jnp.exp2(block[count : count + 1] * (1.0 / STEPS)) * (1.0 / TOP)
    return jnp.where(index < count, block * scale, 0.0)


def to_code(block):
    return block.astype(jnp.int32).astype(jnp.int16)


def from_code(block):
    return block.astype(jnp.int32).astype(jnp.float32)


def matrix_kernel(first, blocks, valid, *refs):
    place_ref = refs[0]
    pieces = refs[1 : 1 + blocks]
    coupling_ref = refs[1 + blocks]
    total_in = None if first else refs[2 + blocks]
    total_out, gathered = refs[-2:]
    rows = pieces[0].shape[0]
    depth = gathered.shape[1]

    @pl.when(pl.program_id(0) == 0)
    def _():
        for piece in range(blocks):
            at = pl.multiple_of(place_ref[piece] * rows, rows)
            gathered[pl.ds(at, rows), :] = pieces[piece][...]

    whole = valid // LANES * LANES
    contract = (((1,), (1,)), ((), ()))
    total = lax.dot_general(
        coupling_ref[:, :whole], gathered[:, :whole], contract, preferred_element_type=jnp.float32
    )
    if whole < valid:
        tail = slice(whole, whole + LANES)
        keep = lambda x: jnp.where(
            lax.broadcasted_iota(jnp.int32, x.shape, 1) < valid - whole, x, jnp.zeros_like(x)
        )
        total += lax.dot_general(
            keep(coupling_ref[:, tail]),
            keep(gathered[:, tail]),
            contract,
            preferred_element_type=jnp.float32,
        )
    for part in range(total_out.shape[0]):
        own = total[:, part * LANES : (part + 1) * LANES]
        total_out[part] = own if first else total_in[part] + own


def multiply(place, pieces, coupling, at, total, padded_columns):
    blocks = len(pieces)
    rows, width = pieces[0].shape
    slab = rows * blocks
    columns = coupling.shape[0]
    depth = min(K_BLOCK, ceil_to(width, LANES))
    pieces = [jnp.pad(p, ((0, 0), (0, depth - width))) if depth > width else p for p in pieces]
    first = total is None
    column_block = min(C_BLOCK, ceil_to(columns, 16))
    block_spec = pl.BlockSpec((slab // LANES, column_block, LANES), lambda i, p: (0, i, 0))
    in_specs = [pl.BlockSpec((rows, depth), lambda i, p: (0, 0))] * blocks
    in_specs += [pl.BlockSpec((column_block, K_BLOCK), lambda i, p: (i, at // K_BLOCK))]
    args = [*pieces, coupling]
    if not first:
        in_specs += [block_spec]
        args += [total]
    return pl.pallas_call(
        functools.partial(matrix_kernel, first, blocks, width),
        out_shape=jax.ShapeDtypeStruct((slab // LANES, padded_columns, LANES), jnp.float32),
        grid_spec=pltpu.PrefetchScalarGridSpec(
            num_scalar_prefetch=1,
            grid=(pl.cdiv(columns, column_block),),
            in_specs=in_specs,
            out_specs=block_spec,
            scratch_shapes=[pltpu.VMEM((slab, depth), jnp.bfloat16)],
        ),
        input_output_aliases={} if first else {len(args): 0},
        compiler_params=pltpu.CompilerParams(
            vmem_limit_bytes=VMEM_LIMIT, dimension_semantics=("arbitrary",)
        ),
        cost_estimate=pl.CostEstimate(
            flops=2 * columns * width * slab,
            bytes_accessed=2 * columns * width + 8 * columns * slab,
            transcendentals=0,
        ),
        name="matrix",
    )(place, *args)


def column_rows(total_ref, part, j, bp, width):
    rows = pl.ds(part * width + j, bp, stride=NOCC)
    return jnp.concatenate([total_ref[h, rows, :] for h in range(total_ref.shape[0])], axis=1)


def first_send_kernel(count, width, rep_ref, total_ref, out_ref):
    low = rep_ref[0] % 2

    def step(j, carry):
        for high in range(2):
            rows = column_rows(total_ref, 2 * high + 1 - low, j, out_ref.shape[2], width)
            out_ref[high, j] = to_code(encode(rows, count))
        return carry

    lax.fori_loop(0, width, step, 0)


def second_send_kernel(count, width, rep_ref, total_ref, got_ref, out_ref):
    low, high = rep_ref[0] % 2, 1 - rep_ref[0] // 2

    def step(j, carry):
        rows = column_rows(total_ref, 2 * high + low, j, out_ref.shape[1], width)
        rows = rows + decode(from_code(got_ref[high, j]), count)
        out_ref[j] = to_code(encode(rows, count))
        return carry

    lax.fori_loop(0, width, step, 0)


def keep_kernel(count, width, rep_ref, total_ref, got_ref, out_ref):
    low, high = rep_ref[0] % 2, rep_ref[0] // 2

    def step(j, carry):
        rows = column_rows(total_ref, 2 * high + low, j, out_ref.shape[1], width)
        out_ref[j] = rows + decode(from_code(got_ref[high, j]), count)
        return carry

    lax.fori_loop(0, width, step, 0)


def third_send_kernel(count, width, rows_dev, kept_ref, got_ref, out_ref):
    pack = LANES // rows_dev
    groups = out_ref.shape[1]
    bp, slab = kept_ref.shape[1:]

    def step(jj, carry):
        coded = []
        for jq in range(pack):
            j = jnp.minimum(jq * groups + jj, width - 1)
            coded.append(encode(kept_ref[j] + decode(from_code(got_ref[j]), count), count))
        for g in range(slab // rows_dev):
            own = [block[:, g * rows_dev : (g + 1) * rows_dev] for block in coded]
            out_ref[g, jj] = to_code(jnp.concatenate(own, axis=1))
        return carry

    lax.fori_loop(0, groups, step, 0)


def update_kernel(
    count,
    width,
    rows_dev,
    occ_energy_ref,
    occ_irrep_ref,
    got_ref,
    integrals_ref,
    row_energy_ref,
    vir_energy_ref,
    row_irrep_ref,
    vir_irrep_ref,
    out_ref,
    stage,
):
    pack = LANES // rows_dev
    groups = got_ref.shape[1]
    for jj in range(groups):
        for g in range(got_ref.shape[0]):
            block = from_code(got_ref[g, jj])
            stage[g * count : (g + 1) * count, :] = decode(block, count)[:count]
        turned = stage[...].T
        for jq in range(pack):
            j = jq * groups + jj
            if j >= width:
                continue
            cycle = turned[jq * rows_dev : (jq + 1) * rows_dev]
            denominator = row_energy_ref[...] + occ_energy_ref[j] - vir_energy_ref[...]
            labels = row_irrep_ref[...] ^ occ_irrep_ref[j] ^ vir_irrep_ref[...]
            out_ref[j] = jnp.where(
                labels == 0, (integrals_ref[j] + cycle) / denominator, jnp.float32(0.0)
            )


def local_call(kernel, out_shape, args, scalars=0, scratch=(), name=None):
    in_specs = [pl.BlockSpec(memory_space=pltpu.SMEM)] * scalars
    in_specs += [pl.BlockSpec(memory_space=pltpu.VMEM)] * (len(args) - scalars)
    return pl.pallas_call(
        kernel,
        out_shape=out_shape,
        in_specs=in_specs,
        out_specs=pl.BlockSpec(memory_space=pltpu.VMEM),
        scratch_shapes=list(scratch),
        compiler_params=pltpu.CompilerParams(vmem_limit_bytes=VMEM_LIMIT),
        cost_estimate=pl.CostEstimate(flops=10**7, bytes_accessed=4 * 10**6, transcendentals=0),
        name=name,
    )(*args)


def body(
    amplitudes,
    coupling,
    integrals,
    row_energy,
    occ_energy,
    vir_energy,
    row_irrep,
    occ_irrep,
    vir_irrep,
):
    grid_size = lax.axis_size("grid")
    me = lax.axis_index("grid")
    rep = lax.axis_index("rep").astype(jnp.int32).reshape(1)
    rows_dev, depth = amplitudes.shape
    coupling = coupling.T
    count = coupling.shape[0] // NOCC
    bp = ceil_to(count + 1, 16)
    slab = rows_dev * grid_size
    width = NOCC // lax.axis_size("rep")

    walk = [*range(0, grid_size, 2), *range(1, grid_size, 2)[::-1]]
    step_of = np.argsort(walk)
    onward = [(walk[i], walk[(i + 1) % grid_size]) for i in range(grid_size)]
    back = [(b, a) for a, b in onward]
    position = jnp.asarray(step_of, jnp.int32)[me]

    total = None
    for number, at in enumerate(range(0, depth, K_BLOCK)):
        own = amplitudes[:, at : at + K_BLOCK]
        pieces, offsets = [own], [0]
        longer = grid_size // 2
        hops = (longer, grid_size - 1 - longer)
        if number % 2:
            hops = hops[::-1]
        ahead = behind = own
        for hop in range(1, longer + 1):
            if hop <= hops[0]:
                ahead = lax.ppermute(ahead, "grid", onward)
                pieces.append(ahead)
                offsets.append(-hop)
            if hop <= hops[1]:
                behind = lax.ppermute(behind, "grid", back)
                pieces.append(behind)
                offsets.append(hop)
        place = jnp.asarray(walk, jnp.int32)[
            (position + jnp.asarray(offsets, jnp.int32) + grid_size) % grid_size
        ]
        total = multiply(place, pieces, coupling, at, total, bp * NOCC)

    low_pairs = [(i, i ^ 1) for i in range(lax.axis_size("rep"))]
    high_pairs = [(i, i ^ 2) for i in range(lax.axis_size("rep"))]
    shape = (width, bp, slab)
    send = local_call(
        functools.partial(first_send_kernel, count, width),
        jax.ShapeDtypeStruct((2, *shape), jnp.int16),
        (rep, total),
        1,
        name="first_send",
    )
    got = lax.ppermute(send, "rep", low_pairs)
    send = local_call(
        functools.partial(second_send_kernel, count, width),
        jax.ShapeDtypeStruct(shape, jnp.int16),
        (rep, total, got),
        1,
        name="second_send",
    )
    kept = local_call(
        functools.partial(keep_kernel, count, width),
        jax.ShapeDtypeStruct(shape, jnp.float32),
        (rep, total, got),
        1,
        name="keep",
    )
    got = lax.ppermute(send, "rep", high_pairs)

    groups = -(-width // (LANES // rows_dev))
    send = local_call(
        functools.partial(third_send_kernel, count, width, rows_dev),
        jax.ShapeDtypeStruct((grid_size, groups, bp, LANES), jnp.int16),
        (kept, got),
        name="third_send",
    )
    got = lax.all_to_all(send, "grid", split_axis=0, concat_axis=0, tiled=True)

    updated = local_call(
        functools.partial(update_kernel, count, width, rows_dev),
        jax.ShapeDtypeStruct((width, rows_dev, count * grid_size), jnp.float32),
        (
            occ_energy,
            occ_irrep,
            got,
            jnp.transpose(integrals, (1, 0, 2)),
            row_energy[:, None],
            vir_energy[None, :],
            row_irrep[:, None],
            vir_irrep[None, :],
        ),
        2,
        scratch=[pltpu.VMEM((count * grid_size, LANES), jnp.float32)],
        name="update",
    )
    return jnp.transpose(updated, (1, 0, 2))


def solution(mesh):
    return jax.shard_map(
        body,
        mesh=mesh,
        in_specs=(
            P("grid", "rep"),
            P("rep", "grid"),
            P("grid", "rep", None),
            P("grid"),
            P("rep"),
            P(),
            P("grid"),
            P("rep"),
            P(),
        ),
        out_specs=P("grid", "rep", None),
        check_vma=False,
    )
```

```python
import functools

import jax
import jax.numpy as jnp
from jax import lax
from jax.experimental import pallas as pl
from jax.experimental.pallas import tpu as pltpu
from jax.sharding import PartitionSpec as P

NOCC = 60
LANES = 128
K_BLOCK = 2048
C_BLOCK = 720
TAIL_PARTS = 2
STEPS = 8.0
TOP = 32767.0
VMEM_LIMIT = 48 * 1024 * 1024


def ceil_to(value, unit):
    return -(-value // unit) * unit


def encode(rows, count):
    index = lax.broadcasted_iota(jnp.int32, rows.shape, 0)
    rows = jnp.where(index < count, rows, 0.0)
    largest = jnp.max(jnp.abs(rows), axis=0, keepdims=True)
    level = jnp.ceil(jnp.log2(jnp.maximum(largest, 1e-30)) * STEPS) + 1.0
    coded = jnp.floor(rows * (jnp.exp2(level * (-1.0 / STEPS)) * TOP) + 0.5)
    return jnp.where(index == count, level, coded)


def decode(block, count):
    index = lax.broadcasted_iota(jnp.int32, block.shape, 0)
    scale = jnp.exp2(block[count : count + 1] * (1.0 / STEPS)) * (1.0 / TOP)
    return jnp.where(index < count, block * scale, 0.0)


def to_code(block):
    return block.astype(jnp.int32).astype(jnp.int16)


def from_code(block):
    return block.astype(jnp.int32).astype(jnp.float32)


def walk_index(place, size):
    return jnp.where(place < size // 2, 2 * place, 2 * (size - 1 - place) + 1)


def walk_place(index, size):
    return jnp.where(index % 2 == 0, index // 2, size - 1 - index // 2)


def matrix_kernel(first, offsets, valid, *refs):
    blocks = len(offsets)
    me_ref = refs[0]
    pieces = refs[1 : 1 + blocks]
    coupling_ref = refs[1 + blocks]
    total_in = None if first else refs[2 + blocks]
    total_out, gathered, turned = refs[-3:]
    rows = pieces[0].shape[0]
    depth = gathered.shape[1]

    @pl.when(pl.program_id(0) == 0)
    def _():
        place = walk_place(me_ref[0], blocks)
        for piece in range(blocks):
            source = walk_index(lax.rem(place + offsets[piece] + blocks, blocks), blocks)
            at = pl.multiple_of(source * rows, rows)
            gathered[pl.ds(at, rows), :valid] = pieces[piece][...]
        for at in range(0, depth, LANES):
            turned[at : at + LANES, :] = gathered[:, at : at + LANES].T
        if valid < depth:
            at = valid // LANES * LANES
            tile = turned[at : at + LANES, :]
            index = lax.broadcasted_iota(jnp.int32, tile.shape, 0)
            turned[at : at + LANES, :] = jnp.where(index < valid - at, tile, jnp.zeros_like(tile))

    whole = valid // LANES * LANES
    total = jnp.dot(
        coupling_ref[:, :whole], turned[:whole, :], preferred_element_type=jnp.float32
    )
    if whole < valid:
        tile = coupling_ref[:, whole : whole + LANES]
        index = lax.broadcasted_iota(jnp.int32, tile.shape, 1)
        tile = jnp.where(index < valid - whole, tile, jnp.zeros_like(tile))
        total += jnp.dot(tile, turned[whole:depth, :], preferred_element_type=jnp.float32)
    for part in range(total_out.shape[0]):
        own = total[:, part * LANES : (part + 1) * LANES]
        total_out[part] = own if first else total_in[part] + own


def multiply(me, offsets, pieces, coupling, at, total, padded_columns):
    blocks = len(pieces)
    rows, width = pieces[0].shape
    slab = rows * blocks
    columns = coupling.shape[0]
    depth = ceil_to(width, LANES)
    first = total is None
    column_block = min(C_BLOCK, ceil_to(columns, 16))
    block_spec = pl.BlockSpec((slab // LANES, column_block, LANES), lambda i, p: (0, i, 0))
    in_specs = [pl.BlockSpec((rows, width), lambda i, p: (0, 0))] * blocks
    in_specs += [pl.BlockSpec((column_block, K_BLOCK), lambda i, p: (i, at // K_BLOCK))]
    args = [*pieces, coupling]
    if not first:
        in_specs += [block_spec]
        args += [total]
    return pl.pallas_call(
        functools.partial(matrix_kernel, first, tuple(offsets), width),
        out_shape=jax.ShapeDtypeStruct((slab // LANES, padded_columns, LANES), jnp.float32),
        grid_spec=pltpu.PrefetchScalarGridSpec(
            num_scalar_prefetch=1,
            grid=(pl.cdiv(columns, column_block),),
            in_specs=in_specs,
            out_specs=block_spec,
            scratch_shapes=[
                pltpu.VMEM((slab, depth), jnp.bfloat16),
                pltpu.VMEM((depth, slab), jnp.bfloat16),
            ],
        ),
        input_output_aliases={} if first else {len(args): 0},
        compiler_params=pltpu.CompilerParams(
            vmem_limit_bytes=VMEM_LIMIT, dimension_semantics=("arbitrary",)
        ),
        cost_estimate=pl.CostEstimate(
            flops=2 * columns * width * slab,
            bytes_accessed=2 * columns * width + 8 * columns * slab,
            transcendentals=0,
        ),
        name="matrix",
    )(me, *args)


def column_rows(total_ref, part, j, bp, width):
    rows = pl.ds(part * width + j, bp, stride=NOCC)
    return jnp.concatenate([total_ref[h, rows, :] for h in range(total_ref.shape[0])], axis=1)


def first_send_kernel(count, width, start, rep_ref, total_ref, out_ref):
    low = rep_ref[0] % 2

    def step(j, carry):
        for high in range(2):
            part = 2 * high + 1 - low
            rows = column_rows(total_ref, part, start + j, out_ref.shape[2], width)
            out_ref[high, j] = to_code(encode(rows, count))
        return carry

    lax.fori_loop(0, out_ref.shape[1], step, 0)


def second_send_kernel(count, width, start, rep_ref, total_ref, got_ref, out_ref):
    low, high = rep_ref[0] % 2, 1 - rep_ref[0] // 2

    def step(j, carry):
        rows = column_rows(total_ref, 2 * high + low, start + j, out_ref.shape[1], width)
        rows = rows + decode(from_code(got_ref[high, j]), count)
        out_ref[j] = to_code(encode(rows, count))
        return carry

    lax.fori_loop(0, out_ref.shape[0], step, 0)


def keep_kernel(count, width, start, rep_ref, total_ref, got_ref, out_ref):
    low, high = rep_ref[0] % 2, rep_ref[0] // 2

    def step(j, carry):
        rows = column_rows(total_ref, 2 * high + low, start + j, out_ref.shape[1], width)
        out_ref[j] = rows + decode(from_code(got_ref[high, j]), count)
        return carry

    lax.fori_loop(0, out_ref.shape[0], step, 0)


def third_send_kernel(count, rows_dev, kept_ref, got_ref, out_ref):
    pack = LANES // rows_dev
    groups = out_ref.shape[1]
    size, _, slab = kept_ref.shape

    def step(jj, carry):
        coded = []
        for jq in range(pack):
            j = jnp.minimum(jq * groups + jj, size - 1)
            coded.append(encode(kept_ref[j] + decode(from_code(got_ref[j]), count), count))
        for g in range(slab // rows_dev):
            own = [block[:, g * rows_dev : (g + 1) * rows_dev] for block in coded]
            out_ref[g, jj] = to_code(jnp.concatenate(own, axis=1))
        return carry

    lax.fori_loop(0, groups, step, 0)


def update_kernel(count, width, rows_dev, parts, occ_energy_ref, occ_irrep_ref, *refs):
    arrived = refs[:parts]
    (
        integrals_ref,
        row_energy_ref,
        vir_energy_ref,
        row_irrep_ref,
        vir_irrep_ref,
        out_ref,
        stage,
    ) = refs[parts:]
    pack = LANES // rows_dev
    start = 0
    for got_ref in arrived:
        groups = got_ref.shape[1]
        size = min(groups * pack, width - start)
        for jj in range(groups):
            for g in range(got_ref.shape[0]):
                block = from_code(got_ref[g, jj])
                stage[g * count : (g + 1) * count, :] = decode(block, count)[:count]
            turned = stage[...].T
            for jq in range(pack):
                if jq * groups + jj >= size:
                    continue
                j = start + jq * groups + jj
                cycle = turned[jq * rows_dev : (jq + 1) * rows_dev]
                denominator = row_energy_ref[...] + occ_energy_ref[j] - vir_energy_ref[...]
                labels = row_irrep_ref[...] ^ occ_irrep_ref[j] ^ vir_irrep_ref[...]
                out_ref[j] = jnp.where(
                    labels == 0, (integrals_ref[j] + cycle) / denominator, jnp.float32(0.0)
                )
        start += size


def local_call(kernel, out_shape, args, scalars=0, scratch=(), name=None):
    in_specs = [pl.BlockSpec(memory_space=pltpu.SMEM)] * scalars
    in_specs += [pl.BlockSpec(memory_space=pltpu.VMEM)] * (len(args) - scalars)
    return pl.pallas_call(
        kernel,
        out_shape=out_shape,
        in_specs=in_specs,
        out_specs=pl.BlockSpec(memory_space=pltpu.VMEM),
        scratch_shapes=list(scratch),
        compiler_params=pltpu.CompilerParams(vmem_limit_bytes=VMEM_LIMIT),
        cost_estimate=pl.CostEstimate(flops=10**7, bytes_accessed=4 * 10**6, transcendentals=0),
        name=name,
    )(*args)


def body(
    amplitudes,
    coupling,
    integrals,
    row_energy,
    occ_energy,
    vir_energy,
    row_irrep,
    occ_irrep,
    vir_irrep,
):
    grid_size = lax.axis_size("grid")
    me = lax.axis_index("grid").astype(jnp.int32).reshape(1)
    rep = lax.axis_index("rep").astype(jnp.int32).reshape(1)
    rows_dev, depth = amplitudes.shape
    coupling = coupling.T
    count = coupling.shape[0] // NOCC
    bp = ceil_to(count + 1, 16)
    slab = rows_dev * grid_size
    width = NOCC // lax.axis_size("rep")

    walk = [*range(0, grid_size, 2), *range(1, grid_size, 2)[::-1]]
    onward = [(walk[i], walk[(i + 1) % grid_size]) for i in range(grid_size)]
    back = [(b, a) for a, b in onward]

    longer = grid_size // 2
    ends = []
    jobs = []
    for number, at in enumerate(range(0, depth, K_BLOCK)):
        own = amplitudes[:, at : at + K_BLOCK]
        if number > 1:
            own, *_ = lax.optimization_barrier((own, *ends[number - 2]))
        pieces, offsets = [own], [0]
        hops = (longer, grid_size - 1 - longer)
        if number % 2:
            hops = hops[::-1]
        ahead = behind = own
        for hop in range(1, longer + 1):
            if hop <= hops[0]:
                ahead = lax.ppermute(ahead, "grid", onward)
                pieces.append(ahead)
                offsets.append(-hop)
            if hop <= hops[1]:
                behind = lax.ppermute(behind, "grid", back)
                pieces.append(behind)
                offsets.append(hop)
        ends.append((ahead, behind))
        jobs.append((at, offsets, pieces))
    total = None
    for number, (at, offsets, pieces) in enumerate(jobs):
        if number + 1 < len(jobs):
            late = jobs[number + 1][2][-3:-1] if number % 2 == 0 else jobs[number + 1][2][1:3]
            pieces = lax.optimization_barrier((*pieces, *late))[: len(pieces)]
        total = multiply(me, offsets, pieces, coupling, at, total, bp * NOCC)

    low_pairs = [(i, i ^ 1) for i in range(lax.axis_size("rep"))]
    high_pairs = [(i, i ^ 2) for i in range(lax.axis_size("rep"))]
    pack = LANES // rows_dev
    cut = ceil_to(-(-width // TAIL_PARTS), pack)
    arrived = []
    for start in range(0, width, cut):
        size = min(cut, width - start)
        span = (count, width, start)
        shape = (size, bp, slab)
        send = local_call(
            functools.partial(first_send_kernel, *span),
            jax.ShapeDtypeStruct((2, *shape), jnp.int16),
            (rep, total),
            1,
            name="first_send",
        )
        got = lax.ppermute(send, "rep", low_pairs)
        send = local_call(
            functools.partial(second_send_kernel, *span),
            jax.ShapeDtypeStruct(shape, jnp.int16),
            (rep, total, got),
            1,
            name="second_send",
        )
        kept = local_call(
            functools.partial(keep_kernel, *span),
            jax.ShapeDtypeStruct(shape, jnp.float32),
            (rep, total, got),
            1,
            name="keep",
        )
        got = lax.ppermute(send, "rep", high_pairs)
        send = local_call(
            functools.partial(third_send_kernel, count, rows_dev),
            jax.ShapeDtypeStruct((grid_size, -(-size // pack), bp, LANES), jnp.int16),
            (kept, got),
            name="third_send",
        )
        arrived.append(lax.all_to_all(send, "grid", split_axis=0, concat_axis=0, tiled=True))

    updated = local_call(
        functools.partial(update_kernel, count, width, rows_dev, len(arrived)),
        jax.ShapeDtypeStruct((width, rows_dev, count * grid_size), jnp.float32),
        (
            occ_energy,
            occ_irrep,
            *arrived,
            jnp.transpose(integrals, (1, 0, 2)),
            row_energy[:, None],
            vir_energy[None, :],
            row_irrep[:, None],
            vir_irrep[None, :],
        ),
        2,
        scratch=[pltpu.VMEM((count * grid_size, LANES), jnp.float32)],
        name="update",
    )
    return jnp.transpose(updated, (1, 0, 2))


def solution(mesh):
    return jax.shard_map(
        body,
        mesh=mesh,
        in_specs=(
            P("grid", "rep"),
            P("rep", "grid"),
            P("grid", "rep", None),
            P("grid"),
            P("rep"),
            P(),
            P("grid"),
            P("rep"),
            P(),
        ),
        out_specs=P("grid", "rep", None),
        check_vma=False,
    )
```

```python
import functools

import jax
import jax.numpy as jnp
from jax import lax
from jax.experimental import pallas as pl
from jax.experimental.pallas import tpu as pltpu
from jax.sharding import PartitionSpec as P

NOCC = 60
LANES = 128
K_BLOCK = 3840
C_BLOCK = 480
B_ROWS = 32
STEPS = 8.0
TOP = 32767.0
MIB = 1024 * 1024


def ceil_to(value, unit):
    return -(-value // unit) * unit


def encode(rows, count):
    index = lax.broadcasted_iota(jnp.int32, rows.shape, 0)
    rows = jnp.where(index < count, rows, 0.0)
    largest = jnp.max(jnp.abs(rows), axis=0, keepdims=True)
    level = jnp.ceil(jnp.log2(jnp.maximum(largest, 1e-30)) * STEPS) + 1.0
    coded = jnp.floor(rows * (jnp.exp2(level * (-1.0 / STEPS)) * TOP) + 0.5)
    return jnp.where(index == count, level, coded)


def decode(block, count):
    index = lax.broadcasted_iota(jnp.int32, block.shape, 0)
    scale = jnp.exp2(block[count : count + 1] * (1.0 / STEPS)) * (1.0 / TOP)
    return jnp.where(index < count, block * scale, 0.0)


def to_code(block):
    return block.astype(jnp.int32).astype(jnp.int16)


def from_code(block):
    return block.astype(jnp.int32).astype(jnp.float32)


def walk_index(place, size):
    return jnp.where(place < size // 2, 2 * place, 2 * (size - 1 - place) + 1)


def walk_place(index, size):
    return jnp.where(index % 2 == 0, index // 2, size - 1 - index // 2)


def gather_pieces(me_ref, offsets, pieces, gathered, turned):
    blocks = len(offsets)
    rows, width = pieces[0].shape
    place = walk_place(me_ref[0], blocks)
    for offset, piece in zip(offsets, pieces):
        source = walk_index(lax.rem(place + offset + blocks, blocks), blocks)
        at = pl.multiple_of(source * rows, rows)
        gathered[pl.ds(at, rows), :width] = piece[...]
    for at in range(0, turned.shape[0], LANES):
        tile = gathered[:, at : at + LANES].T
        if at + LANES > width:
            index = lax.broadcasted_iota(jnp.int32, tile.shape, 0)
            tile = jnp.where(index < width - at, tile, jnp.zeros_like(tile))
        turned[at : at + LANES, :] = tile


def add_products(coupling_ref, edge_ref, at, width, turned, total_in, total_out, columns):
    all_columns = coupling_ref.shape[0]
    block = C_BLOCK if all_columns % 16 == 0 else all_columns
    low, many = columns
    whole = width // LANES * LANES

    def step(coupling_block, edge_block=None):
        total = jnp.dot(coupling_block[...], turned[:whole, :], preferred_element_type=jnp.float32)
        if whole < width:
            total += jnp.dot(
                edge_block[...], turned[whole:, :], preferred_element_type=jnp.float32
            )
        rows = pl.ds(pl.program_id(0) * block, block)
        for part in range(total_out.shape[0]):
            own = total[:, part * LANES : (part + 1) * LANES]
            total_out[part, rows, :] = own if total_in is None else total_in[part, rows, :] + own

    index_map = lambda i: (i, 0)
    specs = [pl.BlockSpec((block, whole), index_map)]
    args = [coupling_ref.at[low : low + many, at : at + whole]]
    if whole < width:
        specs.append(pl.BlockSpec((block, LANES), index_map))
        args.append(edge_ref.at[low : low + many])
    pltpu.emit_pipeline(step, grid=(pl.cdiv(many, block),), in_specs=specs)(*args)


def start_kernel(offsets, at, columns, me_ref, *refs):
    pieces, refs = refs[: len(offsets)], refs[len(offsets) :]
    coupling_ref, edge_ref = refs[:2]
    totals, (gathered, turned) = refs[2:-2], refs[-2:]
    gather_pieces(me_ref, offsets, pieces, gathered, turned)
    width = pieces[0].shape[1]
    outs = totals[-len(columns) :]
    ins = totals[: -len(columns)] or [None] * len(columns)
    for span, total_in, total_out in zip(columns, ins, outs):
        add_products(coupling_ref, edge_ref, at, width, turned, total_in, total_out, span)


def last_kernel(offsets, at, columns, span, me_ref, rep_ref, *refs):
    pieces = refs[: len(offsets)]
    coupling_ref, edge_ref, total_in, total_out, turned, send_ref, gathered = refs[len(offsets) :]
    gather_pieces(me_ref, offsets, pieces, gathered, turned)
    width = pieces[0].shape[1]
    add_products(coupling_ref, edge_ref, at, width, turned, total_in, total_out, columns)
    first_send(span, rep_ref, total_out, send_ref)


def rest_kernel(at, width, columns, span, rep_ref, turned, *refs):
    coupling_ref, edge_ref, total_in, total_out, send = refs
    add_products(coupling_ref, edge_ref, at, width, turned, total_in, total_out, columns)
    first_send(span, rep_ref, total_out, send)


def column_rows(total_ref, width, part, j, offset, bp):
    rows = pl.ds(offset + part * width + j, bp, stride=NOCC)
    return jnp.concatenate([total_ref[h, rows, :] for h in range(total_ref.shape[0])], axis=1)


def first_send(span, rep_ref, total_ref, out_ref):
    offset, count, width = span
    low = rep_ref[0] % 2

    def step(j, carry):
        for high in range(2):
            rows = column_rows(total_ref, width, 2 * high + 1 - low, j, offset, out_ref.shape[2])
            out_ref[high, j] = to_code(encode(rows, count))
        return carry

    lax.fori_loop(0, width, step, 0)


def second_send_kernel(span, rep_ref, total_ref, got_ref, out_ref):
    offset, count, width = span
    low, high = rep_ref[0] % 2, 1 - rep_ref[0] // 2

    def step(j, carry):
        rows = column_rows(total_ref, width, 2 * high + low, j, offset, out_ref.shape[1])
        rows = rows + decode(from_code(got_ref[high, j]), count)
        out_ref[j] = to_code(encode(rows, count))
        return carry

    lax.fori_loop(0, width, step, 0)


def keep_kernel(span, rep_ref, total_ref, got_ref, out_ref):
    offset, count, width = span
    low, high = rep_ref[0] % 2, rep_ref[0] // 2

    def step(j, carry):
        rows = column_rows(total_ref, width, 2 * high + low, j, offset, out_ref.shape[1])
        out_ref[j] = rows + decode(from_code(got_ref[high, j]), count)
        return carry

    lax.fori_loop(0, width, step, 0)


def third_send_kernel(count, rows_dev, kept_ref, got_ref, out_ref):
    pack = LANES // rows_dev
    groups = out_ref.shape[1]
    size, _, slab = kept_ref.shape

    def step(jj, carry):
        coded = []
        for jq in range(pack):
            j = jnp.minimum(jq * groups + jj, size - 1)
            coded.append(encode(kept_ref[j] + decode(from_code(got_ref[j]), count), count))
        for g in range(slab // rows_dev):
            own = [block[:, g * rows_dev : (g + 1) * rows_dev] for block in coded]
            out_ref[g, jj] = to_code(jnp.concatenate(own, axis=1))
        return carry

    lax.fori_loop(0, groups, step, 0)


def update_kernel(counts, width, rows_dev, occ_energy_ref, occ_irrep_ref, *refs):
    arrived = refs[: len(counts)]
    (
        integrals_ref,
        row_energy_ref,
        vir_energy_ref,
        row_irrep_ref,
        vir_irrep_ref,
        out_ref,
        stage,
    ) = refs[len(counts) :]
    pack = LANES // rows_dev
    grid_size, groups = arrived[0].shape[:2]
    for jj in range(groups):
        at = 0
        for g in range(grid_size):
            for count, got_ref in zip(counts, arrived):
                block = decode(from_code(got_ref[g, jj]), count)
                stage[at : at + count, :] = block[:count]
                at += count
        turned = stage[...].T
        for jq in range(pack):
            j = jq * groups + jj
            if j >= width:
                continue
            cycle = turned[jq * rows_dev : (jq + 1) * rows_dev]
            denominator = row_energy_ref[...] + occ_energy_ref[j] - vir_energy_ref[...]
            labels = row_irrep_ref[...] ^ occ_irrep_ref[j] ^ vir_irrep_ref[...]
            out_ref[j] = jnp.where(
                labels == 0, (integrals_ref[j] + cycle) / denominator, jnp.float32(0.0)
            )


def local_call(kernel, out_shape, specs, args, scratch=(), aliases={}, cost=(10**7, 4 * 10**6), room=0):
    spaces = {"s": pltpu.SMEM, "v": pltpu.VMEM, "a": pl.ANY}
    return pl.pallas_call(
        kernel,
        out_shape=out_shape,
        in_specs=[pl.BlockSpec(memory_space=spaces[letter]) for letter in specs],
        out_specs=jax.tree.map(lambda _: pl.BlockSpec(memory_space=pltpu.VMEM), out_shape),
        scratch_shapes=list(scratch),
        input_output_aliases=aliases,
        compiler_params=pltpu.CompilerParams(vmem_limit_bytes=8 * MIB + room),
        cost_estimate=pl.CostEstimate(
            flops=cost[0], bytes_accessed=cost[1], transcendentals=0
        ),
        name=kernel.func.__name__,
    )(*args)


def body(
    amplitudes,
    coupling,
    integrals,
    row_energy,
    occ_energy,
    vir_energy,
    row_irrep,
    occ_irrep,
    vir_irrep,
):
    grid_size = lax.axis_size("grid")
    me = lax.axis_index("grid").astype(jnp.int32).reshape(1)
    rep = lax.axis_index("rep").astype(jnp.int32).reshape(1)
    rows_dev, depth = amplitudes.shape
    coupling = coupling.T
    columns = coupling.shape[0]
    edge = depth % LANES
    edge = jnp.pad(coupling[:, depth - edge :], ((0, 0), (0, LANES - edge)))
    count = columns // NOCC
    slab = rows_dev * grid_size
    width = NOCC // lax.axis_size("rep")

    walk = [*range(0, grid_size, 2), *range(1, grid_size, 2)[::-1]]
    onward = [(walk[i], walk[(i + 1) % grid_size]) for i in range(grid_size)]
    back = [(b, a) for a, b in onward]

    longer = grid_size // 2
    jobs = []
    for number, at in enumerate(range(0, depth, K_BLOCK)):
        own = amplitudes[:, at : at + K_BLOCK]
        pieces, offsets = [own], [0]
        hops = (longer, grid_size - 1 - longer)
        if number % 2:
            hops = hops[::-1]
        ahead = behind = own
        for hop in range(1, longer + 1):
            if hop <= hops[0]:
                ahead = lax.ppermute(ahead, "grid", onward)
                pieces.append(ahead)
                offsets.append(-hop)
            if hop <= hops[1]:
                behind = lax.ppermute(behind, "grid", back)
                pieces.append(behind)
                offsets.append(hop)
        jobs.append((at, tuple(offsets), pieces))

    firsts = list(range(0, count, B_ROWS - 1))
    counts = [min(B_ROWS - 1, count - first) for first in firsts]
    bp = ceil_to(counts[0] + 1, 16)
    send_shape = jax.ShapeDtypeStruct((2, width, bp, slab), jnp.int16)
    lows = [first * NOCC // 16 * 16 for first in firsts]
    highs = [
        min(columns, ceil_to((first + number) * NOCC, 16)) for first, number in zip(firsts, counts)
    ]
    parts = [(low, high - low) for low, high in zip(lows, highs)]
    spans = [
        (first * NOCC - low, number, width) for first, low, number in zip(firsts, lows, counts)
    ]
    total_shapes = [
        jax.ShapeDtypeStruct(
            (slab // LANES, max(span[0] + bp * NOCC, ceil_to(part[1], C_BLOCK)), LANES),
            jnp.float32,
        )
        for span, part in zip(spans, parts)
    ]

    def work(many, size):
        return 2 * many * size * slab, 2 * many * size + 8 * many * slab

    room = 4 * K_BLOCK * ((C_BLOCK if columns % 16 == 0 else columns) + slab)
    sends = []
    totals = []
    for number, (at, offsets, pieces) in enumerate(jobs):
        size = pieces[0].shape[1]
        deep = ceil_to(size, LANES)
        holder = pltpu.VMEM((slab, deep), jnp.bfloat16)
        turned = jax.ShapeDtypeStruct((deep, slab), jnp.bfloat16)
        pieces_specs = "v" * len(pieces)
        if number + 1 < len(jobs):
            args = (me, *pieces, coupling, edge, *totals)
            totals = local_call(
                functools.partial(start_kernel, offsets, at, parts),
                tuple(total_shapes),
                "s" + pieces_specs + "aa" + "v" * len(totals),
                args,
                [holder, pltpu.VMEM((deep, slab), jnp.bfloat16)],
                {len(args) - len(totals) + i: i for i in range(len(totals))},
                work(columns, size),
                room,
            )
            totals = list(totals)
            continue
        totals[0], turned, send = local_call(
            functools.partial(last_kernel, offsets, at, parts[0], spans[0]),
            (total_shapes[0], turned, send_shape),
            "ss" + pieces_specs + "aav",
            (me, rep, *pieces, coupling, edge, totals[0]),
            [holder],
            {len(pieces) + 4: 0},
            work(parts[0][1], size),
            room,
        )
        sends.append(send)
        for part in range(1, len(spans)):
            totals[part], send = local_call(
                functools.partial(rest_kernel, at, size, parts[part], spans[part]),
                (total_shapes[part], send_shape),
                "svaav",
                (rep, turned, coupling, edge, totals[part]),
                aliases={4: 0},
                cost=work(parts[part][1], size),
                room=room,
            )
            sends.append(send)

    low_pairs = [(i, i ^ 1) for i in range(lax.axis_size("rep"))]
    high_pairs = [(i, i ^ 2) for i in range(lax.axis_size("rep"))]
    pack = LANES // rows_dev
    groups = -(-width // pack)
    shape = (width, bp, slab)
    got = [lax.ppermute(send, "rep", low_pairs) for send in sends]
    sends = [
        local_call(
            functools.partial(second_send_kernel, span),
            jax.ShapeDtypeStruct(shape, jnp.int16),
            "svv",
            (rep, total, mine),
        )
        for span, total, mine in zip(spans, totals, got)
    ]
    kept = [
        local_call(
            functools.partial(keep_kernel, span),
            jax.ShapeDtypeStruct(shape, jnp.float32),
            "svv",
            (rep, total, mine),
        )
        for span, total, mine in zip(spans, totals, got)
    ]
    got = [lax.ppermute(send, "rep", high_pairs) for send in sends]
    arrived = []
    for part, span in enumerate(spans):
        mine = kept[part]
        if part + 1 < len(spans):
            mine, _ = lax.optimization_barrier((mine, sends[part + 1]))
        send = local_call(
            functools.partial(third_send_kernel, span[1], rows_dev),
            jax.ShapeDtypeStruct((grid_size, groups, bp, LANES), jnp.int16),
            "vv",
            (mine, got[part]),
        )
        arrived.append(lax.all_to_all(send, "grid", split_axis=0, concat_axis=0, tiled=True))

    updated = local_call(
        functools.partial(update_kernel, counts, width, rows_dev),
        jax.ShapeDtypeStruct((width, rows_dev, count * grid_size), jnp.float32),
        "ss" + "v" * (len(arrived) + 5),
        (
            occ_energy,
            occ_irrep,
            *arrived,
            jnp.transpose(integrals, (1, 0, 2)),
            row_energy[:, None],
            vir_energy[None, :],
            row_irrep[:, None],
            vir_irrep[None, :],
        ),
        [pltpu.VMEM((count * grid_size, LANES), jnp.float32)],
    )
    return jnp.transpose(updated, (1, 0, 2))


def solution(mesh):
    return jax.shard_map(
        body,
        mesh=mesh,
        in_specs=(
            P("grid", "rep"),
            P("rep", "grid"),
            P("grid", "rep", None),
            P("grid"),
            P("rep"),
            P(),
            P("grid"),
            P("rep"),
            P(),
        ),
        out_specs=P("grid", "rep", None),
        check_vma=False,
    )
```

```python
import functools

import jax
import jax.numpy as jnp
from jax import lax
from jax.experimental import pallas as pl
from jax.experimental.pallas import tpu as pltpu
from jax.sharding import PartitionSpec as P

NOCC = 60
LANES = 128
K_BLOCK = 3840
C_BLOCK = 480
SPLIT = 4
B_ROWS = 32
STEPS = 8.0
TOP = 32767.0
MIB = 1024 * 1024


def ceil_to(value, unit):
    return -(-value // unit) * unit


def encode(rows, count):
    index = lax.broadcasted_iota(jnp.int32, rows.shape, 0)
    rows = jnp.where(index < count, rows, 0.0)
    largest = jnp.max(jnp.abs(rows), axis=0, keepdims=True)
    level = jnp.ceil(jnp.log2(jnp.maximum(largest, 1e-30)) * STEPS) + 1.0
    coded = jnp.floor(rows * (jnp.exp2(level * (-1.0 / STEPS)) * TOP) + 0.5)
    return jnp.where(index == count, level, coded)


def decode(block, count):
    index = lax.broadcasted_iota(jnp.int32, block.shape, 0)
    scale = jnp.exp2(block[count : count + 1] * (1.0 / STEPS)) * (1.0 / TOP)
    return jnp.where(index < count, block * scale, 0.0)


def to_code(block):
    return block.astype(jnp.int32).astype(jnp.int16)


def from_code(block):
    return block.astype(jnp.int32).astype(jnp.float32)


def walk_index(place, size):
    return jnp.where(place < size // 2, 2 * place, 2 * (size - 1 - place) + 1)


def walk_place(index, size):
    return jnp.where(index % 2 == 0, index // 2, size - 1 - index // 2)


def gather_pieces(me_ref, offsets, pieces, gathered, turned, sems):
    blocks = len(offsets)
    rows = pieces[0].shape[0]
    place = walk_place(me_ref[0], blocks)
    copies = []
    for number, (offset, piece) in enumerate(zip(offsets, pieces)):
        source = walk_index(lax.rem(place + offset + blocks, blocks), blocks)
        at = pl.multiple_of(source * rows, rows)
        copies.append(
            pltpu.make_async_copy(piece, gathered.at[pl.ds(at, rows), :], sems.at[number])
        )
    for copy in copies:
        copy.start()
    for copy in copies:
        copy.wait()
    for at in range(0, turned.shape[0], LANES):
        turned[at : at + LANES, :] = gathered[:, at : at + LANES].T


def add_products(coupling_ref, edge_ref, at, whole, turned, total_in, total_out, columns):
    all_columns = coupling_ref.shape[0]
    block = C_BLOCK if all_columns % 16 == 0 else all_columns
    low, many = columns
    deep = turned.shape[0]
    quarter = ceil_to(-(-whole // SPLIT), 256)

    def step(coupling_block, edge_block=None):
        terms = [
            jnp.dot(
                coupling_block[:, k : min(k + quarter, whole)],
                turned[k : min(k + quarter, whole), :],
                preferred_element_type=jnp.float32,
            )
            for k in range(0, whole, quarter)
        ]
        if whole < deep:
            terms.append(
                jnp.dot(edge_block[...], turned[whole:, :], preferred_element_type=jnp.float32)
            )
        total = sum(terms[1:], terms[0])
        rows = pl.ds(pl.program_id(0) * block, block)
        for part in range(total_out.shape[0]):
            own = total[:, part * LANES : (part + 1) * LANES]
            total_out[part, rows, :] = own if total_in is None else total_in[part, rows, :] + own

    index_map = lambda i: (i, 0)
    specs = [pl.BlockSpec((block, whole), index_map)]
    args = [coupling_ref.at[low : low + many, at : at + whole]]
    if whole < deep:
        specs.append(pl.BlockSpec((block, LANES), index_map))
        args.append(edge_ref.at[low : low + many])
    pltpu.emit_pipeline(step, grid=(pl.cdiv(many, block),), in_specs=specs)(*args)


def lead_kernel(offsets, at, whole, columns, span, begin, me_ref, rep_ref, *refs):
    pieces, refs = refs[: len(offsets)], list(refs[len(offsets) :])
    coupling_ref, edge_ref = refs[:2]
    gathered, sems = refs[-2:]
    total_in = None if begin else refs[2]
    total_out, turned, *send = refs[2 if begin else 3 : -2]
    gather_pieces(me_ref, offsets, pieces, gathered, turned, sems)
    add_products(coupling_ref, edge_ref, at, whole, turned, total_in, total_out, columns)
    if span is not None:
        first_send(span, rep_ref, total_out, *send)


def rest_kernel(at, whole, columns, span, begin, rep_ref, turned, coupling_ref, edge_ref, *refs):
    total_in = None if begin else refs[0]
    total_out, *send = refs[0 if begin else 1 :]
    add_products(coupling_ref, edge_ref, at, whole, turned, total_in, total_out, columns)
    if span is not None:
        first_send(span, rep_ref, total_out, *send)


def column_rows(total_ref, width, part, j, offset, bp):
    rows = pl.ds(offset + part * width + j, bp, stride=NOCC)
    return jnp.concatenate([total_ref[h, rows, :] for h in range(total_ref.shape[0])], axis=1)


def first_send(span, rep_ref, total_ref, out_ref):
    offset, count, width = span
    low = rep_ref[0] % 2

    def step(j, carry):
        for high in range(2):
            rows = column_rows(total_ref, width, 2 * high + 1 - low, j, offset, out_ref.shape[2])
            out_ref[high, j] = to_code(encode(rows, count))
        return carry

    lax.fori_loop(0, width, step, 0)


def second_send_kernel(span, rep_ref, total_ref, got_ref, out_ref):
    offset, count, width = span
    low, high = rep_ref[0] % 2, 1 - rep_ref[0] // 2

    def step(j, carry):
        rows = column_rows(total_ref, width, 2 * high + low, j, offset, out_ref.shape[1])
        rows = rows + decode(from_code(got_ref[high, j]), count)
        out_ref[j] = to_code(encode(rows, count))
        return carry

    lax.fori_loop(0, width, step, 0)


def keep_kernel(span, rep_ref, total_ref, got_ref, out_ref):
    offset, count, width = span
    low, high = rep_ref[0] % 2, rep_ref[0] // 2

    def step(j, carry):
        rows = column_rows(total_ref, width, 2 * high + low, j, offset, out_ref.shape[1])
        out_ref[j] = rows + decode(from_code(got_ref[high, j]), count)
        return carry

    lax.fori_loop(0, width, step, 0)


def third_send_kernel(count, rows_dev, kept_ref, got_ref, out_ref):
    pack = LANES // rows_dev
    groups = out_ref.shape[1]
    size, _, slab = kept_ref.shape

    def step(jj, carry):
        coded = []
        for jq in range(pack):
            j = jnp.minimum(jq * groups + jj, size - 1)
            coded.append(encode(kept_ref[j] + decode(from_code(got_ref[j]), count), count))
        for g in range(slab // rows_dev):
            own = [block[:, g * rows_dev : (g + 1) * rows_dev] for block in coded]
            out_ref[g, jj] = to_code(jnp.concatenate(own, axis=1))
        return carry

    lax.fori_loop(0, groups, step, 0)


def update_kernel(counts, width, rows_dev, occ_energy_ref, occ_irrep_ref, *refs):
    arrived = refs[: len(counts)]
    (
        integrals_ref,
        row_energy_ref,
        vir_energy_ref,
        row_irrep_ref,
        vir_irrep_ref,
        out_ref,
        stage,
    ) = refs[len(counts) :]
    pack = LANES // rows_dev
    grid_size, groups = arrived[0].shape[:2]
    for jj in range(groups):
        at = 0
        for g in range(grid_size):
            for count, got_ref in zip(counts, arrived):
                block = decode(from_code(got_ref[g, jj]), count)
                stage[at : at + count, :] = block[:count]
                at += count
        turned = stage[...].T
        for jq in range(pack):
            j = jq * groups + jj
            if j >= width:
                continue
            cycle = turned[jq * rows_dev : (jq + 1) * rows_dev]
            denominator = row_energy_ref[...] + occ_energy_ref[j] - vir_energy_ref[...]
            labels = row_irrep_ref[...] ^ occ_irrep_ref[j] ^ vir_irrep_ref[...]
            out_ref[j] = jnp.where(
                labels == 0, (integrals_ref[j] + cycle) / denominator, jnp.float32(0.0)
            )


def local_call(kernel, out_shape, specs, args, scratch=(), aliases={}, cost=(10**7, 4 * 10**6), room=0):
    spaces = {"s": pltpu.SMEM, "v": pltpu.VMEM, "a": pl.ANY}
    return pl.pallas_call(
        kernel,
        out_shape=out_shape,
        in_specs=[pl.BlockSpec(memory_space=spaces[letter]) for letter in specs],
        out_specs=jax.tree.map(lambda _: pl.BlockSpec(memory_space=pltpu.VMEM), out_shape),
        scratch_shapes=list(scratch),
        input_output_aliases=aliases,
        compiler_params=pltpu.CompilerParams(vmem_limit_bytes=8 * MIB + room),
        cost_estimate=pl.CostEstimate(
            flops=cost[0], bytes_accessed=cost[1], transcendentals=0
        ),
        name=kernel.func.__name__,
    )(*args)


def body(
    amplitudes,
    coupling,
    integrals,
    row_energy,
    occ_energy,
    vir_energy,
    row_irrep,
    occ_irrep,
    vir_irrep,
):
    grid_size = lax.axis_size("grid")
    me = lax.axis_index("grid").astype(jnp.int32).reshape(1)
    rep = lax.axis_index("rep").astype(jnp.int32).reshape(1)
    rows_dev, depth = amplitudes.shape
    coupling = coupling.T
    columns = coupling.shape[0]
    edge = depth % LANES
    edge = jnp.pad(coupling[:, depth - edge :], ((0, 0), (0, LANES - edge)))
    count = columns // NOCC
    slab = rows_dev * grid_size
    width = NOCC // lax.axis_size("rep")

    walk = [*range(0, grid_size, 2), *range(1, grid_size, 2)[::-1]]
    onward = [(walk[i], walk[(i + 1) % grid_size]) for i in range(grid_size)]
    back = [(b, a) for a, b in onward]

    longer = grid_size // 2
    jobs = []
    halfway = None
    for number, at in enumerate(range(0, depth, K_BLOCK)):
        own = amplitudes[:, at : at + K_BLOCK]
        size = own.shape[1]
        own = jnp.pad(own, ((0, 0), (0, ceil_to(size, LANES) - size)))
        if halfway is not None:
            own, *_ = lax.optimization_barrier((own, *halfway))
        pieces, offsets, hop_ends = [own], [0], []
        hops = (longer, grid_size - 1 - longer)
        if number % 2:
            hops = hops[::-1]
        ahead = behind = own
        for hop in range(1, longer + 1):
            if hop <= hops[0]:
                ahead = lax.ppermute(ahead, "grid", onward)
                pieces.append(ahead)
                offsets.append(-hop)
            if hop <= hops[1]:
                behind = lax.ppermute(behind, "grid", back)
                pieces.append(behind)
                offsets.append(hop)
            hop_ends.append((ahead, behind))
        halfway = hop_ends[longer // 2 - 1]
        jobs.append((at, size // LANES * LANES, tuple(offsets), pieces, hop_ends))

    firsts = list(range(0, count, B_ROWS - 1))
    counts = [min(B_ROWS - 1, count - first) for first in firsts]
    bp = ceil_to(counts[0] + 1, 16)
    send_shape = jax.ShapeDtypeStruct((2, width, bp, slab), jnp.int16)
    lows = [first * NOCC // 16 * 16 for first in firsts]
    highs = [
        min(columns, ceil_to((first + number) * NOCC, 16)) for first, number in zip(firsts, counts)
    ]
    parts = [(low, high - low) for low, high in zip(lows, highs)]
    spans = [
        (first * NOCC - low, number, width) for first, low, number in zip(firsts, lows, counts)
    ]
    total_shapes = [
        jax.ShapeDtypeStruct(
            (slab // LANES, max(span[0] + bp * NOCC, ceil_to(part[1], C_BLOCK)), LANES),
            jnp.float32,
        )
        for span, part in zip(spans, parts)
    ]

    def work(many, size):
        return 2 * many * size * slab, 2 * many * size + 8 * many * slab

    room = 4 * K_BLOCK * ((C_BLOCK if columns % 16 == 0 else columns) + slab)
    sends = []
    totals = [()] * len(parts)
    for number, (at, whole, offsets, pieces, _) in enumerate(jobs):
        begin, last = number == 0, number + 1 == len(jobs)
        deep = pieces[0].shape[1]
        turned_shape = jax.ShapeDtypeStruct((deep, slab), jnp.bfloat16)
        scratch = [
            pltpu.VMEM((slab, deep), jnp.bfloat16),
            pltpu.SemaphoreType.DMA((len(pieces),)),
        ]
        if not last:
            ends = jobs[number + 1][4][longer // 2 - 1 :]
            pieces = lax.optimization_barrier((*pieces, *ends[0]))[: len(pieces)]
        for part, cols in enumerate(parts):
            span = spans[part] if last else None
            extra = (send_shape,) if last else ()
            cost = work(cols[1], deep)
            if part == 0:
                args = (me, rep, *pieces, coupling, edge, *totals[part])
                total, turned, *send = local_call(
                    functools.partial(lead_kernel, offsets, at, whole, cols, span, begin),
                    (total_shapes[part], turned_shape, *extra),
                    "ss" + "a" * (len(pieces) + 2) + "v" * len(totals[part]),
                    args,
                    scratch,
                    {} if begin else {len(args) - 1: 0},
                    cost,
                    room,
                )
            else:
                if not last:
                    turned, *_ = lax.optimization_barrier((turned, *ends[min(part, 1)]))
                args = (rep, turned, coupling, edge, *totals[part])
                total, *send = local_call(
                    functools.partial(rest_kernel, at, whole, cols, span, begin),
                    (total_shapes[part], *extra),
                    "svaa" + "v" * len(totals[part]),
                    args,
                    (),
                    {} if begin else {len(args) - 1: 0},
                    cost,
                    room,
                )
            totals[part] = (total,)
            sends.extend(send)
    totals = [total for total, in totals]

    low_pairs = [(i, i ^ 1) for i in range(lax.axis_size("rep"))]
    high_pairs = [(i, i ^ 2) for i in range(lax.axis_size("rep"))]
    pack = LANES // rows_dev
    groups = -(-width // pack)
    shape = (width, bp, slab)
    got = [lax.ppermute(send, "rep", low_pairs) for send in sends]
    sends, kept = [], []
    for span, total, mine in zip(spans, totals, got):
        if sends:
            mine, _ = lax.optimization_barrier((mine, sends[-1]))
        args = (rep, total, mine)
        sends.append(
            local_call(
                functools.partial(second_send_kernel, span),
                jax.ShapeDtypeStruct(shape, jnp.int16),
                "svv",
                args,
            )
        )
        kept.append(
            local_call(
                functools.partial(keep_kernel, span),
                jax.ShapeDtypeStruct(shape, jnp.float32),
                "svv",
                args,
            )
        )
    got = [lax.ppermute(send, "rep", high_pairs) for send in sends]
    arrived = []
    send = None
    for part, span in enumerate(spans):
        mine = kept[part]
        if send is not None:
            mine, _ = lax.optimization_barrier((mine, send))
        if part + 1 < len(spans):
            mine, _ = lax.optimization_barrier((mine, sends[part + 1]))
        send = local_call(
            functools.partial(third_send_kernel, span[1], rows_dev),
            jax.ShapeDtypeStruct((grid_size, groups, bp, LANES), jnp.int16),
            "vv",
            (mine, got[part]),
        )
        arrived.append(lax.all_to_all(send, "grid", split_axis=0, concat_axis=0, tiled=True))

    updated = local_call(
        functools.partial(update_kernel, counts, width, rows_dev),
        jax.ShapeDtypeStruct((width, rows_dev, count * grid_size), jnp.float32),
        "ss" + "v" * (len(arrived) + 5),
        (
            occ_energy,
            occ_irrep,
            *arrived,
            jnp.transpose(integrals, (1, 0, 2)),
            row_energy[:, None],
            vir_energy[None, :],
            row_irrep[:, None],
            vir_irrep[None, :],
        ),
        [pltpu.VMEM((count * grid_size, LANES), jnp.float32)],
    )
    return jnp.transpose(updated, (1, 0, 2))


def solution(mesh):
    return jax.shard_map(
        body,
        mesh=mesh,
        in_specs=(
            P("grid", "rep"),
            P("rep", "grid"),
            P("grid", "rep", None),
            P("grid"),
            P("rep"),
            P(),
            P("grid"),
            P("rep"),
            P(),
        ),
        out_specs=P("grid", "rep", None),
        check_vma=False,
    )
```

```python
import functools

import jax
import jax.numpy as jnp
from jax import lax
from jax.experimental import pallas as pl
from jax.experimental.pallas import tpu as pltpu
from jax.sharding import PartitionSpec as P

NOCC = 60
LANES = 128
K_BLOCK = 3840
C_BLOCK = 480
COPIES = 4
FIRST_PART = 47
STEPS = 8.0
TOP = 32767.0
MIB = 1024 * 1024


def ceil_to(value, unit):
    return -(-value // unit) * unit


def encode(rows, count):
    index = lax.broadcasted_iota(jnp.int32, rows.shape, 0)
    rows = jnp.where(index < count, rows, 0.0)
    largest = jnp.max(jnp.abs(rows), axis=0, keepdims=True)
    level = jnp.ceil(jnp.log2(jnp.maximum(largest, 1e-30)) * STEPS) + 1.0
    coded = jnp.floor(rows * (jnp.exp2(level * (-1.0 / STEPS)) * TOP) + 0.5)
    return jnp.where(index == count, level, coded)


def decode(block, count):
    index = lax.broadcasted_iota(jnp.int32, block.shape, 0)
    scale = jnp.exp2(block[count : count + 1] * (1.0 / STEPS)) * (1.0 / TOP)
    return jnp.where(index < count, block * scale, 0.0)


def to_code(block):
    return block.astype(jnp.int32).astype(jnp.int16)


def from_code(block):
    return block.astype(jnp.int32).astype(jnp.float32)


def walk_index(place, size):
    return jnp.where(place < size // 2, 2 * place, 2 * (size - 1 - place) + 1)


def walk_place(index, size):
    return jnp.where(index % 2 == 0, index // 2, size - 1 - index // 2)


def coupling_copies(coupling_ref, edge_ref, buffer, sems, low, start, slot):
    block = buffer.shape[1]
    whole = buffer.shape[2] - LANES
    rows = pl.ds(pl.multiple_of(low + start, 16), block)
    quarter = ceil_to(-(-whole // COPIES), 256)
    copies = []
    for number, k in enumerate(range(0, whole, quarter)):
        pairs = pl.ds(k, min(quarter, whole - k))
        copies.append(
            pltpu.make_async_copy(
                coupling_ref.at[rows, pairs], buffer.at[slot, :, pairs], sems.at[slot, number]
            )
        )
    copies.append(
        pltpu.make_async_copy(
            edge_ref.at[rows, :], buffer.at[slot, :, pl.ds(whole, LANES)], sems.at[slot, COPIES]
        )
    )
    return copies


def multiply(coupling_ref, edge_ref, buffer, sems, turned, total_ref, columns, before=None):
    low, many = columns
    block = buffer.shape[1]
    steps = -(-many // block)

    def copies(step):
        start = jnp.minimum(step * block, many - block)
        return coupling_copies(coupling_ref, edge_ref, buffer, sems, low, start, lax.rem(step, 2))

    for copy in copies(jnp.int32(0)):
        copy.start()
    if before is not None:
        before()

    def step(number, carry):
        @pl.when(number + 1 < steps)
        def _():
            for copy in copies(number + 1):
                copy.start()

        for copy in copies(number):
            copy.wait()
        total = jnp.dot(
            buffer[lax.rem(number, 2)], turned[...], preferred_element_type=jnp.float32
        )
        rows = pl.ds(pl.multiple_of(jnp.minimum(number * block, many - block), 4), block)
        for part in range(total_ref.shape[0]):
            total_ref[part, rows, :] = total[:, part * LANES : (part + 1) * LANES]
        return carry

    lax.fori_loop(0, steps, step, 0)


def gather_pieces(me_ref, offsets, edges, pieces, gathered, turned, sems):
    rows = pieces[0].shape[0]
    grid_size = gathered.shape[0] // rows
    place = walk_place(me_ref[0], grid_size)
    copies = []
    for number, (offset, edge, piece) in enumerate(zip(offsets, edges, pieces)):
        source = walk_index(lax.rem(place + offset + grid_size, grid_size), grid_size)
        target = gathered.at[
            pl.ds(pl.multiple_of(source * rows, rows), rows), pl.ds(edge, piece.shape[1])
        ]
        copies.append(pltpu.make_async_copy(piece, target, sems.at[number]))
    for copy in copies:
        copy.start()
    for copy in copies:
        copy.wait()
    for at in range(0, turned.shape[0], LANES):
        turned[at : at + LANES, :] = gathered[:, at : at + LANES].T


def lead_kernel(offsets, edges, columns, span, me_ref, rep_ref, *refs):
    pieces, refs = refs[: len(offsets)], refs[len(offsets) :]
    coupling_ref, edge_ref, total, turned, send, gathered, sems, buffer, buffer_sems = refs
    multiply(
        coupling_ref,
        edge_ref,
        buffer,
        buffer_sems,
        turned,
        total,
        columns,
        lambda: gather_pieces(me_ref, offsets, edges, pieces, gathered, turned, sems),
    )
    first_send(span, rep_ref, total, send)


def rest_kernel(columns, span, rep_ref, turned, coupling_ref, edge_ref, total, send, buffer, sems):
    multiply(coupling_ref, edge_ref, buffer, sems, turned, total, columns)
    first_send(span, rep_ref, total, send)


def column_rows(total_ref, width, part, j, offset, bp):
    rows = pl.ds(offset + part * width + j, bp, stride=NOCC)
    return jnp.concatenate([total_ref[h, rows, :] for h in range(total_ref.shape[0])], axis=1)


def first_send(span, rep_ref, total_ref, out_ref):
    offset, count, width = span
    low = rep_ref[0] % 2

    def step(j, carry):
        for high in range(2):
            rows = column_rows(total_ref, width, 2 * high + 1 - low, j, offset, out_ref.shape[2])
            out_ref[high, j] = to_code(encode(rows, count))
        return carry

    lax.fori_loop(0, width, step, 0)


def second_send_kernel(span, rep_ref, total_ref, got_ref, out_ref):
    offset, count, width = span
    low, high = rep_ref[0] % 2, 1 - rep_ref[0] // 2

    def step(j, carry):
        rows = column_rows(total_ref, width, 2 * high + low, j, offset, out_ref.shape[1])
        rows = rows + decode(from_code(got_ref[high, j]), count)
        out_ref[j] = to_code(encode(rows, count))
        return carry

    lax.fori_loop(0, width, step, 0)


def keep_kernel(span, rep_ref, total_ref, got_ref, out_ref):
    offset, count, width = span
    low, high = rep_ref[0] % 2, rep_ref[0] // 2

    def step(j, carry):
        rows = column_rows(total_ref, width, 2 * high + low, j, offset, out_ref.shape[1])
        out_ref[j] = rows + decode(from_code(got_ref[high, j]), count)
        return carry

    lax.fori_loop(0, width, step, 0)


def pack_rows(count, rows_dev, kept_ref, got_ref, stage):
    pack = LANES // rows_dev
    groups = stage.shape[1]
    size, _, slab = kept_ref.shape

    def step(jj, carry):
        coded = []
        for jq in range(pack):
            j = jnp.minimum(jq * groups + jj, size - 1)
            coded.append(encode(kept_ref[j] + decode(from_code(got_ref[j]), count), count))
        for g in range(slab // rows_dev):
            own = [block[:, g * rows_dev : (g + 1) * rows_dev] for block in coded]
            stage[g, jj] = to_code(jnp.concatenate(own, axis=1))
        return carry

    lax.fori_loop(0, groups, step, 0)


def third_send_kernel(count, rows_dev, kept_ref, got_ref, stage):
    pack_rows(count, rows_dev, kept_ref, got_ref, stage)


def last_send_kernel(count, rows_dev, parts, me_ref, kept_ref, got_ref, *refs):
    earlier, targets, stage = refs[: parts - 1], refs[parts - 1 : -1], refs[-1]
    pack_rows(count, rows_dev, kept_ref, got_ref, stage)
    for number, target in enumerate(targets):
        at = 0
        for source in (*earlier, stage):
            bp = source.shape[2]
            target[:, at : at + bp, :] = source[me_ref[0] ^ number]
            at += bp


def update_kernel(counts, bps, width, rows_dev, me_ref, occ_energy_ref, occ_irrep_ref, *refs):
    (
        integrals_ref,
        row_energy_ref,
        vir_energy_ref,
        row_irrep_ref,
        vir_irrep_ref,
        out_ref,
        blocks,
        stage,
    ) = refs[-8:]
    arrived = refs[:-8]
    for number, got_ref in enumerate(arrived):
        blocks[me_ref[0] ^ number] = got_ref[...]
    pack = LANES // rows_dev
    for jj in range(blocks.shape[1]):
        at = 0
        for g in range(len(arrived)):
            row = 0
            for count, bp in zip(counts, bps):
                block = decode(from_code(blocks[g, jj, row : row + bp, :]), count)
                stage[at : at + count, :] = block[:count]
                at += count
                row += bp
        turned = stage[...].T
        for jq in range(pack):
            j = jq * blocks.shape[1] + jj
            if j >= width:
                continue
            cycle = turned[jq * rows_dev : (jq + 1) * rows_dev]
            denominator = row_energy_ref[...] + occ_energy_ref[j] - vir_energy_ref[...]
            labels = row_irrep_ref[...] ^ occ_irrep_ref[j] ^ vir_irrep_ref[...]
            out_ref[j] = jnp.where(
                labels == 0, (integrals_ref[j] + cycle) / denominator, jnp.float32(0.0)
            )


def local_call(kernel, out_shape, specs, args, scratch=(), aliases={}, cost=(10**7, 4 * 10**6), room=0):
    spaces = {"s": pltpu.SMEM, "v": pltpu.VMEM, "a": pl.ANY}
    return pl.pallas_call(
        kernel,
        out_shape=out_shape,
        in_specs=[pl.BlockSpec(memory_space=spaces[letter]) for letter in specs],
        out_specs=jax.tree.map(lambda _: pl.BlockSpec(memory_space=pltpu.VMEM), out_shape),
        scratch_shapes=list(scratch),
        input_output_aliases=aliases,
        compiler_params=pltpu.CompilerParams(vmem_limit_bytes=8 * MIB + room),
        cost_estimate=pl.CostEstimate(
            flops=cost[0], bytes_accessed=cost[1], transcendentals=0
        ),
        name=kernel.func.__name__,
    )(*args)


def body(
    amplitudes,
    coupling,
    integrals,
    row_energy,
    occ_energy,
    vir_energy,
    row_irrep,
    occ_irrep,
    vir_irrep,
):
    grid_size = lax.axis_size("grid")
    me = lax.axis_index("grid").astype(jnp.int32).reshape(1)
    rep = lax.axis_index("rep").astype(jnp.int32).reshape(1)
    rows_dev, depth = amplitudes.shape
    coupling = coupling.T
    columns = coupling.shape[0]
    count = columns // NOCC
    ragged = ceil_to(columns, 16) - columns
    if ragged:
        coupling = jnp.pad(coupling, ((0, ragged), (0, 0)))
        columns += ragged
    edge = depth % LANES
    edge = jnp.pad(coupling[:, depth - edge :], ((0, 0), (0, LANES - edge)))
    slab = rows_dev * grid_size
    width = NOCC // lax.axis_size("rep")

    walk = [*range(0, grid_size, 2), *range(1, grid_size, 2)[::-1]]
    onward = [(walk[i], walk[(i + 1) % grid_size]) for i in range(grid_size)]
    back = [(b, a) for a, b in onward]

    longer = grid_size // 2
    pieces, offsets, edges = [], [], []
    for number, at in enumerate(range(0, depth, K_BLOCK)):
        own = amplitudes[:, at : at + K_BLOCK]
        size = own.shape[1]
        own = jnp.pad(own, ((0, 0), (0, ceil_to(size, LANES) - size)))
        hops = (longer, grid_size - 1 - longer)
        if number % 2:
            hops = hops[::-1]
        ahead = behind = own
        pieces.append(own)
        offsets.append(0)
        for hop in range(1, longer + 1):
            if hop <= hops[0]:
                ahead = lax.ppermute(ahead, "grid", onward)
                pieces.append(ahead)
                offsets.append(-hop)
            if hop <= hops[1]:
                behind = lax.ppermute(behind, "grid", back)
                pieces.append(behind)
                offsets.append(hop)
        edges += [at] * grid_size

    counts = [FIRST_PART, count - FIRST_PART] if count > FIRST_PART else [count]
    firsts = [0, FIRST_PART][: len(counts)]
    bps = [ceil_to(number + 1, 16) for number in counts]
    lows = [first * NOCC // 16 * 16 for first in firsts]
    highs = [
        min(columns, ceil_to((first + number) * NOCC, 16)) for first, number in zip(firsts, counts)
    ]
    parts = [(low, high - low) for low, high in zip(lows, highs)]
    spans = [
        (first * NOCC - low, number, width) for first, low, number in zip(firsts, lows, counts)
    ]
    total_shapes = [
        jax.ShapeDtypeStruct((slab // LANES, max(span[0] + bp * NOCC, part[1]), LANES), jnp.float32)
        for span, part, bp in zip(spans, parts, bps)
    ]
    send_shapes = [jax.ShapeDtypeStruct((2, width, bp, slab), jnp.int16) for bp in bps]
    deep = ceil_to(depth, LANES)
    low_pairs = [(i, i ^ 1) for i in range(lax.axis_size("rep"))]
    high_pairs = [(i, i ^ 2) for i in range(lax.axis_size("rep"))]

    totals, sends, got = [], [], []
    for part, (cols, span, bp) in enumerate(zip(parts, spans, bps)):
        block = min(C_BLOCK, ceil_to(cols[1] // 2, 16))
        scratch = [
            pltpu.VMEM((2, block, deep), jnp.bfloat16),
            pltpu.SemaphoreType.DMA((2, COPIES + 1)),
        ]
        cost = (2 * cols[1] * deep * slab, 2 * cols[1] * deep)
        room = 4 * block * deep + (2 * slab * deep if part == 0 else 0)
        if slab > 2 * LANES:
            room += 2 * slab * deep + 4 * slab * total_shapes[part].shape[1]
        if part == 0:
            total, turned, send = local_call(
                functools.partial(lead_kernel, tuple(offsets), tuple(edges), cols, span),
                (
                    total_shapes[0],
                    jax.ShapeDtypeStruct((deep, slab), jnp.bfloat16),
                    send_shapes[0],
                ),
                "ss" + "a" * (len(pieces) + 2),
                (me, rep, *pieces, coupling, edge),
                [
                    pltpu.VMEM((slab, deep), jnp.bfloat16),
                    pltpu.SemaphoreType.DMA((len(pieces),)),
                    *scratch,
                ],
                cost=cost,
                room=room,
            )
        else:
            turned, _ = lax.optimization_barrier((turned, sends[0]))
            total, send = local_call(
                functools.partial(rest_kernel, cols, span),
                (total_shapes[part], send_shapes[part]),
                "svaa",
                (rep, turned, coupling, edge),
                scratch,
                cost=cost,
                room=room,
            )
        arrived = lax.ppermute(send, "rep", low_pairs)
        totals.append(total)
        got.append(arrived)
        sends.append(
            local_call(
                functools.partial(second_send_kernel, span),
                jax.ShapeDtypeStruct((width, bp, slab), jnp.int16),
                "svv",
                (rep, total, arrived),
            )
        )
    kept = [
        local_call(
            functools.partial(keep_kernel, span),
            jax.ShapeDtypeStruct((width, bp, slab), jnp.float32),
            "svv",
            (rep, total, arrived),
        )
        for span, bp, total, arrived in zip(spans, bps, totals, got)
    ]
    got = [lax.ppermute(send, "rep", high_pairs) for send in sends]

    groups = -(-width // (LANES // rows_dev))
    staged = []
    for part, span in enumerate(spans[:-1]):
        mine, _ = lax.optimization_barrier((kept[part], sends[-1]))
        staged.append(
            local_call(
                functools.partial(third_send_kernel, span[1], rows_dev),
                jax.ShapeDtypeStruct((grid_size, groups, bps[part], LANES), jnp.int16),
                "vv",
                (mine, got[part]),
            )
        )
    targets = local_call(
        functools.partial(last_send_kernel, counts[-1], rows_dev, len(counts)),
        (jax.ShapeDtypeStruct((groups, sum(bps), LANES), jnp.int16),) * grid_size,
        "svv" + "v" * len(staged),
        (me, kept[-1], got[-1], *staged),
        [pltpu.VMEM((grid_size, groups, bps[-1], LANES), jnp.int16)],
    )
    arrived = [targets[0]] + [
        lax.ppermute(target, "grid", [(g, g ^ number) for g in range(grid_size)])
        for number, target in list(enumerate(targets))[1:]
    ]

    updated = local_call(
        functools.partial(update_kernel, counts, bps, width, rows_dev),
        jax.ShapeDtypeStruct((width, rows_dev, count * grid_size), jnp.float32),
        "sss" + "v" * (len(arrived) + 5),
        (
            me,
            occ_energy,
            occ_irrep,
            *arrived,
            jnp.transpose(integrals, (1, 0, 2)),
            row_energy[:, None],
            vir_energy[None, :],
            row_irrep[:, None],
            vir_irrep[None, :],
        ),
        [
            pltpu.VMEM((grid_size, groups, sum(bps), LANES), jnp.int16),
            pltpu.VMEM((count * grid_size, LANES), jnp.float32),
        ],
    )
    return jnp.transpose(updated, (1, 0, 2))


def solution(mesh):
    return jax.shard_map(
        body,
        mesh=mesh,
        in_specs=(
            P("grid", "rep"),
            P("rep", "grid"),
            P("grid", "rep", None),
            P("grid"),
            P("rep"),
            P(),
            P("grid"),
            P("rep"),
            P(),
        ),
        out_specs=P("grid", "rep", None),
        check_vma=False,
    )
```

```python
import functools

import jax
import jax.numpy as jnp
from jax import lax
from jax.experimental import pallas as pl
from jax.experimental.pallas import tpu as pltpu
from jax.sharding import PartitionSpec as P

NOCC = 60
LANES = 128
K_BLOCK = 3840
C_BLOCK = 480
SLOTS = 3
COPIES = 4
FIRST_PART = 47
STEPS = 8.0
TOP = 32767.0
MIB = 1024 * 1024


def ceil_to(value, unit):
    return -(-value // unit) * unit


def encode(rows, count):
    index = lax.broadcasted_iota(jnp.int32, rows.shape, 0)
    rows = jnp.where(index < count, rows, 0.0)
    largest = jnp.max(jnp.abs(rows), axis=0, keepdims=True)
    level = jnp.ceil(jnp.log2(jnp.maximum(largest, 1e-30)) * STEPS) + 1.0
    coded = jnp.floor(rows * (jnp.exp2(level * (-1.0 / STEPS)) * TOP) + 0.5)
    return jnp.where(index == count, level, coded)


def decode(block, count):
    index = lax.broadcasted_iota(jnp.int32, block.shape, 0)
    scale = jnp.exp2(block[count : count + 1] * (1.0 / STEPS)) * (1.0 / TOP)
    return jnp.where(index < count, block * scale, 0.0)


def to_code(block):
    return block.astype(jnp.int32).astype(jnp.int16)


def from_code(block):
    return block.astype(jnp.int32).astype(jnp.float32)


def walk_index(place, size):
    return jnp.where(place < size // 2, 2 * place, 2 * (size - 1 - place) + 1)


def walk_place(index, size):
    return jnp.where(index % 2 == 0, index // 2, size - 1 - index // 2)


def coupling_copies(coupling_ref, edge_ref, buffer, sems, low, start, slot):
    block = buffer.shape[1]
    whole = buffer.shape[2] - LANES
    rows = pl.ds(pl.multiple_of(low + start, 16), block)
    quarter = ceil_to(-(-whole // COPIES), 256)
    copies = []
    for number, k in enumerate(range(0, whole, quarter)):
        pairs = pl.ds(k, min(quarter, whole - k))
        copies.append(
            pltpu.make_async_copy(
                coupling_ref.at[rows, pairs], buffer.at[slot, :, pairs], sems.at[slot, number]
            )
        )
    copies.append(
        pltpu.make_async_copy(
            edge_ref.at[rows, :], buffer.at[slot, :, pl.ds(whole, LANES)], sems.at[slot, COPIES]
        )
    )
    return copies


def multiply(coupling_ref, edge_ref, buffer, sems, turned, total_ref, columns, before=None):
    low, many = columns
    block = buffer.shape[1]
    steps = -(-many // block)

    def copies(step):
        start = jnp.minimum(step * block, many - block)
        return coupling_copies(coupling_ref, edge_ref, buffer, sems, low, start, lax.rem(step, SLOTS))

    for ahead in range(min(SLOTS - 1, steps)):
        for copy in copies(jnp.int32(ahead)):
            copy.start()
    if before is not None:
        before()

    def step(number, carry):
        @pl.when(number + SLOTS - 1 < steps)
        def _():
            for copy in copies(number + SLOTS - 1):
                copy.start()

        for copy in copies(number):
            copy.wait()
        total = jnp.dot(
            buffer[lax.rem(number, SLOTS)], turned[...], preferred_element_type=jnp.float32
        )
        rows = pl.ds(pl.multiple_of(jnp.minimum(number * block, many - block), 4), block)
        for part in range(total_ref.shape[0]):
            total_ref[part, rows, :] = total[:, part * LANES : (part + 1) * LANES]
        return carry

    lax.fori_loop(0, steps, step, 0)


def turn_pieces(edges, pieces, gathered, sems, turned, lanes):
    rows = pieces[0].shape[0]
    slots = gathered.shape[0] // rows
    copies = []
    for number, (edge, piece) in enumerate(zip(edges, pieces)):
        target = gathered.at[
            pl.ds(number % slots * rows, rows), pl.ds(edge, piece.shape[1])
        ]
        copies.append(pltpu.make_async_copy(piece, target, sems.at[number]))
    for copy in copies:
        copy.start()
    for copy in copies:
        copy.wait()
    for at in range(0, turned.shape[0], LANES):
        turned[at : at + LANES, lanes : lanes + slots * rows] = gathered[:, at : at + LANES].T


def near_kernel(edges, *refs):
    *pieces, turned, gathered, sems = refs
    turn_pieces(edges, pieces, gathered, sems, turned, 0)


def lead_kernel(edges, columns, span, rep_ref, near, *refs):
    pieces, refs = refs[: len(edges)], refs[len(edges) :]
    coupling_ref, edge_ref, total, turned, send, gathered, sems, buffer, buffer_sems = refs

    def before():
        lanes = near.shape[1]
        turned[:, :lanes] = near[...]
        turn_pieces(edges, pieces, gathered, sems, turned, lanes)

    multiply(coupling_ref, edge_ref, buffer, buffer_sems, turned, total, columns, before)
    first_send(span, rep_ref, total, send)


def rest_kernel(columns, span, rep_ref, turned, coupling_ref, edge_ref, total, send, buffer, sems):
    multiply(coupling_ref, edge_ref, buffer, sems, turned, total, columns)
    first_send(span, rep_ref, total, send)


def column_rows(total_ref, width, part, j, offset, bp):
    rows = pl.ds(offset + part * width + j, bp, stride=NOCC)
    return jnp.concatenate([total_ref[h, rows, :] for h in range(total_ref.shape[0])], axis=1)


def first_send(span, rep_ref, total_ref, out_ref):
    offset, count, width = span
    low = rep_ref[0] % 2

    def step(j, carry):
        for high in range(2):
            rows = column_rows(total_ref, width, 2 * high + 1 - low, j, offset, out_ref.shape[2])
            out_ref[high, j] = to_code(encode(rows, count))
        return carry

    lax.fori_loop(0, width, step, 0)


def second_send_kernel(span, rep_ref, total_ref, got_ref, out_ref):
    offset, count, width = span
    low, high = rep_ref[0] % 2, 1 - rep_ref[0] // 2

    def step(j, carry):
        rows = column_rows(total_ref, width, 2 * high + low, j, offset, out_ref.shape[1])
        rows = rows + decode(from_code(got_ref[high, j]), count)
        out_ref[j] = to_code(encode(rows, count))
        return carry

    lax.fori_loop(0, width, step, 0)


def keep_kernel(span, rep_ref, total_ref, got_ref, out_ref):
    offset, count, width = span
    low, high = rep_ref[0] % 2, rep_ref[0] // 2

    def step(j, carry):
        rows = column_rows(total_ref, width, 2 * high + low, j, offset, out_ref.shape[1])
        out_ref[j] = rows + decode(from_code(got_ref[high, j]), count)
        return carry

    lax.fori_loop(0, width, step, 0)


def pack_rows(count, rows_dev, kept_ref, got_ref, stage):
    pack = LANES // rows_dev
    groups = stage.shape[1]
    size, _, slab = kept_ref.shape

    def step(jj, carry):
        coded = []
        for jq in range(pack):
            j = jnp.minimum(jq * groups + jj, size - 1)
            coded.append(encode(kept_ref[j] + decode(from_code(got_ref[j]), count), count))
        for g in range(slab // rows_dev):
            own = [block[:, g * rows_dev : (g + 1) * rows_dev] for block in coded]
            stage[g, jj] = to_code(jnp.concatenate(own, axis=1))
        return carry

    lax.fori_loop(0, groups, step, 0)


def third_send_kernel(count, rows_dev, kept_ref, got_ref, stage):
    pack_rows(count, rows_dev, kept_ref, got_ref, stage)


def last_send_kernel(count, rows_dev, parts, kept_ref, got_ref, *refs):
    earlier, targets, stage = refs[: parts - 1], refs[parts - 1 : -1], refs[-1]
    pack_rows(count, rows_dev, kept_ref, got_ref, stage)
    for number, target in enumerate(targets):
        at = 0
        for source in (*earlier, stage):
            bp = source.shape[2]
            target[:, at : at + bp, :] = source[number]
            at += bp


def update_kernel(counts, bps, width, rows_dev, order, me_ref, occ_energy_ref, occ_irrep_ref, *refs):
    (
        integrals_ref,
        row_energy_ref,
        vir_energy_ref,
        row_irrep_ref,
        vir_irrep_ref,
        out_ref,
        blocks,
        stage,
    ) = refs[-8:]
    arrived = refs[:-8]
    grid_size = len(arrived)
    place = walk_place(me_ref[0], grid_size)
    for offset, got_ref in zip(order, arrived):
        source = walk_index(lax.rem(place - offset + grid_size, grid_size), grid_size)
        blocks[source] = got_ref[...]
    pack = LANES // rows_dev
    for jj in range(blocks.shape[1]):
        at = 0
        for g in range(len(arrived)):
            row = 0
            for count, bp in zip(counts, bps):
                block = decode(from_code(blocks[g, jj, row : row + bp, :]), count)
                stage[at : at + count, :] = block[:count]
                at += count
                row += bp
        turned = stage[...].T
        for jq in range(pack):
            j = jq * blocks.shape[1] + jj
            if j >= width:
                continue
            cycle = turned[jq * rows_dev : (jq + 1) * rows_dev]
            denominator = row_energy_ref[...] + occ_energy_ref[j] - vir_energy_ref[...]
            labels = row_irrep_ref[...] ^ occ_irrep_ref[j] ^ vir_irrep_ref[...]
            out_ref[j] = jnp.where(
                labels == 0, (integrals_ref[j] + cycle) / denominator, jnp.float32(0.0)
            )


def local_call(kernel, out_shape, specs, args, scratch=(), aliases={}, cost=(10**7, 4 * 10**6), room=0):
    spaces = {"s": pltpu.SMEM, "v": pltpu.VMEM, "a": pl.ANY}
    return pl.pallas_call(
        kernel,
        out_shape=out_shape,
        in_specs=[pl.BlockSpec(memory_space=spaces[letter]) for letter in specs],
        out_specs=jax.tree.map(lambda _: pl.BlockSpec(memory_space=pltpu.VMEM), out_shape),
        scratch_shapes=list(scratch),
        input_output_aliases=aliases,
        compiler_params=pltpu.CompilerParams(vmem_limit_bytes=8 * MIB + room),
        cost_estimate=pl.CostEstimate(
            flops=cost[0], bytes_accessed=cost[1], transcendentals=0
        ),
        name=kernel.func.__name__,
    )(*args)


def body(
    amplitudes,
    coupling,
    integrals,
    row_energy,
    occ_energy,
    vir_energy,
    row_irrep,
    occ_irrep,
    vir_irrep,
):
    grid_size = lax.axis_size("grid")
    me = lax.axis_index("grid").astype(jnp.int32).reshape(1)
    rep = lax.axis_index("rep").astype(jnp.int32).reshape(1)
    rows_dev, depth = amplitudes.shape
    coupling = coupling.T
    columns = coupling.shape[0]
    count = columns // NOCC
    ragged = ceil_to(columns, 16) - columns
    if ragged:
        coupling = jnp.pad(coupling, ((0, ragged), (0, 0)))
        columns += ragged
    edge = depth % LANES
    edge = jnp.pad(coupling[:, depth - edge :], ((0, 0), (0, LANES - edge)))
    slab = rows_dev * grid_size
    width = NOCC // lax.axis_size("rep")

    walk = [*range(0, grid_size, 2), *range(1, grid_size, 2)[::-1]]
    onward = [(walk[i], walk[(i + 1) % grid_size]) for i in range(grid_size)]
    back = [(b, a) for a, b in onward]

    longer = grid_size // 2
    order = [0]
    for hop in range(1, longer):
        order += [-hop, hop]
    order.append(longer)
    near, far, near_edges, far_edges = [], [], [], []
    for number, at in enumerate(range(0, depth, K_BLOCK)):
        own = amplitudes[:, at : at + K_BLOCK]
        size = own.shape[1]
        own = jnp.pad(own, ((0, 0), (0, ceil_to(size, LANES) - size)))
        ahead = behind = own
        pieces = [own]
        for hop in range(1, longer + 1):
            if hop < longer or number % 2 == 0:
                ahead = lax.ppermute(ahead, "grid", onward)
                pieces.append(ahead)
            if hop < longer or number % 2 == 1:
                behind = lax.ppermute(behind, "grid", back)
                pieces.append(behind)
        near += pieces[:longer]
        far += pieces[longer:]
        near_edges += [at] * longer
        far_edges += [at] * longer

    counts = [FIRST_PART, count - FIRST_PART] if count > FIRST_PART else [count]
    firsts = [0, FIRST_PART][: len(counts)]
    bps = [ceil_to(number + 1, 16) for number in counts]
    lows = [first * NOCC // 16 * 16 for first in firsts]
    highs = [
        min(columns, ceil_to((first + number) * NOCC, 16)) for first, number in zip(firsts, counts)
    ]
    parts = [(low, high - low) for low, high in zip(lows, highs)]
    spans = [
        (first * NOCC - low, number, width) for first, low, number in zip(firsts, lows, counts)
    ]
    total_shapes = [
        jax.ShapeDtypeStruct((slab // LANES, max(span[0] + bp * NOCC, part[1]), LANES), jnp.float32)
        for span, part, bp in zip(spans, parts, bps)
    ]
    send_shapes = [jax.ShapeDtypeStruct((2, width, bp, slab), jnp.int16) for bp in bps]
    deep = ceil_to(depth, LANES)
    low_pairs = [(i, i ^ 1) for i in range(lax.axis_size("rep"))]
    high_pairs = [(i, i ^ 2) for i in range(lax.axis_size("rep"))]

    half = slab // 2
    turn_scratch = [
        pltpu.VMEM((half, deep), jnp.bfloat16),
        pltpu.SemaphoreType.DMA((len(near),)),
    ]
    near = local_call(
        functools.partial(near_kernel, tuple(near_edges)),
        jax.ShapeDtypeStruct((deep, half), jnp.bfloat16),
        "a" * len(near),
        near,
        turn_scratch,
        cost=(10**8, 4 * half * deep),
        room=2 * half * deep + (2 * half * deep if slab > 2 * LANES else 0),
    )
    totals, sends, got = [], [], []
    for part, (cols, span, bp) in enumerate(zip(parts, spans, bps)):
        block = min(C_BLOCK, ceil_to(cols[1] // 2, 16))
        scratch = [
            pltpu.VMEM((SLOTS, block, deep), jnp.bfloat16),
            pltpu.SemaphoreType.DMA((SLOTS, COPIES + 1)),
        ]
        cost = (2 * cols[1] * deep * slab, 2 * cols[1] * deep)
        room = 2 * SLOTS * block * deep + (slab * deep if part == 0 else 0)
        if slab > 2 * LANES:
            room += 3 * slab * deep + 4 * slab * total_shapes[part].shape[1]
        if part == 0:
            total, turned, send = local_call(
                functools.partial(lead_kernel, tuple(far_edges), cols, span),
                (
                    total_shapes[0],
                    jax.ShapeDtypeStruct((deep, slab), jnp.bfloat16),
                    send_shapes[0],
                ),
                "sv" + "a" * (len(far) + 2),
                (rep, near, *far, coupling, edge),
                [*turn_scratch, *scratch],
                cost=cost,
                room=room,
            )
        else:
            turned, _ = lax.optimization_barrier((turned, sends[0]))
            total, send = local_call(
                functools.partial(rest_kernel, cols, span),
                (total_shapes[part], send_shapes[part]),
                "svaa",
                (rep, turned, coupling, edge),
                scratch,
                cost=cost,
                room=room,
            )
        arrived = lax.ppermute(send, "rep", low_pairs)
        totals.append(total)
        got.append(arrived)
        sends.append(
            local_call(
                functools.partial(second_send_kernel, span),
                jax.ShapeDtypeStruct((width, bp, slab), jnp.int16),
                "svv",
                (rep, total, arrived),
            )
        )
    kept = [
        local_call(
            functools.partial(keep_kernel, span),
            jax.ShapeDtypeStruct((width, bp, slab), jnp.float32),
            "svv",
            (rep, total, arrived),
        )
        for span, bp, total, arrived in zip(spans, bps, totals, got)
    ]
    got = [lax.ppermute(send, "rep", high_pairs) for send in sends]

    groups = -(-width // (LANES // rows_dev))
    staged = []
    for part, span in enumerate(spans[:-1]):
        mine, _ = lax.optimization_barrier((kept[part], sends[-1]))
        staged.append(
            local_call(
                functools.partial(third_send_kernel, span[1], rows_dev),
                jax.ShapeDtypeStruct((grid_size, groups, bps[part], LANES), jnp.int16),
                "vv",
                (mine, got[part]),
            )
        )
    targets = local_call(
        functools.partial(last_send_kernel, counts[-1], rows_dev, len(counts)),
        (jax.ShapeDtypeStruct((groups, sum(bps), LANES), jnp.int16),) * grid_size,
        "vv" + "v" * len(staged),
        (kept[-1], got[-1], *staged),
        [pltpu.VMEM((grid_size, groups, bps[-1], LANES), jnp.int16)],
    )
    arrived = list(targets)
    for number in range(1, grid_size)[::-1]:
        arrived[number] = lax.ppermute(
            targets[number],
            "grid",
            [(walk[i], walk[(i + order[number]) % grid_size]) for i in range(grid_size)],
        )

    updated = local_call(
        functools.partial(update_kernel, counts, bps, width, rows_dev, order),
        jax.ShapeDtypeStruct((width, rows_dev, count * grid_size), jnp.float32),
        "sss" + "v" * (len(arrived) + 5),
        (
            me,
            occ_energy,
            occ_irrep,
            *arrived,
            jnp.transpose(integrals, (1, 0, 2)),
            row_energy[:, None],
            vir_energy[None, :],
            row_irrep[:, None],
            vir_irrep[None, :],
        ),
        [
            pltpu.VMEM((grid_size, groups, sum(bps), LANES), jnp.int16),
            pltpu.VMEM((count * grid_size, LANES), jnp.float32),
        ],
    )
    return jnp.transpose(updated, (1, 0, 2))


def solution(mesh):
    return jax.shard_map(
        body,
        mesh=mesh,
        in_specs=(
            P("grid", "rep"),
            P("rep", "grid"),
            P("grid", "rep", None),
            P("grid"),
            P("rep"),
            P(),
            P("grid"),
            P("rep"),
            P(),
        ),
        out_specs=P("grid", "rep", None),
        check_vma=False,
    )
```

```python
import functools

import jax
import jax.numpy as jnp
from jax import lax
from jax.experimental import pallas as pl
from jax.experimental.pallas import tpu as pltpu
from jax.sharding import PartitionSpec as P

NOCC = 60
LANES = 128
K_BLOCK = 3840
C_BLOCK = 480
SLOTS = 3
EARLY = 3
COPIES = 4
FIRST_PART = 47
STEPS = 8.0
TOP = 32767.0
MIB = 1024 * 1024


def ceil_to(value, unit):
    return -(-value // unit) * unit


def encode(rows, count):
    index = lax.broadcasted_iota(jnp.int32, rows.shape, 0)
    rows = jnp.where(index < count, rows, 0.0)
    largest = jnp.max(jnp.abs(rows), axis=0, keepdims=True)
    level = jnp.ceil(jnp.log2(jnp.maximum(largest, 1e-30)) * STEPS) + 1.0
    coded = jnp.floor(rows * (jnp.exp2(level * (-1.0 / STEPS)) * TOP) + 0.5)
    return jnp.where(index == count, level, coded)


def decode(block, count):
    index = lax.broadcasted_iota(jnp.int32, block.shape, 0)
    scale = jnp.exp2(block[count : count + 1] * (1.0 / STEPS)) * (1.0 / TOP)
    return jnp.where(index < count, block * scale, 0.0)


def to_code(block):
    return block.astype(jnp.int32).astype(jnp.int16)


def from_code(block):
    return block.astype(jnp.int32).astype(jnp.float32)


def walk_index(place, size):
    return jnp.where(place < size // 2, 2 * place, 2 * (size - 1 - place) + 1)


def walk_place(index, size):
    return jnp.where(index % 2 == 0, index // 2, size - 1 - index // 2)


def coupling_copies(coupling_ref, edge_ref, buffer, sems, low, start, slot):
    block = buffer.shape[1]
    whole = buffer.shape[2] - LANES
    rows = pl.ds(pl.multiple_of(low + start, 16), block)
    quarter = ceil_to(-(-whole // COPIES), 256)
    copies = []
    for number, k in enumerate(range(0, whole, quarter)):
        pairs = pl.ds(k, min(quarter, whole - k))
        copies.append(
            pltpu.make_async_copy(
                coupling_ref.at[rows, pairs], buffer.at[slot, :, pairs], sems.at[slot, number]
            )
        )
    copies.append(
        pltpu.make_async_copy(
            edge_ref.at[rows, :], buffer.at[slot, :, pl.ds(whole, LANES)], sems.at[slot, COPIES]
        )
    )
    return copies


def multiply(coupling_ref, edge_ref, buffer, sems, turned, total_ref, columns, before=None):
    low, many = columns
    block = buffer.shape[1]
    steps = -(-many // block)

    def copies(step):
        start = jnp.minimum(step * block, many - block)
        return coupling_copies(coupling_ref, edge_ref, buffer, sems, low, start, lax.rem(step, SLOTS))

    for ahead in range(min(SLOTS - 1, steps)):
        for copy in copies(jnp.int32(ahead)):
            copy.start()
    if before is not None:
        before()

    def step(number, carry):
        @pl.when(number + SLOTS - 1 < steps)
        def _():
            for copy in copies(number + SLOTS - 1):
                copy.start()

        for copy in copies(number):
            copy.wait()
        total = jnp.dot(
            buffer[lax.rem(number, SLOTS)], turned[...], preferred_element_type=jnp.float32
        )
        rows = pl.ds(pl.multiple_of(jnp.minimum(number * block, many - block), 4), block)
        for part in range(total_ref.shape[0]):
            total_ref[part, rows, :] = total[:, part * LANES : (part + 1) * LANES]
        return carry

    lax.fori_loop(0, steps, step, 0)


def turn_pieces(edges, pieces, gathered, sems, turned, lanes):
    rows = pieces[0].shape[0]
    slots = gathered.shape[0] // rows
    copies = []
    for number, (edge, piece) in enumerate(zip(edges, pieces)):
        target = gathered.at[
            pl.ds(number % slots * rows, rows), pl.ds(edge, piece.shape[1])
        ]
        copies.append(pltpu.make_async_copy(piece, target, sems.at[number]))
    for copy in copies:
        copy.start()
    for copy in copies:
        copy.wait()
    for at in range(0, turned.shape[0], LANES):
        turned[at : at + LANES, lanes : lanes + slots * rows] = gathered[:, at : at + LANES].T


def near_kernel(at, whole, columns, count, *refs):
    pieces, refs = refs[:count], refs[count:]
    if columns is None:
        turned, gathered, sems = refs
        turn_pieces((0,) * count, pieces, gathered, sems, turned, 0)
        return
    coupling_ref, edge_ref, turned, held, gathered, sems, held_sems = refs
    low, many = columns
    rows = pl.ds(low, many)
    quarter = ceil_to(-(-whole // COPIES), LANES)
    copies = []
    for number, k in enumerate(range(0, whole, quarter)):
        size = min(quarter, whole - k)
        copies.append(
            pltpu.make_async_copy(
                coupling_ref.at[rows, pl.ds(at + k, size)],
                held.at[:, pl.ds(k, size)],
                held_sems.at[number],
            )
        )
    if whole < held.shape[1]:
        copies.append(
            pltpu.make_async_copy(
                edge_ref.at[rows, :], held.at[:, pl.ds(whole, LANES)], held_sems.at[COPIES]
            )
        )
    for copy in copies:
        copy.start()
    turn_pieces((0,) * count, pieces, gathered, sems, turned, 0)
    for copy in copies:
        copy.wait()


def lead_kernel(edges, columns, span, nears, rep_ref, *refs):
    near, pieces, refs = refs[:nears], refs[nears : nears + len(edges)], refs[nears + len(edges) :]
    coupling_ref, edge_ref, total, turned, send, gathered, sems, buffer, buffer_sems = refs

    def before():
        at, lanes = 0, near[0].shape[1]
        for part in near:
            turned[at : at + part.shape[0], :lanes] = part[...]
            at += part.shape[0]
        turn_pieces(edges, pieces, gathered, sems, turned, lanes)

    multiply(coupling_ref, edge_ref, buffer, buffer_sems, turned, total, columns, before)
    first_send(span, rep_ref, total, send)


def rest_kernel(span, rep_ref, turned, *refs):
    *held, total, send = refs
    many = held[0].shape[0]
    block = min(C_BLOCK, ceil_to(many // 2, 16))

    def step(number, carry):
        start = pl.multiple_of(jnp.minimum(number * block, many - block), 16)
        rows = pl.ds(start, block)
        at, products = 0, 0.0
        for part in held:
            size = part.shape[1]
            products += jnp.dot(
                part[rows, :], turned[at : at + size, :], preferred_element_type=jnp.float32
            )
            at += size
        for part in range(total.shape[0]):
            total[part, rows, :] = products[:, part * LANES : (part + 1) * LANES]
        return carry

    lax.fori_loop(0, -(-many // block), step, 0)
    first_send(span, rep_ref, total, send)


def column_rows(total_ref, width, part, j, offset, bp):
    rows = pl.ds(offset + part * width + j, bp, stride=NOCC)
    return jnp.concatenate([total_ref[h, rows, :] for h in range(total_ref.shape[0])], axis=1)


def first_send(span, rep_ref, total_ref, out_ref):
    offset, count, width = span
    low = rep_ref[0] % 2

    def step(j, carry):
        for high in range(2):
            rows = column_rows(total_ref, width, 2 * high + 1 - low, j, offset, out_ref.shape[2])
            out_ref[high, j] = to_code(encode(rows, count))
        return carry

    lax.fori_loop(0, width, step, 0)


def second_send_kernel(span, rep_ref, total_ref, got_ref, out_ref):
    offset, count, width = span
    low, high = rep_ref[0] % 2, 1 - rep_ref[0] // 2

    def step(j, carry):
        rows = column_rows(total_ref, width, 2 * high + low, j, offset, out_ref.shape[1])
        rows = rows + decode(from_code(got_ref[high, j]), count)
        out_ref[j] = to_code(encode(rows, count))
        return carry

    lax.fori_loop(0, width, step, 0)


def keep_kernel(span, rep_ref, total_ref, got_ref, out_ref):
    offset, count, width = span
    low, high = rep_ref[0] % 2, rep_ref[0] // 2

    def step(j, carry):
        rows = column_rows(total_ref, width, 2 * high + low, j, offset, out_ref.shape[1])
        out_ref[j] = rows + decode(from_code(got_ref[high, j]), count)
        return carry

    lax.fori_loop(0, width, step, 0)


def pack_rows(count, rows_dev, kept_ref, got_ref, stage):
    pack = LANES // rows_dev
    groups = stage.shape[1]
    size, _, slab = kept_ref.shape

    def step(jj, carry):
        coded = []
        for jq in range(pack):
            j = jnp.minimum(jq * groups + jj, size - 1)
            coded.append(encode(kept_ref[j] + decode(from_code(got_ref[j]), count), count))
        for g in range(slab // rows_dev):
            own = [block[:, g * rows_dev : (g + 1) * rows_dev] for block in coded]
            stage[g, jj] = to_code(jnp.concatenate(own, axis=1))
        return carry

    lax.fori_loop(0, groups, step, 0)


def third_send_kernel(count, rows_dev, kept_ref, got_ref, *outs):
    *early, stage = outs
    pack_rows(count, rows_dev, kept_ref, got_ref, stage)
    for number, target in enumerate(early):
        target[...] = stage[stage.shape[0] - len(early) + number]


def last_send_kernel(count, rows_dev, parts, early, kept_ref, got_ref, *refs):
    earlier, targets, stage = refs[: parts - 1], refs[parts - 1 : -1], refs[-1]
    pack_rows(count, rows_dev, kept_ref, got_ref, stage)
    for number, target in enumerate(targets):
        at = 0
        for source in (*earlier, stage) if number < len(targets) - early else (stage,):
            bp = source.shape[2]
            target[:, at : at + bp, :] = source[number]
            at += bp


def update_kernel(counts, bps, width, rows_dev, order, early, me_ref, occ_energy_ref, occ_irrep_ref, *refs):
    (
        integrals_ref,
        row_energy_ref,
        vir_energy_ref,
        row_irrep_ref,
        vir_irrep_ref,
        out_ref,
        blocks,
        stage,
    ) = refs[-8:]
    ahead, arrived = refs[:early], refs[early:-8]
    grid_size = len(arrived)
    place = walk_place(me_ref[0], grid_size)
    for number, (offset, got_ref) in enumerate(zip(order, arrived)):
        source = walk_index(lax.rem(place - offset + grid_size, grid_size), grid_size)
        ready = ahead[max(number - (grid_size - len(ahead)), 0) :][:1]
        if number < grid_size - len(ahead):
            ready = []
        at = 0
        for piece in (*ready, got_ref):
            blocks[source, :, at : at + piece.shape[1], :] = piece[...]
            at += piece.shape[1]
    pack = LANES // rows_dev
    for jj in range(blocks.shape[1]):
        at = 0
        for g in range(len(arrived)):
            row = 0
            for count, bp in zip(counts, bps):
                block = decode(from_code(blocks[g, jj, row : row + bp, :]), count)
                stage[at : at + count, :] = block[:count]
                at += count
                row += bp
        turned = stage[...].T
        for jq in range(pack):
            j = jq * blocks.shape[1] + jj
            if j >= width:
                continue
            cycle = turned[jq * rows_dev : (jq + 1) * rows_dev]
            denominator = row_energy_ref[...] + occ_energy_ref[j] - vir_energy_ref[...]
            labels = row_irrep_ref[...] ^ occ_irrep_ref[j] ^ vir_irrep_ref[...]
            out_ref[j] = jnp.where(
                labels == 0, (integrals_ref[j] + cycle) / denominator, jnp.float32(0.0)
            )


def local_call(kernel, out_shape, specs, args, scratch=(), aliases={}, cost=(10**7, 4 * 10**6), room=0):
    spaces = {"s": pltpu.SMEM, "v": pltpu.VMEM, "a": pl.ANY}
    return pl.pallas_call(
        kernel,
        out_shape=out_shape,
        in_specs=[pl.BlockSpec(memory_space=spaces[letter]) for letter in specs],
        out_specs=jax.tree.map(lambda _: pl.BlockSpec(memory_space=pltpu.VMEM), out_shape),
        scratch_shapes=list(scratch),
        input_output_aliases=aliases,
        compiler_params=pltpu.CompilerParams(vmem_limit_bytes=5 * MIB + room),
        cost_estimate=pl.CostEstimate(
            flops=cost[0], bytes_accessed=cost[1], transcendentals=0
        ),
        name=kernel.func.__name__,
    )(*args)


def body(
    amplitudes,
    coupling,
    integrals,
    row_energy,
    occ_energy,
    vir_energy,
    row_irrep,
    occ_irrep,
    vir_irrep,
):
    grid_size = lax.axis_size("grid")
    me = lax.axis_index("grid").astype(jnp.int32).reshape(1)
    rep = lax.axis_index("rep").astype(jnp.int32).reshape(1)
    rows_dev, depth = amplitudes.shape
    coupling = coupling.T
    columns = coupling.shape[0]
    count = columns // NOCC
    ragged = ceil_to(columns, 16) - columns
    if ragged:
        coupling = jnp.pad(coupling, ((0, ragged), (0, 0)))
        columns += ragged
    edge = depth % LANES
    edge = jnp.pad(coupling[:, depth - edge :], ((0, 0), (0, LANES - edge)))
    slab = rows_dev * grid_size
    width = NOCC // lax.axis_size("rep")

    walk = [*range(0, grid_size, 2), *range(1, grid_size, 2)[::-1]]
    onward = [(walk[i], walk[(i + 1) % grid_size]) for i in range(grid_size)]
    back = [(b, a) for a, b in onward]

    longer = grid_size // 2
    order = [0]
    for hop in range(1, longer):
        order += [-hop, hop]
    order.append(longer)
    near, far, far_edges = [], [], []
    for number, at in enumerate(range(0, depth, K_BLOCK)):
        own = amplitudes[:, at : at + K_BLOCK]
        size = own.shape[1]
        own = jnp.pad(own, ((0, 0), (0, ceil_to(size, LANES) - size)))
        ahead = behind = own
        pieces = [own]
        for hop in range(1, longer + 1):
            if hop < longer or number % 2 == 0:
                ahead = lax.ppermute(ahead, "grid", onward)
                pieces.append(ahead)
            if hop < longer or number % 2 == 1:
                behind = lax.ppermute(behind, "grid", back)
                pieces.append(behind)
        near.append((at, size // LANES * LANES, pieces[:longer]))
        far += pieces[longer:]
        far_edges += [at] * longer

    counts = [FIRST_PART, count - FIRST_PART] if count > FIRST_PART else [count]
    firsts = [0, FIRST_PART][: len(counts)]
    bps = [ceil_to(number + 1, 16) for number in counts]
    lows = [first * NOCC // 16 * 16 for first in firsts]
    highs = [
        min(columns, ceil_to((first + number) * NOCC, 16)) for first, number in zip(firsts, counts)
    ]
    parts = [(low, high - low) for low, high in zip(lows, highs)]
    spans = [
        (first * NOCC - low, number, width) for first, low, number in zip(firsts, lows, counts)
    ]
    total_shapes = [
        jax.ShapeDtypeStruct((slab // LANES, max(span[0] + bp * NOCC, part[1]), LANES), jnp.float32)
        for span, part, bp in zip(spans, parts, bps)
    ]
    send_shapes = [jax.ShapeDtypeStruct((2, width, bp, slab), jnp.int16) for bp in bps]
    deep = ceil_to(depth, LANES)
    low_pairs = [(i, i ^ 1) for i in range(lax.axis_size("rep"))]
    high_pairs = [(i, i ^ 2) for i in range(lax.axis_size("rep"))]

    half = slab // 2
    large = slab > 2 * LANES
    cols = parts[1] if len(parts) > 1 else None
    turned_near, held = [], []
    for at, whole, pieces in near:
        size = pieces[0].shape[1]
        out_shape = [jax.ShapeDtypeStruct((size, half), jnp.bfloat16)]
        args = list(pieces)
        scratch = [
            pltpu.VMEM((half, size), jnp.bfloat16),
            pltpu.SemaphoreType.DMA((len(pieces),)),
        ]
        if cols is not None:
            out_shape.append(jax.ShapeDtypeStruct((cols[1], size), jnp.bfloat16))
            args += [coupling, edge]
            scratch.append(pltpu.SemaphoreType.DMA((COPIES + 1,)))
        part, *rest = local_call(
            functools.partial(near_kernel, at, whole, cols, len(pieces)),
            tuple(out_shape),
            "a" * len(args),
            args,
            scratch,
            cost=(10**8, 4 * half * size + (2 * cols[1] * size if cols else 0)),
            room=2 * half * size * (2 if large else 1),
        )
        turned_near.append(part)
        held += rest
    totals, sends, got = [], [], []
    for part, (cols, span, bp) in enumerate(zip(parts, spans, bps)):
        cost = (2 * cols[1] * deep * slab, 2 * cols[1] * deep)
        if part == 0:
            block = min(C_BLOCK, ceil_to(cols[1] // 2, 16))
            room = 2 * SLOTS * block * deep + slab * deep
            if large:
                room += 3 * slab * deep + 4 * slab * total_shapes[0].shape[1]
            total, turned, send = local_call(
                functools.partial(lead_kernel, tuple(far_edges), cols, span, len(turned_near)),
                (
                    total_shapes[0],
                    jax.ShapeDtypeStruct((deep, slab), jnp.bfloat16),
                    send_shapes[0],
                ),
                "s" + "v" * len(turned_near) + "a" * (len(far) + 2),
                (rep, *turned_near, *far, coupling, edge),
                [
                    pltpu.VMEM((half, deep), jnp.bfloat16),
                    pltpu.SemaphoreType.DMA((len(far),)),
                    pltpu.VMEM((SLOTS, block, deep), jnp.bfloat16),
                    pltpu.SemaphoreType.DMA((SLOTS, COPIES + 1)),
                ],
                cost=cost,
                room=room,
            )
        else:
            turned, _ = lax.optimization_barrier((turned, sends[0]))
            total, send = local_call(
                functools.partial(rest_kernel, span),
                (total_shapes[part], send_shapes[part]),
                "sv" + "v" * len(held),
                (rep, turned, *held),
                cost=cost,
            )
        arrived = lax.ppermute(send, "rep", low_pairs)
        totals.append(total)
        got.append(arrived)
        sends.append(
            local_call(
                functools.partial(second_send_kernel, span),
                jax.ShapeDtypeStruct((width, bp, slab), jnp.int16),
                "svv",
                (rep, total, arrived),
            )
        )
    kept = [
        local_call(
            functools.partial(keep_kernel, span),
            jax.ShapeDtypeStruct((width, bp, slab), jnp.float32),
            "svv",
            (rep, total, arrived),
        )
        for span, bp, total, arrived in zip(spans, bps, totals, got)
    ]
    got = [lax.ppermute(send, "rep", high_pairs) for send in sends]

    groups = -(-width // (LANES // rows_dev))
    staged, left = [], []
    early = min(EARLY, grid_size - 1) if len(spans) > 1 else 0
    for part, span in enumerate(spans[:-1]):
        mine, _ = lax.optimization_barrier((kept[part], sends[-1]))
        *leaving, stage = local_call(
            functools.partial(third_send_kernel, span[1], rows_dev),
            (jax.ShapeDtypeStruct((groups, bps[part], LANES), jnp.int16),) * early
            + (jax.ShapeDtypeStruct((grid_size, groups, bps[part], LANES), jnp.int16),),
            "vv",
            (mine, got[part]),
        )
        staged.append(stage)
        left += leaving
    rows = [sum(bps)] * (grid_size - early) + [bps[-1]] * early
    targets = local_call(
        functools.partial(last_send_kernel, counts[-1], rows_dev, len(counts), early),
        tuple(jax.ShapeDtypeStruct((groups, many, LANES), jnp.int16) for many in rows),
        "vv" + "v" * len(staged),
        (kept[-1], got[-1], *staged),
        [pltpu.VMEM((grid_size, groups, bps[-1], LANES), jnp.int16)],
    )

    def go_back(block, number):
        pairs = [(walk[i], walk[(i + order[number]) % grid_size]) for i in range(grid_size)]
        return lax.ppermute(block, "grid", pairs)

    ahead = [go_back(block, grid_size - early + i) for i, block in enumerate(left)]
    arrived = list(targets)
    for number in range(1, grid_size)[::-1]:
        arrived[number] = go_back(targets[number], number)

    updated = local_call(
        functools.partial(update_kernel, counts, bps, width, rows_dev, order, early),
        jax.ShapeDtypeStruct((width, rows_dev, count * grid_size), jnp.float32),
        "sss" + "v" * (early + len(arrived) + 5),
        (
            me,
            occ_energy,
            occ_irrep,
            *ahead,
            *arrived,
            jnp.transpose(integrals, (1, 0, 2)),
            row_energy[:, None],
            vir_energy[None, :],
            row_irrep[:, None],
            vir_irrep[None, :],
        ),
        [
            pltpu.VMEM((grid_size, groups, sum(bps), LANES), jnp.int16),
            pltpu.VMEM((count * grid_size, LANES), jnp.float32),
        ],
    )
    return jnp.transpose(updated, (1, 0, 2))


def solution(mesh):
    return jax.shard_map(
        body,
        mesh=mesh,
        in_specs=(
            P("grid", "rep"),
            P("rep", "grid"),
            P("grid", "rep", None),
            P("grid"),
            P("rep"),
            P(),
            P("grid"),
            P("rep"),
            P(),
        ),
        out_specs=P("grid", "rep", None),
        check_vma=False,
    )
```

```python
import functools

import jax
import jax.numpy as jnp
from jax import lax
from jax.experimental import pallas as pl
from jax.experimental.pallas import tpu as pltpu
from jax.sharding import PartitionSpec as P

NOCC = 60
LANES = 128
K_BLOCK = 3840
C_BLOCK = 480
SLOTS = 3
EARLY = 0
COPIES = 4
FIRST_PART = 47
STEPS = 8.0
TOP = 32767.0
MIB = 1024 * 1024


def ceil_to(value, unit):
    return -(-value // unit) * unit


def encode(rows, count):
    index = lax.broadcasted_iota(jnp.int32, rows.shape, 0)
    rows = jnp.where(index < count, rows, 0.0)
    largest = jnp.max(jnp.abs(rows), axis=0, keepdims=True)
    level = jnp.ceil(jnp.log2(jnp.maximum(largest, 1e-30)) * STEPS) + 1.0
    coded = jnp.floor(rows * (jnp.exp2(level * (-1.0 / STEPS)) * TOP) + 0.5)
    return jnp.where(index == count, level, coded)


def decode(block, count):
    index = lax.broadcasted_iota(jnp.int32, block.shape, 0)
    scale = jnp.exp2(block[count : count + 1] * (1.0 / STEPS)) * (1.0 / TOP)
    return jnp.where(index < count, block * scale, 0.0)


def to_code(block):
    return block.astype(jnp.int32).astype(jnp.int16)


def from_code(block):
    return block.astype(jnp.int32).astype(jnp.float32)


def walk_index(place, size):
    return jnp.where(place < size // 2, 2 * place, 2 * (size - 1 - place) + 1)


def walk_place(index, size):
    return jnp.where(index % 2 == 0, index // 2, size - 1 - index // 2)


def coupling_copies(coupling_ref, edge_ref, buffer, sems, low, start, slot):
    block = buffer.shape[1]
    whole = buffer.shape[2] - LANES
    rows = pl.ds(pl.multiple_of(low + start, 16), block)
    quarter = ceil_to(-(-whole // COPIES), 256)
    copies = []
    for number, k in enumerate(range(0, whole, quarter)):
        pairs = pl.ds(k, min(quarter, whole - k))
        copies.append(
            pltpu.make_async_copy(
                coupling_ref.at[rows, pairs], buffer.at[slot, :, pairs], sems.at[slot, number]
            )
        )
    copies.append(
        pltpu.make_async_copy(
            edge_ref.at[rows, :], buffer.at[slot, :, pl.ds(whole, LANES)], sems.at[slot, COPIES]
        )
    )
    return copies


def multiply(coupling_ref, edge_ref, buffer, sems, turned, total_ref, columns, before=None):
    low, many = columns
    block = buffer.shape[1]
    steps = -(-many // block)

    def copies(step):
        start = jnp.minimum(step * block, many - block)
        return coupling_copies(coupling_ref, edge_ref, buffer, sems, low, start, lax.rem(step, SLOTS))

    for ahead in range(min(SLOTS - 1, steps)):
        for copy in copies(jnp.int32(ahead)):
            copy.start()
    if before is not None:
        before()

    def step(number, carry):
        @pl.when(number + SLOTS - 1 < steps)
        def _():
            for copy in copies(number + SLOTS - 1):
                copy.start()

        for copy in copies(number):
            copy.wait()
        total = jnp.dot(
            buffer[lax.rem(number, SLOTS)], turned[...], preferred_element_type=jnp.float32
        )
        rows = pl.ds(pl.multiple_of(jnp.minimum(number * block, many - block), 4), block)
        for part in range(total_ref.shape[0]):
            total_ref[part, rows, :] = total[:, part * LANES : (part + 1) * LANES]
        return carry

    lax.fori_loop(0, steps, step, 0)


def turn_pieces(edges, pieces, gathered, sems, turned, lanes):
    rows = pieces[0].shape[0]
    slots = gathered.shape[0] // rows
    copies = []
    for number, (edge, piece) in enumerate(zip(edges, pieces)):
        target = gathered.at[
            pl.ds(number % slots * rows, rows), pl.ds(edge, piece.shape[1])
        ]
        copies.append(pltpu.make_async_copy(piece, target, sems.at[number]))
    for copy in copies:
        copy.start()
    for copy in copies:
        copy.wait()
    for at in range(0, turned.shape[0], LANES):
        turned[at : at + LANES, lanes : lanes + slots * rows] = gathered[:, at : at + LANES].T


def near_kernel(at, whole, columns, count, *refs):
    pieces, refs = refs[:count], refs[count:]
    if columns is None:
        turned, gathered, sems = refs
        turn_pieces((0,) * count, pieces, gathered, sems, turned, 0)
        return
    coupling_ref, edge_ref, turned, held, gathered, sems, held_sems = refs
    low, many = columns
    rows = pl.ds(low, many)
    quarter = ceil_to(-(-whole // COPIES), LANES)
    copies = []
    for number, k in enumerate(range(0, whole, quarter)):
        size = min(quarter, whole - k)
        copies.append(
            pltpu.make_async_copy(
                coupling_ref.at[rows, pl.ds(at + k, size)],
                held.at[:, pl.ds(k, size)],
                held_sems.at[number],
            )
        )
    if whole < held.shape[1]:
        copies.append(
            pltpu.make_async_copy(
                edge_ref.at[rows, :], held.at[:, pl.ds(whole, LANES)], held_sems.at[COPIES]
            )
        )
    for copy in copies:
        copy.start()
    turn_pieces((0,) * count, pieces, gathered, sems, turned, 0)
    for copy in copies:
        copy.wait()


def lead_kernel(edges, columns, span, nears, rep_ref, *refs):
    near, pieces, refs = refs[:nears], refs[nears : nears + len(edges)], refs[nears + len(edges) :]
    coupling_ref, edge_ref, total, turned, send, gathered, sems, buffer, buffer_sems = refs

    def before():
        at, lanes = 0, near[0].shape[1]
        for part in near:
            turned[at : at + part.shape[0], :lanes] = part[...]
            at += part.shape[0]
        turn_pieces(edges, pieces, gathered, sems, turned, lanes)

    multiply(coupling_ref, edge_ref, buffer, buffer_sems, turned, total, columns, before)
    first_send(span, rep_ref, total, send)


def rest_kernel(span, rep_ref, turned, *refs):
    *held, total, send = refs
    many = held[0].shape[0]
    block = min(C_BLOCK, ceil_to(many // 2, 16))

    def step(number, carry):
        start = pl.multiple_of(jnp.minimum(number * block, many - block), 16)
        rows = pl.ds(start, block)
        at, products = 0, 0.0
        for part in held:
            size = part.shape[1]
            products += jnp.dot(
                part[rows, :], turned[at : at + size, :], preferred_element_type=jnp.float32
            )
            at += size
        for part in range(total.shape[0]):
            total[part, rows, :] = products[:, part * LANES : (part + 1) * LANES]
        return carry

    lax.fori_loop(0, -(-many // block), step, 0)
    first_send(span, rep_ref, total, send)


def column_rows(total_ref, width, part, j, offset, bp):
    rows = pl.ds(offset + part * width + j, bp, stride=NOCC)
    return jnp.concatenate([total_ref[h, rows, :] for h in range(total_ref.shape[0])], axis=1)


def first_send(span, rep_ref, total_ref, out_ref):
    offset, count, width = span
    low = rep_ref[0] % 2

    def step(j, carry):
        for high in range(2):
            rows = column_rows(total_ref, width, 2 * high + 1 - low, j, offset, out_ref.shape[2])
            out_ref[high, j] = to_code(encode(rows, count))
        return carry

    lax.fori_loop(0, width, step, 0)


def second_send_kernel(span, rep_ref, total_ref, got_ref, out_ref):
    offset, count, width = span
    low, high = rep_ref[0] % 2, 1 - rep_ref[0] // 2

    def step(j, carry):
        rows = column_rows(total_ref, width, 2 * high + low, j, offset, out_ref.shape[1])
        rows = rows + decode(from_code(got_ref[high, j]), count)
        out_ref[j] = to_code(encode(rows, count))
        return carry

    lax.fori_loop(0, width, step, 0)


def keep_kernel(span, rep_ref, total_ref, got_ref, out_ref):
    offset, count, width = span
    low, high = rep_ref[0] % 2, rep_ref[0] // 2

    def step(j, carry):
        rows = column_rows(total_ref, width, 2 * high + low, j, offset, out_ref.shape[1])
        out_ref[j] = rows + decode(from_code(got_ref[high, j]), count)
        return carry

    lax.fori_loop(0, width, step, 0)


def pack_rows(count, rows_dev, kept_ref, got_ref, stage):
    pack = LANES // rows_dev
    groups = stage.shape[1]
    size, _, slab = kept_ref.shape

    def step(jj, carry):
        coded = []
        for jq in range(pack):
            j = jnp.minimum(jq * groups + jj, size - 1)
            coded.append(encode(kept_ref[j] + decode(from_code(got_ref[j]), count), count))
        for g in range(slab // rows_dev):
            own = [block[:, g * rows_dev : (g + 1) * rows_dev] for block in coded]
            stage[g, jj] = to_code(jnp.concatenate(own, axis=1))
        return carry

    lax.fori_loop(0, groups, step, 0)


def third_send_kernel(count, rows_dev, kept_ref, got_ref, *outs):
    *early, stage = outs
    pack_rows(count, rows_dev, kept_ref, got_ref, stage)
    for number, target in enumerate(early):
        target[...] = stage[stage.shape[0] - len(early) + number]


def last_send_kernel(count, rows_dev, parts, early, kept_ref, got_ref, *refs):
    earlier, targets, stage = refs[: parts - 1], refs[parts - 1 : -1], refs[-1]
    pack_rows(count, rows_dev, kept_ref, got_ref, stage)
    for number, target in enumerate(targets):
        at = 0
        for source in (*earlier, stage) if number < len(targets) - early else (stage,):
            bp = source.shape[2]
            target[:, at : at + bp, :] = source[number]
            at += bp


def update_kernel(counts, bps, width, rows_dev, order, early, me_ref, occ_energy_ref, occ_irrep_ref, *refs):
    (
        integrals_ref,
        row_energy_ref,
        vir_energy_ref,
        row_irrep_ref,
        vir_irrep_ref,
        out_ref,
        blocks,
        stage,
    ) = refs[-8:]
    ahead, arrived = refs[:early], refs[early:-8]
    grid_size = len(arrived)
    place = walk_place(me_ref[0], grid_size)
    for number, (offset, got_ref) in enumerate(zip(order, arrived)):
        source = walk_index(lax.rem(place - offset + grid_size, grid_size), grid_size)
        ready = ahead[max(number - (grid_size - len(ahead)), 0) :][:1]
        if number < grid_size - len(ahead):
            ready = []
        at = 0
        for piece in (*ready, got_ref):
            blocks[source, :, at : at + piece.shape[1], :] = piece[...]
            at += piece.shape[1]
    pack = LANES // rows_dev
    for jj in range(blocks.shape[1]):
        at = 0
        for g in range(len(arrived)):
            row = 0
            for count, bp in zip(counts, bps):
                block = decode(from_code(blocks[g, jj, row : row + bp, :]), count)
                stage[at : at + count, :] = block[:count]
                at += count
                row += bp
        turned = stage[...].T
        for jq in range(pack):
            j = jq * blocks.shape[1] + jj
            if j >= width:
                continue
            cycle = turned[jq * rows_dev : (jq + 1) * rows_dev]
            denominator = row_energy_ref[...] + occ_energy_ref[j] - vir_energy_ref[...]
            labels = row_irrep_ref[...] ^ occ_irrep_ref[j] ^ vir_irrep_ref[...]
            out_ref[j] = jnp.where(
                labels == 0, (integrals_ref[j] + cycle) / denominator, jnp.float32(0.0)
            )


def local_call(kernel, out_shape, specs, args, scratch=(), aliases={}, cost=(10**7, 4 * 10**6), room=0):
    spaces = {"s": pltpu.SMEM, "v": pltpu.VMEM, "a": pl.ANY}
    return pl.pallas_call(
        kernel,
        out_shape=out_shape,
        in_specs=[pl.BlockSpec(memory_space=spaces[letter]) for letter in specs],
        out_specs=jax.tree.map(lambda _: pl.BlockSpec(memory_space=pltpu.VMEM), out_shape),
        scratch_shapes=list(scratch),
        input_output_aliases=aliases,
        compiler_params=pltpu.CompilerParams(vmem_limit_bytes=8 * MIB + room),
        cost_estimate=pl.CostEstimate(
            flops=cost[0], bytes_accessed=cost[1], transcendentals=0
        ),
        name=kernel.func.__name__,
    )(*args)


def body(
    amplitudes,
    coupling,
    integrals,
    row_energy,
    occ_energy,
    vir_energy,
    row_irrep,
    occ_irrep,
    vir_irrep,
):
    grid_size = lax.axis_size("grid")
    me = lax.axis_index("grid").astype(jnp.int32).reshape(1)
    rep = lax.axis_index("rep").astype(jnp.int32).reshape(1)
    rows_dev, depth = amplitudes.shape
    coupling = coupling.T
    columns = coupling.shape[0]
    count = columns // NOCC
    ragged = ceil_to(columns, 16) - columns
    if ragged:
        coupling = jnp.pad(coupling, ((0, ragged), (0, 0)))
        columns += ragged
    edge = depth % LANES
    edge = jnp.pad(coupling[:, depth - edge :], ((0, 0), (0, LANES - edge)))
    slab = rows_dev * grid_size
    width = NOCC // lax.axis_size("rep")

    walk = [*range(0, grid_size, 2), *range(1, grid_size, 2)[::-1]]
    onward = [(walk[i], walk[(i + 1) % grid_size]) for i in range(grid_size)]
    back = [(b, a) for a, b in onward]

    counts = [FIRST_PART, count - FIRST_PART] if count > FIRST_PART else [count]
    firsts = [0, FIRST_PART][: len(counts)]
    bps = [ceil_to(number + 1, 16) for number in counts]
    lows = [first * NOCC // 16 * 16 for first in firsts]
    highs = [
        min(columns, ceil_to((first + number) * NOCC, 16)) for first, number in zip(firsts, counts)
    ]
    parts = [(low, high - low) for low, high in zip(lows, highs)]
    spans = [
        (first * NOCC - low, number, width) for first, low, number in zip(firsts, lows, counts)
    ]
    total_shapes = [
        jax.ShapeDtypeStruct((slab // LANES, max(span[0] + bp * NOCC, part[1]), LANES), jnp.float32)
        for span, part, bp in zip(spans, parts, bps)
    ]
    send_shapes = [jax.ShapeDtypeStruct((2, width, bp, slab), jnp.int16) for bp in bps]
    deep = ceil_to(depth, LANES)
    low_pairs = [(i, i ^ 1) for i in range(lax.axis_size("rep"))]
    high_pairs = [(i, i ^ 2) for i in range(lax.axis_size("rep"))]

    half = slab // 2
    large = slab > 2 * LANES
    held_columns = parts[1] if len(parts) > 1 else None

    def turn_near(at, whole, pieces):
        size = pieces[0].shape[1]
        out_shape = [jax.ShapeDtypeStruct((size, half), jnp.bfloat16)]
        args = list(pieces)
        scratch = [
            pltpu.VMEM((half, size), jnp.bfloat16),
            pltpu.SemaphoreType.DMA((len(pieces),)),
        ]
        cost = 4 * half * size
        if held_columns is not None:
            out_shape.append(jax.ShapeDtypeStruct((held_columns[1], size), jnp.bfloat16))
            args += [coupling, edge]
            scratch.append(pltpu.SemaphoreType.DMA((COPIES + 1,)))
            cost += 2 * held_columns[1] * size
        return local_call(
            functools.partial(near_kernel, at, whole, held_columns, len(pieces)),
            tuple(out_shape),
            "a" * len(args),
            args,
            scratch,
            cost=(10**8, cost),
            room=2 * half * size * (2 if large else 1),
        )

    longer = grid_size // 2
    order = [0]
    for hop in range(1, longer):
        order += [-hop, hop]
    order.append(longer)
    turned_near, held, far, far_edges = [], [], [], []
    for number, at in enumerate(range(0, depth, K_BLOCK)):
        own = amplitudes[:, at : at + K_BLOCK]
        size = own.shape[1]
        own = jnp.pad(own, ((0, 0), (0, ceil_to(size, LANES) - size)))
        ahead = behind = own
        pieces = [own]
        for hop in range(1, longer + 1):
            if hop == longer:
                part, *rest = turn_near(at, size // LANES * LANES, pieces[:longer])
                ahead, behind, part = lax.optimization_barrier((ahead, behind, part))
                turned_near.append(part)
                held += rest
            if hop < longer or number % 2 == 0:
                ahead = lax.ppermute(ahead, "grid", onward)
                pieces.append(ahead)
            if hop < longer or number % 2 == 1:
                behind = lax.ppermute(behind, "grid", back)
                pieces.append(behind)
        far += pieces[longer:]
        far_edges += [at] * longer

    totals, sends, got = [], [], []
    for part, (cols, span, bp) in enumerate(zip(parts, spans, bps)):
        cost = (2 * cols[1] * deep * slab, 2 * cols[1] * deep)
        if part == 0:
            block = min(C_BLOCK, ceil_to(cols[1] // 2, 16))
            room = 2 * SLOTS * block * deep + slab * deep
            if large:
                room += 3 * slab * deep + 4 * slab * total_shapes[0].shape[1]
            total, turned, send = local_call(
                functools.partial(lead_kernel, tuple(far_edges), cols, span, len(turned_near)),
                (
                    total_shapes[0],
                    jax.ShapeDtypeStruct((deep, slab), jnp.bfloat16),
                    send_shapes[0],
                ),
                "s" + "v" * len(turned_near) + "a" * (len(far) + 2),
                (rep, *turned_near, *far, coupling, edge),
                [
                    pltpu.VMEM((half, deep), jnp.bfloat16),
                    pltpu.SemaphoreType.DMA((len(far),)),
                    pltpu.VMEM((SLOTS, block, deep), jnp.bfloat16),
                    pltpu.SemaphoreType.DMA((SLOTS, COPIES + 1)),
                ],
                cost=cost,
                room=room,
            )
        else:
            turned, _ = lax.optimization_barrier((turned, sends[0]))
            total, send = local_call(
                functools.partial(rest_kernel, span),
                (total_shapes[part], send_shapes[part]),
                "sv" + "v" * len(held),
                (rep, turned, *held),
                cost=cost,
            )
        arrived = lax.ppermute(send, "rep", low_pairs)
        totals.append(total)
        got.append(arrived)
        sends.append(
            local_call(
                functools.partial(second_send_kernel, span),
                jax.ShapeDtypeStruct((width, bp, slab), jnp.int16),
                "svv",
                (rep, total, arrived),
            )
        )
    kept = [
        local_call(
            functools.partial(keep_kernel, span),
            jax.ShapeDtypeStruct((width, bp, slab), jnp.float32),
            "svv",
            (rep, total, arrived),
        )
        for span, bp, total, arrived in zip(spans, bps, totals, got)
    ]
    got = [lax.ppermute(send, "rep", high_pairs) for send in sends]

    groups = -(-width // (LANES // rows_dev))
    staged, left = [], []
    early = min(EARLY, grid_size - 1) if len(spans) > 1 else 0
    for part, span in enumerate(spans[:-1]):
        mine, _ = lax.optimization_barrier((kept[part], sends[-1]))
        *leaving, stage = local_call(
            functools.partial(third_send_kernel, span[1], rows_dev),
            (jax.ShapeDtypeStruct((groups, bps[part], LANES), jnp.int16),) * early
            + (jax.ShapeDtypeStruct((grid_size, groups, bps[part], LANES), jnp.int16),),
            "vv",
            (mine, got[part]),
        )
        staged.append(stage)
        left += leaving
    rows = [sum(bps)] * (grid_size - early) + [bps[-1]] * early
    targets = local_call(
        functools.partial(last_send_kernel, counts[-1], rows_dev, len(counts), early),
        tuple(jax.ShapeDtypeStruct((groups, many, LANES), jnp.int16) for many in rows),
        "vv" + "v" * len(staged),
        (kept[-1], got[-1], *staged),
        [pltpu.VMEM((grid_size, groups, bps[-1], LANES), jnp.int16)],
    )

    def go_back(block, number):
        pairs = [(walk[i], walk[(i + order[number]) % grid_size]) for i in range(grid_size)]
        return lax.ppermute(block, "grid", pairs)

    ahead = [go_back(block, grid_size - early + i) for i, block in enumerate(left)]
    arrived = list(targets)
    for number in range(1, grid_size)[::-1]:
        arrived[number] = go_back(targets[number], number)

    updated = local_call(
        functools.partial(update_kernel, counts, bps, width, rows_dev, order, early),
        jax.ShapeDtypeStruct((width, rows_dev, count * grid_size), jnp.float32),
        "sss" + "v" * (early + len(arrived) + 5),
        (
            me,
            occ_energy,
            occ_irrep,
            *ahead,
            *arrived,
            jnp.transpose(integrals, (1, 0, 2)),
            row_energy[:, None],
            vir_energy[None, :],
            row_irrep[:, None],
            vir_irrep[None, :],
        ),
        [
            pltpu.VMEM((grid_size, groups, sum(bps), LANES), jnp.int16),
            pltpu.VMEM((count * grid_size, LANES), jnp.float32),
        ],
    )
    return jnp.transpose(updated, (1, 0, 2))


def solution(mesh):
    return jax.shard_map(
        body,
        mesh=mesh,
        in_specs=(
            P("grid", "rep"),
            P("rep", "grid"),
            P("grid", "rep", None),
            P("grid"),
            P("rep"),
            P(),
            P("grid"),
            P("rep"),
            P(),
        ),
        out_specs=P("grid", "rep", None),
        check_vma=False,
    )
```

```python
import functools

import jax
import jax.numpy as jnp
from jax import lax
from jax.experimental import pallas as pl
from jax.experimental.pallas import tpu as pltpu
from jax.sharding import PartitionSpec as P

NOCC = 60
LANES = 128
K_BLOCK = 3840
C_BLOCK = 480
SLOTS = 3
COPIES = 4
FIRST_PART = 45
STEPS = 8.0
TOP = 32767.0
MIB = 1024 * 1024


def ceil_to(value, unit):
    return -(-value // unit) * unit


def encode(rows, count):
    index = lax.broadcasted_iota(jnp.int32, rows.shape, 0)
    rows = jnp.where(index < count, rows, 0.0)
    largest = jnp.max(jnp.abs(rows), axis=0, keepdims=True)
    level = jnp.ceil(jnp.log2(jnp.maximum(largest, 1e-30)) * STEPS) + 1.0
    coded = jnp.floor(rows * (jnp.exp2(level * (-1.0 / STEPS)) * TOP) + 0.5)
    return jnp.where(index == count, level, coded)


def decode(block, count):
    index = lax.broadcasted_iota(jnp.int32, block.shape, 0)
    scale = jnp.exp2(block[count : count + 1] * (1.0 / STEPS)) * (1.0 / TOP)
    return jnp.where(index < count, block * scale, 0.0)


def to_code(block):
    return block.astype(jnp.int32).astype(jnp.int16)


def from_code(block):
    return block.astype(jnp.int32).astype(jnp.float32)


def walk_index(place, size):
    return jnp.where(place < size // 2, 2 * place, 2 * (size - 1 - place) + 1)


def walk_place(index, size):
    return jnp.where(index % 2 == 0, index // 2, size - 1 - index // 2)


def coupling_copies(coupling_ref, edge_ref, buffer, sems, low, start, slot):
    block = buffer.shape[1]
    whole = buffer.shape[2] - LANES
    rows = pl.ds(pl.multiple_of(low + start, 16), block)
    quarter = ceil_to(-(-whole // COPIES), 256)
    copies = []
    for number, k in enumerate(range(0, whole, quarter)):
        pairs = pl.ds(k, min(quarter, whole - k))
        copies.append(
            pltpu.make_async_copy(
                coupling_ref.at[rows, pairs], buffer.at[slot, :, pairs], sems.at[slot, number]
            )
        )
    copies.append(
        pltpu.make_async_copy(
            edge_ref.at[rows, :], buffer.at[slot, :, pl.ds(whole, LANES)], sems.at[slot, COPIES]
        )
    )
    return copies


def multiply(coupling_ref, edge_ref, buffer, sems, turned, total_ref, columns, before=None):
    low, many = columns
    block = buffer.shape[1]
    steps = -(-many // block)

    def copies(step):
        start = jnp.minimum(step * block, many - block)
        return coupling_copies(coupling_ref, edge_ref, buffer, sems, low, start, lax.rem(step, SLOTS))

    for ahead in range(min(SLOTS - 1, steps)):
        for copy in copies(jnp.int32(ahead)):
            copy.start()
    if before is not None:
        before()

    def step(number, carry):
        @pl.when(number + SLOTS - 1 < steps)
        def _():
            for copy in copies(number + SLOTS - 1):
                copy.start()

        for copy in copies(number):
            copy.wait()
        total = jnp.dot(
            buffer[lax.rem(number, SLOTS)], turned[...], preferred_element_type=jnp.float32
        )
        rows = pl.ds(pl.multiple_of(jnp.minimum(number * block, many - block), 4), block)
        for part in range(total_ref.shape[0]):
            total_ref[part, rows, :] = total[:, part * LANES : (part + 1) * LANES]
        return carry

    lax.fori_loop(0, steps, step, 0)


def turn_pieces(edges, pieces, gathered, sems, turned, lanes):
    rows = pieces[0].shape[0]
    slots = gathered.shape[0] // rows
    copies = []
    for number, (edge, piece) in enumerate(zip(edges, pieces)):
        target = gathered.at[
            pl.ds(number % slots * rows, rows), pl.ds(edge, piece.shape[1])
        ]
        copies.append(pltpu.make_async_copy(piece, target, sems.at[number]))
    for copy in copies:
        copy.start()
    for copy in copies:
        copy.wait()
    for at in range(0, turned.shape[0], LANES):
        turned[at : at + LANES, lanes : lanes + slots * rows] = gathered[:, at : at + LANES].T


def near_kernel(edges, *refs):
    *pieces, turned, gathered, sems = refs
    turn_pieces(edges, pieces, gathered, sems, turned, 0)


def lead_kernel(edges, columns, span, rep_ref, near, *refs):
    pieces, refs = refs[: len(edges)], refs[len(edges) :]
    coupling_ref, edge_ref, total, turned, send, gathered, sems, buffer, buffer_sems = refs

    def before():
        lanes = near.shape[1]
        turned[:, :lanes] = near[...]
        turn_pieces(edges, pieces, gathered, sems, turned, lanes)

    multiply(coupling_ref, edge_ref, buffer, buffer_sems, turned, total, columns, before)
    first_send(span, rep_ref, total, send)


def rest_kernel(columns, span, rep_ref, turned, coupling_ref, edge_ref, total, send, buffer, sems):
    multiply(coupling_ref, edge_ref, buffer, sems, turned, total, columns)
    first_send(span, rep_ref, total, send)


def column_rows(total_ref, width, part, j, offset, bp):
    rows = pl.ds(offset + part * width + j, bp, stride=NOCC)
    return jnp.concatenate([total_ref[h, rows, :] for h in range(total_ref.shape[0])], axis=1)


def first_send(span, rep_ref, total_ref, out_ref):
    offset, count, width = span
    low = rep_ref[0] % 2

    def step(j, carry):
        for high in range(2):
            rows = column_rows(total_ref, width, 2 * high + 1 - low, j, offset, out_ref.shape[2])
            out_ref[high, j] = to_code(encode(rows, count))
        return carry

    lax.fori_loop(0, width, step, 0)


def second_send_kernel(span, rep_ref, total_ref, got_ref, out_ref):
    offset, count, width = span
    low, high = rep_ref[0] % 2, 1 - rep_ref[0] // 2

    def step(j, carry):
        rows = column_rows(total_ref, width, 2 * high + low, j, offset, out_ref.shape[1])
        rows = rows + decode(from_code(got_ref[high, j]), count)
        out_ref[j] = to_code(encode(rows, count))
        return carry

    lax.fori_loop(0, width, step, 0)


def keep_kernel(span, rep_ref, total_ref, got_ref, out_ref):
    offset, count, width = span
    low, high = rep_ref[0] % 2, rep_ref[0] // 2

    def step(j, carry):
        rows = column_rows(total_ref, width, 2 * high + low, j, offset, out_ref.shape[1])
        out_ref[j] = rows + decode(from_code(got_ref[high, j]), count)
        return carry

    lax.fori_loop(0, width, step, 0)


def third_send_kernel(count, rows_dev, order, me_ref, kept_ref, got_ref, out_ref):
    pack = LANES // rows_dev
    groups = out_ref.shape[1]
    size = kept_ref.shape[0]
    grid_size = len(order)
    place = walk_place(me_ref[0], grid_size)

    def step(jj, carry):
        coded = []
        for jq in range(pack):
            j = jnp.minimum(jq * groups + jj, size - 1)
            coded.append(encode(kept_ref[j] + decode(from_code(got_ref[j]), count), count))
        for number, offset in enumerate(order):
            own = [block[:, number * rows_dev : (number + 1) * rows_dev] for block in coded]
            target = walk_index(lax.rem(place + offset + grid_size, grid_size), grid_size)
            out_ref[target, jj] = to_code(jnp.concatenate(own, axis=1))
        return carry

    lax.fori_loop(0, groups, step, 0)


def update_kernel(counts, width, rows_dev, occ_energy_ref, occ_irrep_ref, *refs):
    (
        integrals_ref,
        row_energy_ref,
        vir_energy_ref,
        row_irrep_ref,
        vir_irrep_ref,
        out_ref,
        stage,
    ) = refs[-7:]
    arrived = refs[:-7]
    pack = LANES // rows_dev
    grid_size, groups = arrived[0].shape[:2]
    for jj in range(groups):
        at = 0
        for g in range(grid_size):
            for count, got_ref in zip(counts, arrived):
                block = decode(from_code(got_ref[g, jj]), count)
                stage[at : at + count, :] = block[:count]
                at += count
        turned = stage[...].T
        for jq in range(pack):
            j = jq * groups + jj
            if j >= width:
                continue
            cycle = turned[jq * rows_dev : (jq + 1) * rows_dev]
            denominator = row_energy_ref[...] + occ_energy_ref[j] - vir_energy_ref[...]
            labels = row_irrep_ref[...] ^ occ_irrep_ref[j] ^ vir_irrep_ref[...]
            out_ref[j] = jnp.where(
                labels == 0, (integrals_ref[j] + cycle) / denominator, jnp.float32(0.0)
            )


def local_call(kernel, out_shape, specs, args, scratch=(), aliases={}, cost=(10**7, 4 * 10**6), room=0):
    spaces = {"s": pltpu.SMEM, "v": pltpu.VMEM, "a": pl.ANY}
    return pl.pallas_call(
        kernel,
        out_shape=out_shape,
        in_specs=[pl.BlockSpec(memory_space=spaces[letter]) for letter in specs],
        out_specs=jax.tree.map(lambda _: pl.BlockSpec(memory_space=pltpu.VMEM), out_shape),
        scratch_shapes=list(scratch),
        input_output_aliases=aliases,
        compiler_params=pltpu.CompilerParams(vmem_limit_bytes=8 * MIB + room),
        cost_estimate=pl.CostEstimate(
            flops=cost[0], bytes_accessed=cost[1], transcendentals=0
        ),
        name=kernel.func.__name__,
    )(*args)


def body(
    amplitudes,
    coupling,
    integrals,
    row_energy,
    occ_energy,
    vir_energy,
    row_irrep,
    occ_irrep,
    vir_irrep,
):
    grid_size = lax.axis_size("grid")
    me = lax.axis_index("grid").astype(jnp.int32).reshape(1)
    rep = lax.axis_index("rep").astype(jnp.int32).reshape(1)
    rows_dev, depth = amplitudes.shape
    coupling = coupling.T
    columns = coupling.shape[0]
    count = columns // NOCC
    ragged = ceil_to(columns, 16) - columns
    if ragged:
        coupling = jnp.pad(coupling, ((0, ragged), (0, 0)))
        columns += ragged
    edge = depth % LANES
    edge = jnp.pad(coupling[:, depth - edge :], ((0, 0), (0, LANES - edge)))
    slab = rows_dev * grid_size
    width = NOCC // lax.axis_size("rep")

    walk = [*range(0, grid_size, 2), *range(1, grid_size, 2)[::-1]]
    onward = [(walk[i], walk[(i + 1) % grid_size]) for i in range(grid_size)]
    back = [(b, a) for a, b in onward]

    longer = grid_size // 2
    order = [0]
    for hop in range(1, longer):
        order += [-hop, hop]
    order.append(longer)
    near, far, near_edges, far_edges = [], [], [], []
    for number, at in enumerate(range(0, depth, K_BLOCK)):
        own = amplitudes[:, at : at + K_BLOCK]
        size = own.shape[1]
        own = jnp.pad(own, ((0, 0), (0, ceil_to(size, LANES) - size)))
        ahead = behind = own
        pieces = [own]
        for hop in range(1, longer + 1):
            if hop < longer or number % 2 == 0:
                ahead = lax.ppermute(ahead, "grid", onward)
                pieces.append(ahead)
            if hop < longer or number % 2 == 1:
                behind = lax.ppermute(behind, "grid", back)
                pieces.append(behind)
        near += pieces[:longer]
        far += pieces[longer:]
        near_edges += [at] * longer
        far_edges += [at] * longer

    counts = [FIRST_PART, count - FIRST_PART] if count > FIRST_PART else [count]
    firsts = [0, FIRST_PART][: len(counts)]
    bps = [ceil_to(number + 1, 16) for number in counts]
    lows = [first * NOCC // 16 * 16 for first in firsts]
    highs = [
        min(columns, ceil_to((first + number) * NOCC, 16)) for first, number in zip(firsts, counts)
    ]
    parts = [(low, high - low) for low, high in zip(lows, highs)]
    spans = [
        (first * NOCC - low, number, width) for first, low, number in zip(firsts, lows, counts)
    ]
    total_shapes = [
        jax.ShapeDtypeStruct((slab // LANES, max(span[0] + bp * NOCC, part[1]), LANES), jnp.float32)
        for span, part, bp in zip(spans, parts, bps)
    ]
    send_shapes = [jax.ShapeDtypeStruct((2, width, bp, slab), jnp.int16) for bp in bps]
    deep = ceil_to(depth, LANES)
    low_pairs = [(i, i ^ 1) for i in range(lax.axis_size("rep"))]
    high_pairs = [(i, i ^ 2) for i in range(lax.axis_size("rep"))]

    half = slab // 2
    turn_scratch = [
        pltpu.VMEM((half, deep), jnp.bfloat16),
        pltpu.SemaphoreType.DMA((len(near),)),
    ]
    near = local_call(
        functools.partial(near_kernel, tuple(near_edges)),
        jax.ShapeDtypeStruct((deep, half), jnp.bfloat16),
        "a" * len(near),
        near,
        turn_scratch,
        cost=(10**8, 4 * half * deep),
        room=2 * half * deep + (2 * half * deep if slab > 2 * LANES else 0),
    )
    groups = -(-width // (LANES // rows_dev))
    sends, arrived = [], []
    for part, (cols, span, bp) in enumerate(zip(parts, spans, bps)):
        block = min(C_BLOCK, ceil_to(cols[1] // 2, 16))
        scratch = [
            pltpu.VMEM((SLOTS, block, deep), jnp.bfloat16),
            pltpu.SemaphoreType.DMA((SLOTS, COPIES + 1)),
        ]
        cost = (2 * cols[1] * deep * slab, 2 * cols[1] * deep)
        room = 2 * SLOTS * block * deep + (slab * deep if part == 0 else 0)
        if slab > 2 * LANES:
            room += 3 * slab * deep + 4 * slab * total_shapes[part].shape[1]
        if part == 0:
            total, turned, send = local_call(
                functools.partial(lead_kernel, tuple(far_edges), cols, span),
                (
                    total_shapes[0],
                    jax.ShapeDtypeStruct((deep, slab), jnp.bfloat16),
                    send_shapes[0],
                ),
                "sv" + "a" * (len(far) + 2),
                (rep, near, *far, coupling, edge),
                [*turn_scratch, *scratch],
                cost=cost,
                room=room,
            )
        else:
            turned, _ = lax.optimization_barrier((turned, sends[0]))
            total, send = local_call(
                functools.partial(rest_kernel, cols, span),
                (total_shapes[part], send_shapes[part]),
                "svaa",
                (rep, turned, coupling, edge),
                scratch,
                cost=cost,
                room=room,
            )
        got = lax.ppermute(send, "rep", low_pairs)
        if arrived:
            got, _ = lax.optimization_barrier((got, back_send))
        send = local_call(
            functools.partial(second_send_kernel, span),
            jax.ShapeDtypeStruct((width, bp, slab), jnp.int16),
            "svv",
            (rep, total, got),
        )
        sends.append(send)
        kept = local_call(
            functools.partial(keep_kernel, span),
            jax.ShapeDtypeStruct((width, bp, slab), jnp.float32),
            "svv",
            (rep, total, got),
        )
        got = lax.ppermute(send, "rep", high_pairs)
        back_send = local_call(
            functools.partial(third_send_kernel, span[1], rows_dev, order),
            jax.ShapeDtypeStruct((grid_size, groups, bp, LANES), jnp.int16),
            "svv",
            (me, kept, got),
        )
        arrived.append(
            lax.all_to_all(back_send, "grid", split_axis=0, concat_axis=0, tiled=True)
        )

    updated = local_call(
        functools.partial(update_kernel, counts, width, rows_dev),
        jax.ShapeDtypeStruct((width, rows_dev, count * grid_size), jnp.float32),
        "ss" + "v" * (len(arrived) + 5),
        (
            occ_energy,
            occ_irrep,
            *arrived,
            jnp.transpose(integrals, (1, 0, 2)),
            row_energy[:, None],
            vir_energy[None, :],
            row_irrep[:, None],
            vir_irrep[None, :],
        ),
        [pltpu.VMEM((count * grid_size, LANES), jnp.float32)],
    )
    return jnp.transpose(updated, (1, 0, 2))


def solution(mesh):
    return jax.shard_map(
        body,
        mesh=mesh,
        in_specs=(
            P("grid", "rep"),
            P("rep", "grid"),
            P("grid", "rep", None),
            P("grid"),
            P("rep"),
            P(),
            P("grid"),
            P("rep"),
            P(),
        ),
        out_specs=P("grid", "rep", None),
        check_vma=False,
    )
```

```python
import functools

import jax
import jax.numpy as jnp
from jax import lax
from jax.experimental import pallas as pl
from jax.experimental.pallas import tpu as pltpu
from jax.sharding import PartitionSpec as P

NOCC = 60
LANES = 128
K_BLOCK = 3840
C_BLOCK = 480
SLOTS = 3
EARLY = 0
COPIES = 4
FIRST_PART = 47
STEPS = 8.0
TOP = 32767.0
MIB = 1024 * 1024


def ceil_to(value, unit):
    return -(-value // unit) * unit


def encode(rows, count):
    index = lax.broadcasted_iota(jnp.int32, rows.shape, 0)
    rows = jnp.where(index < count, rows, 0.0)
    largest = jnp.max(jnp.abs(rows), axis=0, keepdims=True)
    level = jnp.ceil(jnp.log2(jnp.maximum(largest, 1e-30)) * STEPS) + 1.0
    coded = jnp.floor(rows * (jnp.exp2(level * (-1.0 / STEPS)) * TOP) + 0.5)
    return jnp.where(index == count, level, coded)


def decode(block, count):
    index = lax.broadcasted_iota(jnp.int32, block.shape, 0)
    scale = jnp.exp2(block[count : count + 1] * (1.0 / STEPS)) * (1.0 / TOP)
    return jnp.where(index < count, block * scale, 0.0)


def to_code(block):
    return block.astype(jnp.int32).astype(jnp.int16)


def from_code(block):
    return block.astype(jnp.int32).astype(jnp.float32)


def walk_index(place, size):
    return jnp.where(place < size // 2, 2 * place, 2 * (size - 1 - place) + 1)


def walk_place(index, size):
    return jnp.where(index % 2 == 0, index // 2, size - 1 - index // 2)


def coupling_copies(coupling_ref, edge_ref, buffer, sems, low, start, slot):
    block = buffer.shape[1]
    whole = buffer.shape[2] - LANES
    rows = pl.ds(pl.multiple_of(low + start, 16), block)
    quarter = ceil_to(-(-whole // COPIES), 256)
    copies = []
    for number, k in enumerate(range(0, whole, quarter)):
        pairs = pl.ds(k, min(quarter, whole - k))
        copies.append(
            pltpu.make_async_copy(
                coupling_ref.at[rows, pairs], buffer.at[slot, :, pairs], sems.at[slot, number]
            )
        )
    copies.append(
        pltpu.make_async_copy(
            edge_ref.at[rows, :], buffer.at[slot, :, pl.ds(whole, LANES)], sems.at[slot, COPIES]
        )
    )
    return copies


def multiply(coupling_ref, edge_ref, buffer, sems, turned, total_ref, columns, before=None):
    low, many = columns
    block = buffer.shape[1]
    steps = -(-many // block)

    def copies(step):
        start = jnp.minimum(step * block, many - block)
        return coupling_copies(coupling_ref, edge_ref, buffer, sems, low, start, lax.rem(step, SLOTS))

    for ahead in range(min(SLOTS - 1, steps)):
        for copy in copies(jnp.int32(ahead)):
            copy.start()
    if before is not None:
        before()

    def step(number, carry):
        @pl.when(number + SLOTS - 1 < steps)
        def _():
            for copy in copies(number + SLOTS - 1):
                copy.start()

        for copy in copies(number):
            copy.wait()
        total = jnp.dot(
            buffer[lax.rem(number, SLOTS)], turned[...], preferred_element_type=jnp.float32
        )
        rows = pl.ds(pl.multiple_of(jnp.minimum(number * block, many - block), 4), block)
        for part in range(total_ref.shape[0]):
            total_ref[part, rows, :] = total[:, part * LANES : (part + 1) * LANES]
        return carry

    lax.fori_loop(0, steps, step, 0)


def turn_pieces(edges, pieces, gathered, sems, turned, lanes):
    rows = pieces[0].shape[0]
    slots = gathered.shape[0] // rows
    copies = []
    for number, (edge, piece) in enumerate(zip(edges, pieces)):
        target = gathered.at[
            pl.ds(number % slots * rows, rows), pl.ds(edge, piece.shape[1])
        ]
        copies.append(pltpu.make_async_copy(piece, target, sems.at[number]))
    for copy in copies:
        copy.start()
    for copy in copies:
        copy.wait()
    for at in range(0, turned.shape[0], LANES):
        turned[at : at + LANES, lanes : lanes + slots * rows] = gathered[:, at : at + LANES].T


def near_kernel(edges, *refs):
    *pieces, turned, gathered, sems = refs
    turn_pieces(edges, pieces, gathered, sems, turned, 0)


def lead_kernel(edges, columns, span, nears, rep_ref, *refs):
    near, pieces, refs = refs[:nears], refs[nears : nears + len(edges)], refs[nears + len(edges) :]
    coupling_ref, edge_ref, total, turned, send, gathered, sems, buffer, buffer_sems = refs

    def before():
        at, lanes = 0, near[0].shape[1]
        for part in near:
            turned[at : at + part.shape[0], :lanes] = part[...]
            at += part.shape[0]
        turn_pieces(edges, pieces, gathered, sems, turned, lanes)

    multiply(coupling_ref, edge_ref, buffer, buffer_sems, turned, total, columns, before)
    first_send(span, rep_ref, total, send)


def rest_kernel(columns, span, rep_ref, turned, coupling_ref, edge_ref, total, send, buffer, sems):
    multiply(coupling_ref, edge_ref, buffer, sems, turned, total, columns)
    first_send(span, rep_ref, total, send)


def column_rows(total_ref, width, part, j, offset, bp):
    rows = pl.ds(offset + part * width + j, bp, stride=NOCC)
    return jnp.concatenate([total_ref[h, rows, :] for h in range(total_ref.shape[0])], axis=1)


def first_send(span, rep_ref, total_ref, out_ref):
    offset, count, width = span
    low = rep_ref[0] % 2

    def step(j, carry):
        for high in range(2):
            rows = column_rows(total_ref, width, 2 * high + 1 - low, j, offset, out_ref.shape[2])
            out_ref[high, j] = to_code(encode(rows, count))
        return carry

    lax.fori_loop(0, width, step, 0)


def second_send_kernel(span, rep_ref, total_ref, got_ref, out_ref):
    offset, count, width = span
    low, high = rep_ref[0] % 2, 1 - rep_ref[0] // 2

    def step(j, carry):
        rows = column_rows(total_ref, width, 2 * high + low, j, offset, out_ref.shape[1])
        rows = rows + decode(from_code(got_ref[high, j]), count)
        out_ref[j] = to_code(encode(rows, count))
        return carry

    lax.fori_loop(0, width, step, 0)


def keep_kernel(span, rep_ref, total_ref, got_ref, out_ref):
    offset, count, width = span
    low, high = rep_ref[0] % 2, rep_ref[0] // 2

    def step(j, carry):
        rows = column_rows(total_ref, width, 2 * high + low, j, offset, out_ref.shape[1])
        out_ref[j] = rows + decode(from_code(got_ref[high, j]), count)
        return carry

    lax.fori_loop(0, width, step, 0)


def pack_rows(count, rows_dev, kept_ref, got_ref, stage):
    pack = LANES // rows_dev
    groups = stage.shape[1]
    size, _, slab = kept_ref.shape

    def step(jj, carry):
        coded = []
        for jq in range(pack):
            j = jnp.minimum(jq * groups + jj, size - 1)
            coded.append(encode(kept_ref[j] + decode(from_code(got_ref[j]), count), count))
        for g in range(slab // rows_dev):
            own = [block[:, g * rows_dev : (g + 1) * rows_dev] for block in coded]
            stage[g, jj] = to_code(jnp.concatenate(own, axis=1))
        return carry

    lax.fori_loop(0, groups, step, 0)


def third_send_kernel(count, rows_dev, kept_ref, got_ref, *outs):
    *early, stage = outs
    pack_rows(count, rows_dev, kept_ref, got_ref, stage)
    for number, target in enumerate(early):
        target[...] = stage[stage.shape[0] - len(early) + number]


def last_send_kernel(count, rows_dev, parts, early, kept_ref, got_ref, *refs):
    earlier, targets, stage = refs[: parts - 1], refs[parts - 1 : -1], refs[-1]
    pack_rows(count, rows_dev, kept_ref, got_ref, stage)
    for number, target in enumerate(targets):
        at = 0
        for source in (*earlier, stage) if number < len(targets) - early else (stage,):
            bp = source.shape[2]
            target[:, at : at + bp, :] = source[number]
            at += bp


def update_kernel(counts, bps, width, rows_dev, order, early, me_ref, occ_energy_ref, occ_irrep_ref, *refs):
    (
        integrals_ref,
        row_energy_ref,
        vir_energy_ref,
        row_irrep_ref,
        vir_irrep_ref,
        out_ref,
        blocks,
        stage,
    ) = refs[-8:]
    ahead, arrived = refs[:early], refs[early:-8]
    grid_size = len(arrived)
    place = walk_place(me_ref[0], grid_size)
    for number, (offset, got_ref) in enumerate(zip(order, arrived)):
        source = walk_index(lax.rem(place - offset + grid_size, grid_size), grid_size)
        ready = ahead[max(number - (grid_size - len(ahead)), 0) :][:1]
        if number < grid_size - len(ahead):
            ready = []
        at = 0
        for piece in (*ready, got_ref):
            blocks[source, :, at : at + piece.shape[1], :] = piece[...]
            at += piece.shape[1]
    pack = LANES // rows_dev
    for jj in range(blocks.shape[1]):
        at = 0
        for g in range(len(arrived)):
            row = 0
            for count, bp in zip(counts, bps):
                block = decode(from_code(blocks[g, jj, row : row + bp, :]), count)
                stage[at : at + count, :] = block[:count]
                at += count
                row += bp
        turned = stage[...].T
        for jq in range(pack):
            j = jq * blocks.shape[1] + jj
            if j >= width:
                continue
            cycle = turned[jq * rows_dev : (jq + 1) * rows_dev]
            denominator = row_energy_ref[...] + occ_energy_ref[j] - vir_energy_ref[...]
            labels = row_irrep_ref[...] ^ occ_irrep_ref[j] ^ vir_irrep_ref[...]
            out_ref[j] = jnp.where(
                labels == 0, (integrals_ref[j] + cycle) / denominator, jnp.float32(0.0)
            )


def local_call(kernel, out_shape, specs, args, scratch=(), aliases={}, cost=(10**7, 4 * 10**6), room=0):
    spaces = {"s": pltpu.SMEM, "v": pltpu.VMEM, "a": pl.ANY}
    return pl.pallas_call(
        kernel,
        out_shape=out_shape,
        in_specs=[pl.BlockSpec(memory_space=spaces[letter]) for letter in specs],
        out_specs=jax.tree.map(lambda _: pl.BlockSpec(memory_space=pltpu.VMEM), out_shape),
        scratch_shapes=list(scratch),
        input_output_aliases=aliases,
        compiler_params=pltpu.CompilerParams(vmem_limit_bytes=8 * MIB + room),
        cost_estimate=pl.CostEstimate(
            flops=cost[0], bytes_accessed=cost[1], transcendentals=0
        ),
        name=kernel.func.__name__,
    )(*args)


def body(
    amplitudes,
    coupling,
    integrals,
    row_energy,
    occ_energy,
    vir_energy,
    row_irrep,
    occ_irrep,
    vir_irrep,
):
    grid_size = lax.axis_size("grid")
    me = lax.axis_index("grid").astype(jnp.int32).reshape(1)
    rep = lax.axis_index("rep").astype(jnp.int32).reshape(1)
    rows_dev, depth = amplitudes.shape
    coupling = coupling.T
    columns = coupling.shape[0]
    count = columns // NOCC
    ragged = ceil_to(columns, 16) - columns
    if ragged:
        coupling = jnp.pad(coupling, ((0, ragged), (0, 0)))
        columns += ragged
    edge = depth % LANES
    edge = jnp.pad(coupling[:, depth - edge :], ((0, 0), (0, LANES - edge)))
    slab = rows_dev * grid_size
    width = NOCC // lax.axis_size("rep")

    walk = [*range(0, grid_size, 2), *range(1, grid_size, 2)[::-1]]
    onward = [(walk[i], walk[(i + 1) % grid_size]) for i in range(grid_size)]
    back = [(b, a) for a, b in onward]

    counts = [FIRST_PART, count - FIRST_PART] if count > FIRST_PART else [count]
    firsts = [0, FIRST_PART][: len(counts)]
    bps = [ceil_to(number + 1, 16) for number in counts]
    lows = [first * NOCC // 16 * 16 for first in firsts]
    highs = [
        min(columns, ceil_to((first + number) * NOCC, 16)) for first, number in zip(firsts, counts)
    ]
    parts = [(low, high - low) for low, high in zip(lows, highs)]
    spans = [
        (first * NOCC - low, number, width) for first, low, number in zip(firsts, lows, counts)
    ]
    total_shapes = [
        jax.ShapeDtypeStruct((slab // LANES, max(span[0] + bp * NOCC, part[1]), LANES), jnp.float32)
        for span, part, bp in zip(spans, parts, bps)
    ]
    send_shapes = [jax.ShapeDtypeStruct((2, width, bp, slab), jnp.int16) for bp in bps]
    deep = ceil_to(depth, LANES)
    low_pairs = [(i, i ^ 1) for i in range(lax.axis_size("rep"))]
    high_pairs = [(i, i ^ 2) for i in range(lax.axis_size("rep"))]

    half = slab // 2
    large = slab > 2 * LANES

    def turn_near(pieces):
        size = pieces[0].shape[1]
        return local_call(
            functools.partial(near_kernel, (0,) * len(pieces)),
            jax.ShapeDtypeStruct((size, half), jnp.bfloat16),
            "a" * len(pieces),
            pieces,
            [pltpu.VMEM((half, size), jnp.bfloat16), pltpu.SemaphoreType.DMA((len(pieces),))],
            cost=(10**8, 4 * half * size),
            room=2 * half * size * (2 if large else 1),
        )

    longer = grid_size // 2
    order = [0]
    for hop in range(1, longer):
        order += [-hop, hop]
    order.append(longer)
    turned_near, far, far_edges = [], [], []
    for number, at in enumerate(range(0, depth, K_BLOCK)):
        own = amplitudes[:, at : at + K_BLOCK]
        size = own.shape[1]
        own = jnp.pad(own, ((0, 0), (0, ceil_to(size, LANES) - size)))
        ahead = behind = own
        pieces = [own]
        for hop in range(1, longer + 1):
            if hop == longer:
                part = turn_near(pieces[:longer])
                ahead, behind, part = lax.optimization_barrier((ahead, behind, part))
                turned_near.append(part)
            if hop < longer or number % 2 == 0:
                ahead = lax.ppermute(ahead, "grid", onward)
                pieces.append(ahead)
            if hop < longer or number % 2 == 1:
                behind = lax.ppermute(behind, "grid", back)
                pieces.append(behind)
        far += pieces[longer:]
        far_edges += [at] * longer

    totals, sends, got = [], [], []
    for part, (cols, span, bp) in enumerate(zip(parts, spans, bps)):
        cost = (2 * cols[1] * deep * slab, 2 * cols[1] * deep)
        if part == 0:
            block = min(C_BLOCK, ceil_to(cols[1] // 2, 16))
            room = 2 * SLOTS * block * deep + slab * deep
            if large:
                room += 3 * slab * deep + 4 * slab * total_shapes[0].shape[1]
            total, turned, send = local_call(
                functools.partial(lead_kernel, tuple(far_edges), cols, span, len(turned_near)),
                (
                    total_shapes[0],
                    jax.ShapeDtypeStruct((deep, slab), jnp.bfloat16),
                    send_shapes[0],
                ),
                "s" + "v" * len(turned_near) + "a" * (len(far) + 2),
                (rep, *turned_near, *far, coupling, edge),
                [
                    pltpu.VMEM((half, deep), jnp.bfloat16),
                    pltpu.SemaphoreType.DMA((len(far),)),
                    pltpu.VMEM((SLOTS, block, deep), jnp.bfloat16),
                    pltpu.SemaphoreType.DMA((SLOTS, COPIES + 1)),
                ],
                cost=cost,
                room=room,
            )
        else:
            turned, _ = lax.optimization_barrier((turned, sends[0]))
            block = min(C_BLOCK, ceil_to(cols[1] // 2, 16))
            total, send = local_call(
                functools.partial(rest_kernel, cols, span),
                (total_shapes[part], send_shapes[part]),
                "svaa",
                (rep, turned, coupling, edge),
                [
                    pltpu.VMEM((SLOTS, block, deep), jnp.bfloat16),
                    pltpu.SemaphoreType.DMA((SLOTS, COPIES + 1)),
                ],
                cost=cost,
                room=2 * SLOTS * block * deep,
            )
        arrived = lax.ppermute(send, "rep", low_pairs)
        totals.append(total)
        got.append(arrived)
        sends.append(
            local_call(
                functools.partial(second_send_kernel, span),
                jax.ShapeDtypeStruct((width, bp, slab), jnp.int16),
                "svv",
                (rep, total, arrived),
            )
        )
    kept = [
        local_call(
            functools.partial(keep_kernel, span),
            jax.ShapeDtypeStruct((width, bp, slab), jnp.float32),
            "svv",
            (rep, total, arrived),
        )
        for span, bp, total, arrived in zip(spans, bps, totals, got)
    ]
    got = [lax.ppermute(send, "rep", high_pairs) for send in sends]

    groups = -(-width // (LANES // rows_dev))
    staged, left = [], []
    early = min(EARLY, grid_size - 1) if len(spans) > 1 else 0
    for part, span in enumerate(spans[:-1]):
        mine, _ = lax.optimization_barrier((kept[part], sends[-1]))
        *leaving, stage = local_call(
            functools.partial(third_send_kernel, span[1], rows_dev),
            (jax.ShapeDtypeStruct((groups, bps[part], LANES), jnp.int16),) * early
            + (jax.ShapeDtypeStruct((grid_size, groups, bps[part], LANES), jnp.int16),),
            "vv",
            (mine, got[part]),
        )
        staged.append(stage)
        left += leaving
    rows = [sum(bps)] * (grid_size - early) + [bps[-1]] * early
    targets = local_call(
        functools.partial(last_send_kernel, counts[-1], rows_dev, len(counts), early),
        tuple(jax.ShapeDtypeStruct((groups, many, LANES), jnp.int16) for many in rows),
        "vv" + "v" * len(staged),
        (kept[-1], got[-1], *staged),
        [pltpu.VMEM((grid_size, groups, bps[-1], LANES), jnp.int16)],
    )

    def go_back(block, number):
        pairs = [(walk[i], walk[(i + order[number]) % grid_size]) for i in range(grid_size)]
        return lax.ppermute(block, "grid", pairs)

    ahead = [go_back(block, grid_size - early + i) for i, block in enumerate(left)]
    arrived = list(targets)
    for number in range(1, grid_size)[::-1]:
        arrived[number] = go_back(targets[number], number)

    updated = local_call(
        functools.partial(update_kernel, counts, bps, width, rows_dev, order, early),
        jax.ShapeDtypeStruct((width, rows_dev, count * grid_size), jnp.float32),
        "sss" + "v" * (early + len(arrived) + 5),
        (
            me,
            occ_energy,
            occ_irrep,
            *ahead,
            *arrived,
            jnp.transpose(integrals, (1, 0, 2)),
            row_energy[:, None],
            vir_energy[None, :],
            row_irrep[:, None],
            vir_irrep[None, :],
        ),
        [
            pltpu.VMEM((grid_size, groups, sum(bps), LANES), jnp.int16),
            pltpu.VMEM((count * grid_size, LANES), jnp.float32),
        ],
    )
    return jnp.transpose(updated, (1, 0, 2))


def solution(mesh):
    return jax.shard_map(
        body,
        mesh=mesh,
        in_specs=(
            P("grid", "rep"),
            P("rep", "grid"),
            P("grid", "rep", None),
            P("grid"),
            P("rep"),
            P(),
            P("grid"),
            P("rep"),
            P(),
        ),
        out_specs=P("grid", "rep", None),
        check_vma=False,
    )
```

```python
import functools

import jax
import jax.numpy as jnp
from jax import lax
from jax.experimental import pallas as pl
from jax.experimental.pallas import tpu as pltpu
from jax.sharding import PartitionSpec as P

NOCC = 60
LANES = 128
K_BLOCK = 3840
C_BLOCK = 480
SLOTS = 3
COPIES = 4
FIRST_PART = 47
STEPS = 8.0
TOP = 32767.0
MIB = 1024 * 1024


def ceil_to(value, unit):
    return -(-value // unit) * unit


def encode(rows, count):
    index = lax.broadcasted_iota(jnp.int32, rows.shape, 0)
    rows = jnp.where(index < count, rows, 0.0)
    largest = jnp.max(jnp.abs(rows), axis=0, keepdims=True)
    level = jnp.ceil(jnp.log2(jnp.maximum(largest, 1e-30)) * STEPS) + 1.0
    coded = jnp.floor(rows * (jnp.exp2(level * (-1.0 / STEPS)) * TOP) + 0.5)
    return jnp.where(index == count, level, coded)


def decode(block, count):
    index = lax.broadcasted_iota(jnp.int32, block.shape, 0)
    scale = jnp.exp2(block[count : count + 1] * (1.0 / STEPS)) * (1.0 / TOP)
    return jnp.where(index < count, block * scale, 0.0)


def to_code(block):
    return block.astype(jnp.int32).astype(jnp.int16)


def from_code(block):
    return block.astype(jnp.int32).astype(jnp.float32)


def walk_index(place, size):
    return jnp.where(place < size // 2, 2 * place, 2 * (size - 1 - place) + 1)


def walk_place(index, size):
    return jnp.where(index % 2 == 0, index // 2, size - 1 - index // 2)


def coupling_copies(coupling_ref, edge_ref, buffer, sems, low, start, slot):
    block = buffer.shape[1]
    whole = buffer.shape[2] - LANES
    rows = pl.ds(pl.multiple_of(low + start, 16), block)
    quarter = ceil_to(-(-whole // COPIES), 256)
    copies = []
    for number, k in enumerate(range(0, whole, quarter)):
        pairs = pl.ds(k, min(quarter, whole - k))
        copies.append(
            pltpu.make_async_copy(
                coupling_ref.at[rows, pairs], buffer.at[slot, :, pairs], sems.at[slot, number]
            )
        )
    copies.append(
        pltpu.make_async_copy(
            edge_ref.at[rows, :], buffer.at[slot, :, pl.ds(whole, LANES)], sems.at[slot, COPIES]
        )
    )
    return copies


def multiply(coupling_ref, edge_ref, buffer, sems, turned, total_ref, columns, before=None):
    low, many = columns
    block = buffer.shape[1]
    steps = -(-many // block)

    def copies(step):
        start = jnp.minimum(step * block, many - block)
        return coupling_copies(coupling_ref, edge_ref, buffer, sems, low, start, lax.rem(step, SLOTS))

    for ahead in range(min(SLOTS - 1, steps)):
        for copy in copies(jnp.int32(ahead)):
            copy.start()
    if before is not None:
        before()

    def step(number, carry):
        @pl.when(number + SLOTS - 1 < steps)
        def _():
            for copy in copies(number + SLOTS - 1):
                copy.start()

        for copy in copies(number):
            copy.wait()
        total = jnp.dot(
            buffer[lax.rem(number, SLOTS)], turned[...], preferred_element_type=jnp.float32
        )
        rows = pl.ds(pl.multiple_of(jnp.minimum(number * block, many - block), 4), block)
        for part in range(total_ref.shape[0]):
            total_ref[part, rows, :] = total[:, part * LANES : (part + 1) * LANES]
        return carry

    lax.fori_loop(0, steps, step, 0)


def turn_pieces(edges, pieces, gathered, sems, turned, lanes):
    rows = pieces[0].shape[0]
    slots = gathered.shape[0] // rows
    copies = []
    for number, (edge, piece) in enumerate(zip(edges, pieces)):
        target = gathered.at[
            pl.ds(number % slots * rows, rows), pl.ds(edge, piece.shape[1])
        ]
        copies.append(pltpu.make_async_copy(piece, target, sems.at[number]))
    for copy in copies:
        copy.start()
    for copy in copies:
        copy.wait()
    for at in range(0, turned.shape[0], LANES):
        turned[at : at + LANES, lanes : lanes + slots * rows] = gathered[:, at : at + LANES].T


def near_kernel(edges, *refs):
    *pieces, turned, gathered, sems = refs
    turn_pieces(edges, pieces, gathered, sems, turned, 0)


def lead_kernel(edges, columns, span, rep_ref, near, *refs):
    pieces, refs = refs[: len(edges)], refs[len(edges) :]
    coupling_ref, edge_ref, total, turned, send, gathered, sems, buffer, buffer_sems = refs

    def before():
        lanes = near.shape[1]
        turned[:, :lanes] = near[...]
        turn_pieces(edges, pieces, gathered, sems, turned, lanes)

    multiply(coupling_ref, edge_ref, buffer, buffer_sems, turned, total, columns, before)
    first_send(span, rep_ref, total, send)


def rest_kernel(columns, span, rep_ref, turned, coupling_ref, edge_ref, total, send, buffer, sems):
    multiply(coupling_ref, edge_ref, buffer, sems, turned, total, columns)
    first_send(span, rep_ref, total, send)


def column_rows(total_ref, width, part, j, offset, bp):
    rows = pl.ds(offset + part * width + j, bp, stride=NOCC)
    return jnp.concatenate([total_ref[h, rows, :] for h in range(total_ref.shape[0])], axis=1)


def first_send(span, rep_ref, total_ref, out_ref):
    offset, count, width = span
    low = rep_ref[0] % 2

    def step(j, carry):
        for high in range(2):
            rows = column_rows(total_ref, width, 2 * high + 1 - low, j, offset, out_ref.shape[2])
            out_ref[high, j] = to_code(encode(rows, count))
        return carry

    lax.fori_loop(0, width, step, 0)


def second_send_kernel(span, rep_ref, total_ref, got_ref, out_ref):
    offset, count, width = span
    low, high = rep_ref[0] % 2, 1 - rep_ref[0] // 2

    def step(j, carry):
        rows = column_rows(total_ref, width, 2 * high + low, j, offset, out_ref.shape[1])
        rows = rows + decode(from_code(got_ref[high, j]), count)
        out_ref[j] = to_code(encode(rows, count))
        return carry

    lax.fori_loop(0, width, step, 0)


def keep_kernel(span, rep_ref, total_ref, got_ref, out_ref):
    offset, count, width = span
    low, high = rep_ref[0] % 2, rep_ref[0] // 2

    def step(j, carry):
        rows = column_rows(total_ref, width, 2 * high + low, j, offset, out_ref.shape[1])
        out_ref[j] = rows + decode(from_code(got_ref[high, j]), count)
        return carry

    lax.fori_loop(0, width, step, 0)


def pack_rows(count, rows_dev, kept_ref, got_ref, stage):
    pack = LANES // rows_dev
    groups = stage.shape[1]
    size, _, slab = kept_ref.shape

    def step(jj, carry):
        coded = []
        for jq in range(pack):
            j = jnp.minimum(jq * groups + jj, size - 1)
            coded.append(encode(kept_ref[j] + decode(from_code(got_ref[j]), count), count))
        for g in range(slab // rows_dev):
            own = [block[:, g * rows_dev : (g + 1) * rows_dev] for block in coded]
            stage[g, jj] = to_code(jnp.concatenate(own, axis=1))
        return carry

    lax.fori_loop(0, groups, step, 0)


def third_send_kernel(count, rows_dev, kept_ref, got_ref, stage):
    pack_rows(count, rows_dev, kept_ref, got_ref, stage)


def last_send_kernel(count, rows_dev, parts, kept_ref, got_ref, *refs):
    earlier, targets, stage = refs[: parts - 1], refs[parts - 1 : -1], refs[-1]
    pack_rows(count, rows_dev, kept_ref, got_ref, stage)
    for number, target in enumerate(targets):
        at = 0
        for source in (*earlier, stage):
            bp = source.shape[2]
            target[:, at : at + bp, :] = source[number]
            at += bp


def update_kernel(counts, bps, width, rows_dev, order, me_ref, occ_energy_ref, occ_irrep_ref, *refs):
    (
        integrals_ref,
        row_energy_ref,
        vir_energy_ref,
        row_irrep_ref,
        vir_irrep_ref,
        out_ref,
        blocks,
        stage,
    ) = refs[-8:]
    arrived = refs[:-8]
    grid_size = len(arrived)
    place = walk_place(me_ref[0], grid_size)
    for offset, got_ref in zip(order, arrived):
        source = walk_index(lax.rem(place - offset + grid_size, grid_size), grid_size)
        blocks[source] = got_ref[...]
    pack = LANES // rows_dev
    for jj in range(blocks.shape[1]):
        at = 0
        for g in range(len(arrived)):
            row = 0
            for count, bp in zip(counts, bps):
                block = decode(from_code(blocks[g, jj, row : row + bp, :]), count)
                stage[at : at + count, :] = block[:count]
                at += count
                row += bp
        turned = stage[...].T
        for jq in range(pack):
            j = jq * blocks.shape[1] + jj
            if j >= width:
                continue
            cycle = turned[jq * rows_dev : (jq + 1) * rows_dev]
            denominator = row_energy_ref[...] + occ_energy_ref[j] - vir_energy_ref[...]
            labels = row_irrep_ref[...] ^ occ_irrep_ref[j] ^ vir_irrep_ref[...]
            out_ref[j] = jnp.where(
                labels == 0, (integrals_ref[j] + cycle) / denominator, jnp.float32(0.0)
            )


def local_call(kernel, out_shape, specs, args, scratch=(), aliases={}, cost=(10**7, 4 * 10**6), room=0):
    spaces = {"s": pltpu.SMEM, "v": pltpu.VMEM, "a": pl.ANY}
    return pl.pallas_call(
        kernel,
        out_shape=out_shape,
        in_specs=[pl.BlockSpec(memory_space=spaces[letter]) for letter in specs],
        out_specs=jax.tree.map(lambda _: pl.BlockSpec(memory_space=pltpu.VMEM), out_shape),
        scratch_shapes=list(scratch),
        input_output_aliases=aliases,
        compiler_params=pltpu.CompilerParams(vmem_limit_bytes=8 * MIB + room),
        cost_estimate=pl.CostEstimate(
            flops=cost[0], bytes_accessed=cost[1], transcendentals=0
        ),
        name=kernel.func.__name__,
    )(*args)


def body(
    amplitudes,
    coupling,
    integrals,
    row_energy,
    occ_energy,
    vir_energy,
    row_irrep,
    occ_irrep,
    vir_irrep,
):
    grid_size = lax.axis_size("grid")
    me = lax.axis_index("grid").astype(jnp.int32).reshape(1)
    rep = lax.axis_index("rep").astype(jnp.int32).reshape(1)
    rows_dev, depth = amplitudes.shape
    coupling = coupling.T
    columns = coupling.shape[0]
    count = columns // NOCC
    ragged = ceil_to(columns, 16) - columns
    if ragged:
        coupling = jnp.pad(coupling, ((0, ragged), (0, 0)))
        columns += ragged
    edge = depth % LANES
    edge = jnp.pad(coupling[:, depth - edge :], ((0, 0), (0, LANES - edge)))
    slab = rows_dev * grid_size
    width = NOCC // lax.axis_size("rep")

    walk = [*range(0, grid_size, 2), *range(1, grid_size, 2)[::-1]]
    onward = [(walk[i], walk[(i + 1) % grid_size]) for i in range(grid_size)]
    back = [(b, a) for a, b in onward]

    longer = grid_size // 2
    order = [0]
    for hop in range(1, longer):
        order += [-hop, hop]
    order.append(longer)
    near, far, near_edges, far_edges = [], [], [], []
    for number, at in enumerate(range(0, depth, K_BLOCK)):
        own = amplitudes[:, at : at + K_BLOCK]
        size = own.shape[1]
        own = jnp.pad(own, ((0, 0), (0, ceil_to(size, LANES) - size)))
        ahead = behind = own
        pieces = [own]
        for hop in range(1, longer + 1):
            if hop == longer:
                ahead, behind = lax.optimization_barrier((ahead, behind))
            if hop < longer or number % 2 == 0:
                ahead = lax.ppermute(ahead, "grid", onward)
                pieces.append(ahead)
            if hop < longer or number % 2 == 1:
                behind = lax.ppermute(behind, "grid", back)
                pieces.append(behind)
        near += pieces[:longer]
        far += pieces[longer:]
        near_edges += [at] * longer
        far_edges += [at] * longer

    counts = [FIRST_PART, count - FIRST_PART] if count > FIRST_PART else [count]
    firsts = [0, FIRST_PART][: len(counts)]
    bps = [ceil_to(number + 1, 16) for number in counts]
    lows = [first * NOCC // 16 * 16 for first in firsts]
    highs = [
        min(columns, ceil_to((first + number) * NOCC, 16)) for first, number in zip(firsts, counts)
    ]
    parts = [(low, high - low) for low, high in zip(lows, highs)]
    spans = [
        (first * NOCC - low, number, width) for first, low, number in zip(firsts, lows, counts)
    ]
    total_shapes = [
        jax.ShapeDtypeStruct((slab // LANES, max(span[0] + bp * NOCC, part[1]), LANES), jnp.float32)
        for span, part, bp in zip(spans, parts, bps)
    ]
    send_shapes = [jax.ShapeDtypeStruct((2, width, bp, slab), jnp.int16) for bp in bps]
    deep = ceil_to(depth, LANES)
    low_pairs = [(i, i ^ 1) for i in range(lax.axis_size("rep"))]
    high_pairs = [(i, i ^ 2) for i in range(lax.axis_size("rep"))]

    half = slab // 2
    turn_scratch = [
        pltpu.VMEM((half, deep), jnp.bfloat16),
        pltpu.SemaphoreType.DMA((len(near),)),
    ]
    near = local_call(
        functools.partial(near_kernel, tuple(near_edges)),
        jax.ShapeDtypeStruct((deep, half), jnp.bfloat16),
        "a" * len(near),
        near,
        turn_scratch,
        cost=(10**8, 4 * half * deep),
        room=2 * half * deep + (2 * half * deep if slab > 2 * LANES else 0),
    )
    totals, sends, got = [], [], []
    for part, (cols, span, bp) in enumerate(zip(parts, spans, bps)):
        block = min(C_BLOCK, ceil_to(cols[1] // 2, 16))
        scratch = [
            pltpu.VMEM((SLOTS, block, deep), jnp.bfloat16),
            pltpu.SemaphoreType.DMA((SLOTS, COPIES + 1)),
        ]
        cost = (2 * cols[1] * deep * slab, 2 * cols[1] * deep)
        room = 2 * SLOTS * block * deep + (slab * deep if part == 0 else 0)
        if slab > 2 * LANES:
            room += 3 * slab * deep + 4 * slab * total_shapes[part].shape[1]
        if part == 0:
            total, turned, send = local_call(
                functools.partial(lead_kernel, tuple(far_edges), cols, span),
                (
                    total_shapes[0],
                    jax.ShapeDtypeStruct((deep, slab), jnp.bfloat16),
                    send_shapes[0],
                ),
                "sv" + "a" * (len(far) + 2),
                (rep, near, *far, coupling, edge),
                [*turn_scratch, *scratch],
                cost=cost,
                room=room,
            )
        else:
            turned, _ = lax.optimization_barrier((turned, sends[0]))
            total, send = local_call(
                functools.partial(rest_kernel, cols, span),
                (total_shapes[part], send_shapes[part]),
                "svaa",
                (rep, turned, coupling, edge),
                scratch,
                cost=cost,
                room=room,
            )
        arrived = lax.ppermute(send, "rep", low_pairs)
        totals.append(total)
        got.append(arrived)
        sends.append(
            local_call(
                functools.partial(second_send_kernel, span),
                jax.ShapeDtypeStruct((width, bp, slab), jnp.int16),
                "svv",
                (rep, total, arrived),
            )
        )
    kept = [
        local_call(
            functools.partial(keep_kernel, span),
            jax.ShapeDtypeStruct((width, bp, slab), jnp.float32),
            "svv",
            (rep, total, arrived),
        )
        for span, bp, total, arrived in zip(spans, bps, totals, got)
    ]
    got = [lax.ppermute(send, "rep", high_pairs) for send in sends]

    groups = -(-width // (LANES // rows_dev))
    staged = []
    for part, span in enumerate(spans[:-1]):
        mine, _ = lax.optimization_barrier((kept[part], sends[-1]))
        staged.append(
            local_call(
                functools.partial(third_send_kernel, span[1], rows_dev),
                jax.ShapeDtypeStruct((grid_size, groups, bps[part], LANES), jnp.int16),
                "vv",
                (mine, got[part]),
            )
        )
    targets = local_call(
        functools.partial(last_send_kernel, counts[-1], rows_dev, len(counts)),
        (jax.ShapeDtypeStruct((groups, sum(bps), LANES), jnp.int16),) * grid_size,
        "vv" + "v" * len(staged),
        (kept[-1], got[-1], *staged),
        [pltpu.VMEM((grid_size, groups, bps[-1], LANES), jnp.int16)],
    )
    arrived = list(targets)
    for number in range(1, grid_size)[::-1]:
        arrived[number] = lax.ppermute(
            targets[number],
            "grid",
            [(walk[i], walk[(i + order[number]) % grid_size]) for i in range(grid_size)],
        )

    updated = local_call(
        functools.partial(update_kernel, counts, bps, width, rows_dev, order),
        jax.ShapeDtypeStruct((width, rows_dev, count * grid_size), jnp.float32),
        "sss" + "v" * (len(arrived) + 5),
        (
            me,
            occ_energy,
            occ_irrep,
            *arrived,
            jnp.transpose(integrals, (1, 0, 2)),
            row_energy[:, None],
            vir_energy[None, :],
            row_irrep[:, None],
            vir_irrep[None, :],
        ),
        [
            pltpu.VMEM((grid_size, groups, sum(bps), LANES), jnp.int16),
            pltpu.VMEM((count * grid_size, LANES), jnp.float32),
        ],
    )
    return jnp.transpose(updated, (1, 0, 2))


def solution(mesh):
    return jax.shard_map(
        body,
        mesh=mesh,
        in_specs=(
            P("grid", "rep"),
            P("rep", "grid"),
            P("grid", "rep", None),
            P("grid"),
            P("rep"),
            P(),
            P("grid"),
            P("rep"),
            P(),
        ),
        out_specs=P("grid", "rep", None),
        check_vma=False,
    )
```

```python
import functools

import jax
import jax.numpy as jnp
from jax import lax
from jax.experimental import pallas as pl
from jax.experimental.pallas import tpu as pltpu
from jax.sharding import PartitionSpec as P

NOCC = 60
LANES = 128
K_BLOCK = 3840
C_BLOCK = 320
SLOTS = 4
COPIES = 4
FIRST_PART = 47
STEPS = 8.0
TOP = 32767.0
MIB = 1024 * 1024


def ceil_to(value, unit):
    return -(-value // unit) * unit


def encode(rows, count):
    index = lax.broadcasted_iota(jnp.int32, rows.shape, 0)
    rows = jnp.where(index < count, rows, 0.0)
    largest = jnp.max(jnp.abs(rows), axis=0, keepdims=True)
    level = jnp.ceil(jnp.log2(jnp.maximum(largest, 1e-30)) * STEPS) + 1.0
    coded = jnp.floor(rows * (jnp.exp2(level * (-1.0 / STEPS)) * TOP) + 0.5)
    return jnp.where(index == count, level, coded)


def decode(block, count):
    index = lax.broadcasted_iota(jnp.int32, block.shape, 0)
    scale = jnp.exp2(block[count : count + 1] * (1.0 / STEPS)) * (1.0 / TOP)
    return jnp.where(index < count, block * scale, 0.0)


def to_code(block):
    return block.astype(jnp.int32).astype(jnp.int16)


def from_code(block):
    return block.astype(jnp.int32).astype(jnp.float32)


def walk_index(place, size):
    return jnp.where(place < size // 2, 2 * place, 2 * (size - 1 - place) + 1)


def walk_place(index, size):
    return jnp.where(index % 2 == 0, index // 2, size - 1 - index // 2)


def coupling_copies(coupling_ref, edge_ref, buffer, sems, low, start, slot):
    block = buffer.shape[1]
    whole = buffer.shape[2] - LANES
    rows = pl.ds(pl.multiple_of(low + start, 16), block)
    quarter = ceil_to(-(-whole // COPIES), 256)
    copies = []
    for number, k in enumerate(range(0, whole, quarter)):
        pairs = pl.ds(k, min(quarter, whole - k))
        copies.append(
            pltpu.make_async_copy(
                coupling_ref.at[rows, pairs], buffer.at[slot, :, pairs], sems.at[slot, number]
            )
        )
    copies.append(
        pltpu.make_async_copy(
            edge_ref.at[rows, :], buffer.at[slot, :, pl.ds(whole, LANES)], sems.at[slot, COPIES]
        )
    )
    return copies


def multiply(coupling_ref, edge_ref, buffer, sems, turned, total_ref, columns, before=None):
    low, many = columns
    block = buffer.shape[1]
    steps = -(-many // block)

    def copies(step):
        start = jnp.minimum(step * block, many - block)
        return coupling_copies(coupling_ref, edge_ref, buffer, sems, low, start, lax.rem(step, SLOTS))

    for ahead in range(min(SLOTS - 1, steps)):
        for copy in copies(jnp.int32(ahead)):
            copy.start()
    if before is not None:
        before()

    def step(number, carry):
        @pl.when(number + SLOTS - 1 < steps)
        def _():
            for copy in copies(number + SLOTS - 1):
                copy.start()

        for copy in copies(number):
            copy.wait()
        total = jnp.dot(
            buffer[lax.rem(number, SLOTS)], turned[...], preferred_element_type=jnp.float32
        )
        rows = pl.ds(pl.multiple_of(jnp.minimum(number * block, many - block), 4), block)
        for part in range(total_ref.shape[0]):
            total_ref[part, rows, :] = total[:, part * LANES : (part + 1) * LANES]
        return carry

    lax.fori_loop(0, steps, step, 0)


def turn_pieces(edges, pieces, gathered, sems, turned, lanes):
    rows = pieces[0].shape[0]
    slots = gathered.shape[0] // rows
    copies = []
    for number, (edge, piece) in enumerate(zip(edges, pieces)):
        target = gathered.at[
            pl.ds(number % slots * rows, rows), pl.ds(edge, piece.shape[1])
        ]
        copies.append(pltpu.make_async_copy(piece, target, sems.at[number]))
    for copy in copies:
        copy.start()
    for copy in copies:
        copy.wait()
    for at in range(0, turned.shape[0], LANES):
        turned[at : at + LANES, lanes : lanes + slots * rows] = gathered[:, at : at + LANES].T


def near_kernel(edges, *refs):
    *pieces, turned, gathered, sems = refs
    turn_pieces(edges, pieces, gathered, sems, turned, 0)


def lead_kernel(edges, columns, span, rep_ref, near, *refs):
    pieces, refs = refs[: len(edges)], refs[len(edges) :]
    coupling_ref, edge_ref, total, turned, send, gathered, sems, buffer, buffer_sems = refs

    def before():
        lanes = near.shape[1]
        turned[:, :lanes] = near[...]
        turn_pieces(edges, pieces, gathered, sems, turned, lanes)

    multiply(coupling_ref, edge_ref, buffer, buffer_sems, turned, total, columns, before)
    first_send(span, rep_ref, total, send)


def rest_kernel(columns, span, rep_ref, turned, coupling_ref, edge_ref, total, send, buffer, sems):
    multiply(coupling_ref, edge_ref, buffer, sems, turned, total, columns)
    first_send(span, rep_ref, total, send)


def column_rows(total_ref, width, part, j, offset, bp):
    rows = pl.ds(offset + part * width + j, bp, stride=NOCC)
    return jnp.concatenate([total_ref[h, rows, :] for h in range(total_ref.shape[0])], axis=1)


def first_send(span, rep_ref, total_ref, out_ref):
    offset, count, width = span
    low = rep_ref[0] % 2

    def step(j, carry):
        for high in range(2):
            rows = column_rows(total_ref, width, 2 * high + 1 - low, j, offset, out_ref.shape[2])
            out_ref[high, j] = to_code(encode(rows, count))
        return carry

    lax.fori_loop(0, width, step, 0)


def second_send_kernel(span, rep_ref, total_ref, got_ref, out_ref):
    offset, count, width = span
    low, high = rep_ref[0] % 2, 1 - rep_ref[0] // 2

    def step(j, carry):
        rows = column_rows(total_ref, width, 2 * high + low, j, offset, out_ref.shape[1])
        rows = rows + decode(from_code(got_ref[high, j]), count)
        out_ref[j] = to_code(encode(rows, count))
        return carry

    lax.fori_loop(0, width, step, 0)


def keep_kernel(span, rep_ref, total_ref, got_ref, out_ref):
    offset, count, width = span
    low, high = rep_ref[0] % 2, rep_ref[0] // 2

    def step(j, carry):
        rows = column_rows(total_ref, width, 2 * high + low, j, offset, out_ref.shape[1])
        out_ref[j] = rows + decode(from_code(got_ref[high, j]), count)
        return carry

    lax.fori_loop(0, width, step, 0)


def pack_rows(count, rows_dev, kept_ref, got_ref, stage):
    pack = LANES // rows_dev
    groups = stage.shape[1]
    size, _, slab = kept_ref.shape

    def step(jj, carry):
        coded = []
        for jq in range(pack):
            j = jnp.minimum(jq * groups + jj, size - 1)
            coded.append(encode(kept_ref[j] + decode(from_code(got_ref[j]), count), count))
        for g in range(slab // rows_dev):
            own = [block[:, g * rows_dev : (g + 1) * rows_dev] for block in coded]
            stage[g, jj] = to_code(jnp.concatenate(own, axis=1))
        return carry

    lax.fori_loop(0, groups, step, 0)


def third_send_kernel(count, rows_dev, kept_ref, got_ref, stage):
    pack_rows(count, rows_dev, kept_ref, got_ref, stage)


def last_send_kernel(count, rows_dev, parts, kept_ref, got_ref, *refs):
    earlier, targets, stage = refs[: parts - 1], refs[parts - 1 : -1], refs[-1]
    pack_rows(count, rows_dev, kept_ref, got_ref, stage)
    for number, target in enumerate(targets):
        at = 0
        for source in (*earlier, stage):
            bp = source.shape[2]
            target[:, at : at + bp, :] = source[number]
            at += bp


def update_kernel(counts, bps, width, rows_dev, order, me_ref, occ_energy_ref, occ_irrep_ref, *refs):
    (
        integrals_ref,
        row_energy_ref,
        vir_energy_ref,
        row_irrep_ref,
        vir_irrep_ref,
        out_ref,
        blocks,
        stage,
    ) = refs[-8:]
    arrived = refs[:-8]
    grid_size = len(arrived)
    place = walk_place(me_ref[0], grid_size)
    for offset, got_ref in zip(order, arrived):
        source = walk_index(lax.rem(place - offset + grid_size, grid_size), grid_size)
        blocks[source] = got_ref[...]
    pack = LANES // rows_dev
    for jj in range(blocks.shape[1]):
        at = 0
        for g in range(len(arrived)):
            row = 0
            for count, bp in zip(counts, bps):
                block = decode(from_code(blocks[g, jj, row : row + bp, :]), count)
                stage[at : at + count, :] = block[:count]
                at += count
                row += bp
        turned = stage[...].T
        for jq in range(pack):
            j = jq * blocks.shape[1] + jj
            if j >= width:
                continue
            cycle = turned[jq * rows_dev : (jq + 1) * rows_dev]
            denominator = row_energy_ref[...] + occ_energy_ref[j] - vir_energy_ref[...]
            labels = row_irrep_ref[...] ^ occ_irrep_ref[j] ^ vir_irrep_ref[...]
            out_ref[j] = jnp.where(
                labels == 0, (integrals_ref[j] + cycle) / denominator, jnp.float32(0.0)
            )


def local_call(kernel, out_shape, specs, args, scratch=(), aliases={}, cost=(10**7, 4 * 10**6), room=0):
    spaces = {"s": pltpu.SMEM, "v": pltpu.VMEM, "a": pl.ANY}
    return pl.pallas_call(
        kernel,
        out_shape=out_shape,
        in_specs=[pl.BlockSpec(memory_space=spaces[letter]) for letter in specs],
        out_specs=jax.tree.map(lambda _: pl.BlockSpec(memory_space=pltpu.VMEM), out_shape),
        scratch_shapes=list(scratch),
        input_output_aliases=aliases,
        compiler_params=pltpu.CompilerParams(vmem_limit_bytes=8 * MIB + room),
        cost_estimate=pl.CostEstimate(
            flops=cost[0], bytes_accessed=cost[1], transcendentals=0
        ),
        name=kernel.func.__name__,
    )(*args)


def body(
    amplitudes,
    coupling,
    integrals,
    row_energy,
    occ_energy,
    vir_energy,
    row_irrep,
    occ_irrep,
    vir_irrep,
):
    grid_size = lax.axis_size("grid")
    me = lax.axis_index("grid").astype(jnp.int32).reshape(1)
    rep = lax.axis_index("rep").astype(jnp.int32).reshape(1)
    rows_dev, depth = amplitudes.shape
    coupling = coupling.T
    columns = coupling.shape[0]
    count = columns // NOCC
    ragged = ceil_to(columns, 16) - columns
    if ragged:
        coupling = jnp.pad(coupling, ((0, ragged), (0, 0)))
        columns += ragged
    edge = depth % LANES
    edge = jnp.pad(coupling[:, depth - edge :], ((0, 0), (0, LANES - edge)))
    slab = rows_dev * grid_size
    width = NOCC // lax.axis_size("rep")

    walk = [*range(0, grid_size, 2), *range(1, grid_size, 2)[::-1]]
    onward = [(walk[i], walk[(i + 1) % grid_size]) for i in range(grid_size)]
    back = [(b, a) for a, b in onward]

    longer = grid_size // 2
    order = [0]
    for hop in range(1, longer):
        order += [-hop, hop]
    order.append(longer)
    near, far, near_edges, far_edges = [], [], [], []
    for number, at in enumerate(range(0, depth, K_BLOCK)):
        own = amplitudes[:, at : at + K_BLOCK]
        size = own.shape[1]
        own = jnp.pad(own, ((0, 0), (0, ceil_to(size, LANES) - size)))
        ahead = behind = own
        pieces = [own]
        for hop in range(1, longer + 1):
            if hop == longer:
                ahead, behind = lax.optimization_barrier((ahead, behind))
            if hop < longer or number % 2 == 0:
                ahead = lax.ppermute(ahead, "grid", onward)
                pieces.append(ahead)
            if hop < longer or number % 2 == 1:
                behind = lax.ppermute(behind, "grid", back)
                pieces.append(behind)
        near += pieces[:longer]
        far += pieces[longer:]
        near_edges += [at] * longer
        far_edges += [at] * longer

    counts = [FIRST_PART, count - FIRST_PART] if count > FIRST_PART else [count]
    firsts = [0, FIRST_PART][: len(counts)]
    bps = [ceil_to(number + 1, 16) for number in counts]
    lows = [first * NOCC // 16 * 16 for first in firsts]
    highs = [
        min(columns, ceil_to((first + number) * NOCC, 16)) for first, number in zip(firsts, counts)
    ]
    parts = [(low, high - low) for low, high in zip(lows, highs)]
    spans = [
        (first * NOCC - low, number, width) for first, low, number in zip(firsts, lows, counts)
    ]
    total_shapes = [
        jax.ShapeDtypeStruct((slab // LANES, max(span[0] + bp * NOCC, part[1]), LANES), jnp.float32)
        for span, part, bp in zip(spans, parts, bps)
    ]
    send_shapes = [jax.ShapeDtypeStruct((2, width, bp, slab), jnp.int16) for bp in bps]
    deep = ceil_to(depth, LANES)
    low_pairs = [(i, i ^ 1) for i in range(lax.axis_size("rep"))]
    high_pairs = [(i, i ^ 2) for i in range(lax.axis_size("rep"))]

    half = slab // 2
    turn_scratch = [
        pltpu.VMEM((half, deep), jnp.bfloat16),
        pltpu.SemaphoreType.DMA((len(near),)),
    ]
    near = local_call(
        functools.partial(near_kernel, tuple(near_edges)),
        jax.ShapeDtypeStruct((deep, half), jnp.bfloat16),
        "a" * len(near),
        near,
        turn_scratch,
        cost=(10**8, 4 * half * deep),
        room=2 * half * deep + (2 * half * deep if slab > 2 * LANES else 0),
    )
    totals, sends, got = [], [], []
    for part, (cols, span, bp) in enumerate(zip(parts, spans, bps)):
        block = min(C_BLOCK, ceil_to(-(-cols[1] // 3), 16))
        scratch = [
            pltpu.VMEM((SLOTS, block, deep), jnp.bfloat16),
            pltpu.SemaphoreType.DMA((SLOTS, COPIES + 1)),
        ]
        cost = (2 * cols[1] * deep * slab, 2 * cols[1] * deep)
        room = 2 * SLOTS * block * deep + (slab * deep if part == 0 else 0)
        if slab > 2 * LANES:
            room += 3 * slab * deep + 4 * slab * total_shapes[part].shape[1]
        if part == 0:
            total, turned, send = local_call(
                functools.partial(lead_kernel, tuple(far_edges), cols, span),
                (
                    total_shapes[0],
                    jax.ShapeDtypeStruct((deep, slab), jnp.bfloat16),
                    send_shapes[0],
                ),
                "sv" + "a" * (len(far) + 2),
                (rep, near, *far, coupling, edge),
                [*turn_scratch, *scratch],
                cost=cost,
                room=room,
            )
        else:
            turned, _ = lax.optimization_barrier((turned, sends[0]))
            total, send = local_call(
                functools.partial(rest_kernel, cols, span),
                (total_shapes[part], send_shapes[part]),
                "svaa",
                (rep, turned, coupling, edge),
                scratch,
                cost=cost,
                room=room,
            )
        arrived = lax.ppermute(send, "rep", low_pairs)
        totals.append(total)
        got.append(arrived)
        sends.append(
            local_call(
                functools.partial(second_send_kernel, span),
                jax.ShapeDtypeStruct((width, bp, slab), jnp.int16),
                "svv",
                (rep, total, arrived),
            )
        )
    kept = [
        local_call(
            functools.partial(keep_kernel, span),
            jax.ShapeDtypeStruct((width, bp, slab), jnp.float32),
            "svv",
            (rep, total, arrived),
        )
        for span, bp, total, arrived in zip(spans, bps, totals, got)
    ]
    got = [lax.ppermute(send, "rep", high_pairs) for send in sends]

    groups = -(-width // (LANES // rows_dev))
    staged = []
    for part, span in enumerate(spans[:-1]):
        mine, _ = lax.optimization_barrier((kept[part], sends[-1]))
        staged.append(
            local_call(
                functools.partial(third_send_kernel, span[1], rows_dev),
                jax.ShapeDtypeStruct((grid_size, groups, bps[part], LANES), jnp.int16),
                "vv",
                (mine, got[part]),
            )
        )
    targets = local_call(
        functools.partial(last_send_kernel, counts[-1], rows_dev, len(counts)),
        (jax.ShapeDtypeStruct((groups, sum(bps), LANES), jnp.int16),) * grid_size,
        "vv" + "v" * len(staged),
        (kept[-1], got[-1], *staged),
        [pltpu.VMEM((grid_size, groups, bps[-1], LANES), jnp.int16)],
    )
    arrived = list(targets)
    for number in range(1, grid_size)[::-1]:
        arrived[number] = lax.ppermute(
            targets[number],
            "grid",
            [(walk[i], walk[(i + order[number]) % grid_size]) for i in range(grid_size)],
        )

    updated = local_call(
        functools.partial(update_kernel, counts, bps, width, rows_dev, order),
        jax.ShapeDtypeStruct((width, rows_dev, count * grid_size), jnp.float32),
        "sss" + "v" * (len(arrived) + 5),
        (
            me,
            occ_energy,
            occ_irrep,
            *arrived,
            jnp.transpose(integrals, (1, 0, 2)),
            row_energy[:, None],
            vir_energy[None, :],
            row_irrep[:, None],
            vir_irrep[None, :],
        ),
        [
            pltpu.VMEM((grid_size, groups, sum(bps), LANES), jnp.int16),
            pltpu.VMEM((count * grid_size, LANES), jnp.float32),
        ],
    )
    return jnp.transpose(updated, (1, 0, 2))


def solution(mesh):
    return jax.shard_map(
        body,
        mesh=mesh,
        in_specs=(
            P("grid", "rep"),
            P("rep", "grid"),
            P("grid", "rep", None),
            P("grid"),
            P("rep"),
            P(),
            P("grid"),
            P("rep"),
            P(),
        ),
        out_specs=P("grid", "rep", None),
        check_vma=False,
    )
```

```python
import functools

import jax
import jax.numpy as jnp
from jax import lax
from jax.experimental import pallas as pl
from jax.experimental.pallas import tpu as pltpu
from jax.sharding import PartitionSpec as P

NOCC = 60
LANES = 128
K_BLOCK = 3840
C_BLOCK = 320
SLOTS = 4
COPIES = 4
FIRST_PART = 47
STEPS = 8.0
TOP = 32767.0
MIB = 1024 * 1024


def ceil_to(value, unit):
    return -(-value // unit) * unit


def encode(rows, count):
    index = lax.broadcasted_iota(jnp.int32, rows.shape, 0)
    rows = jnp.where(index < count, rows, 0.0)
    largest = jnp.max(jnp.abs(rows), axis=0, keepdims=True)
    level = jnp.ceil(jnp.log2(jnp.maximum(largest, 1e-30)) * STEPS) + 1.0
    coded = jnp.floor(rows * (jnp.exp2(level * (-1.0 / STEPS)) * TOP) + 0.5)
    return jnp.where(index == count, level, coded)


def decode(block, count):
    index = lax.broadcasted_iota(jnp.int32, block.shape, 0)
    scale = jnp.exp2(block[count : count + 1] * (1.0 / STEPS)) * (1.0 / TOP)
    return jnp.where(index < count, block * scale, 0.0)


def to_code(block):
    return block.astype(jnp.int32).astype(jnp.int16)


def from_code(block):
    return block.astype(jnp.int32).astype(jnp.float32)


def walk_index(place, size):
    return jnp.where(place < size // 2, 2 * place, 2 * (size - 1 - place) + 1)


def walk_place(index, size):
    return jnp.where(index % 2 == 0, index // 2, size - 1 - index // 2)


def coupling_copies(coupling_ref, edge_ref, buffer, sems, low, start, slot):
    block = buffer.shape[1]
    whole = buffer.shape[2] - LANES
    rows = pl.ds(pl.multiple_of(low + start, 16), block)
    quarter = ceil_to(-(-whole // COPIES), 256)
    copies = []
    for number, k in enumerate(range(0, whole, quarter)):
        pairs = pl.ds(k, min(quarter, whole - k))
        copies.append(
            pltpu.make_async_copy(
                coupling_ref.at[rows, pairs], buffer.at[slot, :, pairs], sems.at[slot, number]
            )
        )
    copies.append(
        pltpu.make_async_copy(
            edge_ref.at[rows, :], buffer.at[slot, :, pl.ds(whole, LANES)], sems.at[slot, COPIES]
        )
    )
    return copies


def multiply(coupling_ref, edge_ref, buffer, sems, turned, total_ref, columns, before=None):
    low, many = columns
    block = buffer.shape[1]
    steps = -(-many // block)

    def copies(step):
        start = jnp.minimum(step * block, many - block)
        return coupling_copies(coupling_ref, edge_ref, buffer, sems, low, start, lax.rem(step, SLOTS))

    for ahead in range(min(SLOTS - 1, steps)):
        for copy in copies(jnp.int32(ahead)):
            copy.start()
    if before is not None:
        before()

    def step(number, carry):
        @pl.when(number + SLOTS - 1 < steps)
        def _():
            for copy in copies(number + SLOTS - 1):
                copy.start()

        for copy in copies(number):
            copy.wait()
        total = jnp.dot(
            buffer[lax.rem(number, SLOTS)], turned[...], preferred_element_type=jnp.float32
        )
        rows = pl.ds(pl.multiple_of(jnp.minimum(number * block, many - block), 4), block)
        for part in range(total_ref.shape[0]):
            total_ref[part, rows, :] = total[:, part * LANES : (part + 1) * LANES]
        return carry

    lax.fori_loop(0, steps, step, 0)


def turn_pieces(edges, pieces, gathered, sems, turned, lanes):
    rows = pieces[0].shape[0]
    slots = gathered.shape[0] // rows
    copies = []
    for number, (edge, piece) in enumerate(zip(edges, pieces)):
        target = gathered.at[
            pl.ds(number % slots * rows, rows), pl.ds(edge, piece.shape[1])
        ]
        copies.append(pltpu.make_async_copy(piece, target, sems.at[number]))
    for copy in copies:
        copy.start()
    for copy in copies:
        copy.wait()
    for at in range(0, turned.shape[0], LANES):
        turned[at : at + LANES, lanes : lanes + slots * rows] = gathered[:, at : at + LANES].T


def near_kernel(edges, *refs):
    *pieces, turned, gathered, sems = refs
    turn_pieces(edges, pieces, gathered, sems, turned, 0)


def lead_kernel(edges, columns, span, rep_ref, near, *refs):
    pieces, refs = refs[: len(edges)], refs[len(edges) :]
    coupling_ref, edge_ref, total, turned, send, gathered, sems, buffer, buffer_sems = refs

    def before():
        lanes = near.shape[1]
        turned[:, :lanes] = near[...]
        turn_pieces(edges, pieces, gathered, sems, turned, lanes)

    multiply(coupling_ref, edge_ref, buffer, buffer_sems, turned, total, columns, before)
    first_send(span, rep_ref, total, send)


def some_kernel(columns, turned, coupling_ref, edge_ref, total, buffer, sems):
    multiply(coupling_ref, edge_ref, buffer, sems, turned, total, columns)


def rest_kernel(columns, span, rep_ref, turned, begun, coupling_ref, edge_ref, *refs):
    total, send, buffer, sems = refs
    done = begun.shape[1]

    def before():
        total[:, :done, :] = begun[...]

    low, many = columns
    multiply(
        coupling_ref,
        edge_ref,
        buffer,
        sems,
        turned,
        total.at[:, done : done + many, :],
        columns,
        before,
    )
    first_send(span, rep_ref, total, send)


def column_rows(total_ref, width, part, j, offset, bp):
    rows = pl.ds(offset + part * width + j, bp, stride=NOCC)
    return jnp.concatenate([total_ref[h, rows, :] for h in range(total_ref.shape[0])], axis=1)


def first_send(span, rep_ref, total_ref, out_ref):
    offset, count, width = span
    low = rep_ref[0] % 2

    def step(j, carry):
        for high in range(2):
            rows = column_rows(total_ref, width, 2 * high + 1 - low, j, offset, out_ref.shape[2])
            out_ref[high, j] = to_code(encode(rows, count))
        return carry

    lax.fori_loop(0, width, step, 0)


def second_send_kernel(span, rep_ref, total_ref, got_ref, out_ref):
    offset, count, width = span
    low, high = rep_ref[0] % 2, 1 - rep_ref[0] // 2

    def step(j, carry):
        rows = column_rows(total_ref, width, 2 * high + low, j, offset, out_ref.shape[1])
        rows = rows + decode(from_code(got_ref[high, j]), count)
        out_ref[j] = to_code(encode(rows, count))
        return carry

    lax.fori_loop(0, width, step, 0)


def keep_kernel(span, rep_ref, total_ref, got_ref, out_ref):
    offset, count, width = span
    low, high = rep_ref[0] % 2, rep_ref[0] // 2

    def step(j, carry):
        rows = column_rows(total_ref, width, 2 * high + low, j, offset, out_ref.shape[1])
        out_ref[j] = rows + decode(from_code(got_ref[high, j]), count)
        return carry

    lax.fori_loop(0, width, step, 0)


def pack_rows(count, rows_dev, kept_ref, got_ref, stage):
    pack = LANES // rows_dev
    groups = stage.shape[1]
    size, _, slab = kept_ref.shape

    def step(jj, carry):
        coded = []
        for jq in range(pack):
            j = jnp.minimum(jq * groups + jj, size - 1)
            coded.append(encode(kept_ref[j] + decode(from_code(got_ref[j]), count), count))
        for g in range(slab // rows_dev):
            own = [block[:, g * rows_dev : (g + 1) * rows_dev] for block in coded]
            stage[g, jj] = to_code(jnp.concatenate(own, axis=1))
        return carry

    lax.fori_loop(0, groups, step, 0)


def third_send_kernel(count, rows_dev, kept_ref, got_ref, stage):
    pack_rows(count, rows_dev, kept_ref, got_ref, stage)


def last_send_kernel(count, rows_dev, parts, kept_ref, got_ref, *refs):
    earlier, targets, stage = refs[: parts - 1], refs[parts - 1 : -1], refs[-1]
    pack_rows(count, rows_dev, kept_ref, got_ref, stage)
    for number, target in enumerate(targets):
        at = 0
        for source in (*earlier, stage):
            bp = source.shape[2]
            target[:, at : at + bp, :] = source[number]
            at += bp


def update_kernel(counts, bps, width, rows_dev, order, me_ref, occ_energy_ref, occ_irrep_ref, *refs):
    (
        integrals_ref,
        row_energy_ref,
        vir_energy_ref,
        row_irrep_ref,
        vir_irrep_ref,
        out_ref,
        blocks,
        stage,
    ) = refs[-8:]
    arrived = refs[:-8]
    grid_size = len(arrived)
    place = walk_place(me_ref[0], grid_size)
    for offset, got_ref in zip(order, arrived):
        source = walk_index(lax.rem(place - offset + grid_size, grid_size), grid_size)
        blocks[source] = got_ref[...]
    pack = LANES // rows_dev
    for jj in range(blocks.shape[1]):
        at = 0
        for g in range(len(arrived)):
            row = 0
            for count, bp in zip(counts, bps):
                block = decode(from_code(blocks[g, jj, row : row + bp, :]), count)
                stage[at : at + count, :] = block[:count]
                at += count
                row += bp
        turned = stage[...].T
        for jq in range(pack):
            j = jq * blocks.shape[1] + jj
            if j >= width:
                continue
            cycle = turned[jq * rows_dev : (jq + 1) * rows_dev]
            denominator = row_energy_ref[...] + occ_energy_ref[j] - vir_energy_ref[...]
            labels = row_irrep_ref[...] ^ occ_irrep_ref[j] ^ vir_irrep_ref[...]
            out_ref[j] = jnp.where(
                labels == 0, (integrals_ref[j] + cycle) / denominator, jnp.float32(0.0)
            )


def local_call(kernel, out_shape, specs, args, scratch=(), aliases={}, cost=(10**7, 4 * 10**6), room=0):
    spaces = {"s": pltpu.SMEM, "v": pltpu.VMEM, "a": pl.ANY}
    return pl.pallas_call(
        kernel,
        out_shape=out_shape,
        in_specs=[pl.BlockSpec(memory_space=spaces[letter]) for letter in specs],
        out_specs=jax.tree.map(lambda _: pl.BlockSpec(memory_space=pltpu.VMEM), out_shape),
        scratch_shapes=list(scratch),
        input_output_aliases=aliases,
        compiler_params=pltpu.CompilerParams(vmem_limit_bytes=8 * MIB + room),
        cost_estimate=pl.CostEstimate(
            flops=cost[0], bytes_accessed=cost[1], transcendentals=0
        ),
        name=kernel.func.__name__,
    )(*args)


def body(
    amplitudes,
    coupling,
    integrals,
    row_energy,
    occ_energy,
    vir_energy,
    row_irrep,
    occ_irrep,
    vir_irrep,
):
    grid_size = lax.axis_size("grid")
    me = lax.axis_index("grid").astype(jnp.int32).reshape(1)
    rep = lax.axis_index("rep").astype(jnp.int32).reshape(1)
    rows_dev, depth = amplitudes.shape
    coupling = coupling.T
    columns = coupling.shape[0]
    count = columns // NOCC
    ragged = ceil_to(columns, 16) - columns
    if ragged:
        coupling = jnp.pad(coupling, ((0, ragged), (0, 0)))
        columns += ragged
    edge = depth % LANES
    edge = jnp.pad(coupling[:, depth - edge :], ((0, 0), (0, LANES - edge)))
    slab = rows_dev * grid_size
    width = NOCC // lax.axis_size("rep")

    walk = [*range(0, grid_size, 2), *range(1, grid_size, 2)[::-1]]
    onward = [(walk[i], walk[(i + 1) % grid_size]) for i in range(grid_size)]
    back = [(b, a) for a, b in onward]

    longer = grid_size // 2
    order = [0]
    for hop in range(1, longer):
        order += [-hop, hop]
    order.append(longer)
    near, far, near_edges, far_edges = [], [], [], []
    for number, at in enumerate(range(0, depth, K_BLOCK)):
        own = amplitudes[:, at : at + K_BLOCK]
        size = own.shape[1]
        own = jnp.pad(own, ((0, 0), (0, ceil_to(size, LANES) - size)))
        ahead = behind = own
        pieces = [own]
        for hop in range(1, longer + 1):
            if hop == longer:
                ahead, behind = lax.optimization_barrier((ahead, behind))
            if hop < longer or number % 2 == 0:
                ahead = lax.ppermute(ahead, "grid", onward)
                pieces.append(ahead)
            if hop < longer or number % 2 == 1:
                behind = lax.ppermute(behind, "grid", back)
                pieces.append(behind)
        near += pieces[:longer]
        far += pieces[longer:]
        near_edges += [at] * longer
        far_edges += [at] * longer

    counts = [FIRST_PART, count - FIRST_PART] if count > FIRST_PART else [count]
    firsts = [0, FIRST_PART][: len(counts)]
    bps = [ceil_to(number + 1, 16) for number in counts]
    lows = [first * NOCC // 16 * 16 for first in firsts]
    highs = [
        min(columns, ceil_to((first + number) * NOCC, 16)) for first, number in zip(firsts, counts)
    ]
    parts = [(low, high - low) for low, high in zip(lows, highs)]
    spans = [
        (first * NOCC - low, number, width) for first, low, number in zip(firsts, lows, counts)
    ]
    total_shapes = [
        jax.ShapeDtypeStruct((slab // LANES, max(span[0] + bp * NOCC, part[1]), LANES), jnp.float32)
        for span, part, bp in zip(spans, parts, bps)
    ]
    send_shapes = [jax.ShapeDtypeStruct((2, width, bp, slab), jnp.int16) for bp in bps]
    deep = ceil_to(depth, LANES)
    low_pairs = [(i, i ^ 1) for i in range(lax.axis_size("rep"))]
    high_pairs = [(i, i ^ 2) for i in range(lax.axis_size("rep"))]

    half = slab // 2
    turn_scratch = [
        pltpu.VMEM((half, deep), jnp.bfloat16),
        pltpu.SemaphoreType.DMA((len(near),)),
    ]
    near = local_call(
        functools.partial(near_kernel, tuple(near_edges)),
        jax.ShapeDtypeStruct((deep, half), jnp.bfloat16),
        "a" * len(near),
        near,
        turn_scratch,
        cost=(10**8, 4 * half * deep),
        room=2 * half * deep + (2 * half * deep if slab > 2 * LANES else 0),
    )
    totals, sends, got = [], [], []
    def buffers(many, steps):
        block = min(C_BLOCK, ceil_to(-(-many // steps), 16))
        scratch = [
            pltpu.VMEM((SLOTS, block, deep), jnp.bfloat16),
            pltpu.SemaphoreType.DMA((SLOTS, COPIES + 1)),
        ]
        return scratch, 2 * SLOTS * block * deep

    def work(many):
        return 2 * many * deep * slab, 2 * many * deep

    for part, (cols, span, bp) in enumerate(zip(parts, spans, bps)):
        low, many = cols
        if part == 0:
            scratch, room = buffers(many, 3)
            room += slab * deep
            if slab > 2 * LANES:
                room += 3 * slab * deep + 4 * slab * total_shapes[part].shape[1]
            total, turned, send = local_call(
                functools.partial(lead_kernel, tuple(far_edges), cols, span),
                (
                    total_shapes[0],
                    jax.ShapeDtypeStruct((deep, slab), jnp.bfloat16),
                    send_shapes[0],
                ),
                "sv" + "a" * (len(far) + 2),
                (rep, near, *far, coupling, edge),
                [*turn_scratch, *scratch],
                cost=work(many),
                room=room,
            )
            if len(parts) > 1:
                first, other = parts[1]
                begun_columns = other // 3 // 16 * 16
                scratch, room = buffers(begun_columns, 2)
                begun = local_call(
                    functools.partial(some_kernel, (first, begun_columns)),
                    jax.ShapeDtypeStruct((slab // LANES, begun_columns, LANES), jnp.float32),
                    "vaa",
                    (turned, coupling, edge),
                    scratch,
                    cost=work(begun_columns),
                    room=room,
                )
        else:
            turned, _ = lax.optimization_barrier((turned, sends[0]))
            rest_columns = (low + begun_columns, many - begun_columns)
            scratch, room = buffers(rest_columns[1], 3)
            total, send = local_call(
                functools.partial(rest_kernel, rest_columns, span),
                (total_shapes[part], send_shapes[part]),
                "svvaa",
                (rep, turned, begun, coupling, edge),
                scratch,
                cost=work(rest_columns[1]),
                room=room,
            )

        arrived = lax.ppermute(send, "rep", low_pairs)
        if part == 0 and len(parts) > 1:
            arrived, begun = lax.optimization_barrier((arrived, begun))
        totals.append(total)
        got.append(arrived)
        sends.append(
            local_call(
                functools.partial(second_send_kernel, span),
                jax.ShapeDtypeStruct((width, bp, slab), jnp.int16),
                "svv",
                (rep, total, arrived),
            )
        )
    kept = [
        local_call(
            functools.partial(keep_kernel, span),
            jax.ShapeDtypeStruct((width, bp, slab), jnp.float32),
            "svv",
            (rep, total, arrived),
        )
        for span, bp, total, arrived in zip(spans, bps, totals, got)
    ]
    got = [lax.ppermute(send, "rep", high_pairs) for send in sends]

    groups = -(-width // (LANES // rows_dev))
    staged = []
    for part, span in enumerate(spans[:-1]):
        mine, _ = lax.optimization_barrier((kept[part], sends[-1]))
        staged.append(
            local_call(
                functools.partial(third_send_kernel, span[1], rows_dev),
                jax.ShapeDtypeStruct((grid_size, groups, bps[part], LANES), jnp.int16),
                "vv",
                (mine, got[part]),
            )
        )
    targets = local_call(
        functools.partial(last_send_kernel, counts[-1], rows_dev, len(counts)),
        (jax.ShapeDtypeStruct((groups, sum(bps), LANES), jnp.int16),) * grid_size,
        "vv" + "v" * len(staged),
        (kept[-1], got[-1], *staged),
        [pltpu.VMEM((grid_size, groups, bps[-1], LANES), jnp.int16)],
    )
    arrived = list(targets)
    for number in range(1, grid_size)[::-1]:
        arrived[number] = lax.ppermute(
            targets[number],
            "grid",
            [(walk[i], walk[(i + order[number]) % grid_size]) for i in range(grid_size)],
        )

    updated = local_call(
        functools.partial(update_kernel, counts, bps, width, rows_dev, order),
        jax.ShapeDtypeStruct((width, rows_dev, count * grid_size), jnp.float32),
        "sss" + "v" * (len(arrived) + 5),
        (
            me,
            occ_energy,
            occ_irrep,
            *arrived,
            jnp.transpose(integrals, (1, 0, 2)),
            row_energy[:, None],
            vir_energy[None, :],
            row_irrep[:, None],
            vir_irrep[None, :],
        ),
        [
            pltpu.VMEM((grid_size, groups, sum(bps), LANES), jnp.int16),
            pltpu.VMEM((count * grid_size, LANES), jnp.float32),
        ],
    )
    return jnp.transpose(updated, (1, 0, 2))


def solution(mesh):
    return jax.shard_map(
        body,
        mesh=mesh,
        in_specs=(
            P("grid", "rep"),
            P("rep", "grid"),
            P("grid", "rep", None),
            P("grid"),
            P("rep"),
            P(),
            P("grid"),
            P("rep"),
            P(),
        ),
        out_specs=P("grid", "rep", None),
        check_vma=False,
    )
```

```python
import functools

import jax
import jax.numpy as jnp
from jax import lax
from jax.experimental import pallas as pl
from jax.experimental.pallas import tpu as pltpu
from jax.sharding import PartitionSpec as P

NOCC = 60
LANES = 128
K_BLOCK = 3840
C_BLOCK = 320
SLOTS = 4
COPIES = 4
FIRST_PART = 47
STEPS = 8.0
TOP = 32767.0
MIB = 1024 * 1024


def ceil_to(value, unit):
    return -(-value // unit) * unit


def encode(rows, count):
    index = lax.broadcasted_iota(jnp.int32, rows.shape, 0)
    rows = jnp.where(index < count, rows, 0.0)
    largest = jnp.max(jnp.abs(rows), axis=0, keepdims=True)
    level = jnp.ceil(jnp.log2(jnp.maximum(largest, 1e-30)) * STEPS) + 1.0
    coded = jnp.floor(rows * (jnp.exp2(level * (-1.0 / STEPS)) * TOP) + 0.5)
    return jnp.where(index == count, level, coded)


def decode(block, count):
    index = lax.broadcasted_iota(jnp.int32, block.shape, 0)
    scale = jnp.exp2(block[count : count + 1] * (1.0 / STEPS)) * (1.0 / TOP)
    return jnp.where(index < count, block * scale, 0.0)


def to_code(block):
    return block.astype(jnp.int32).astype(jnp.int16)


def from_code(block):
    return block.astype(jnp.int32).astype(jnp.float32)


def walk_index(place, size):
    return jnp.where(place < size // 2, 2 * place, 2 * (size - 1 - place) + 1)


def walk_place(index, size):
    return jnp.where(index % 2 == 0, index // 2, size - 1 - index // 2)


def coupling_copies(coupling_ref, edge_ref, buffer, sems, low, start, slot):
    block = buffer.shape[1]
    whole = buffer.shape[2] - LANES
    rows = pl.ds(pl.multiple_of(low + start, 16), block)
    quarter = ceil_to(-(-whole // COPIES), 256)
    copies = []
    for number, k in enumerate(range(0, whole, quarter)):
        pairs = pl.ds(k, min(quarter, whole - k))
        copies.append(
            pltpu.make_async_copy(
                coupling_ref.at[rows, pairs], buffer.at[slot, :, pairs], sems.at[slot, number]
            )
        )
    copies.append(
        pltpu.make_async_copy(
            edge_ref.at[rows, :], buffer.at[slot, :, pl.ds(whole, LANES)], sems.at[slot, COPIES]
        )
    )
    return copies


def multiply(coupling_ref, edge_ref, buffer, sems, turned, total_ref, columns, before=None):
    low, many = columns
    block = buffer.shape[1]
    steps = -(-many // block)

    def copies(step):
        start = jnp.minimum(step * block, many - block)
        return coupling_copies(coupling_ref, edge_ref, buffer, sems, low, start, lax.rem(step, SLOTS))

    for ahead in range(min(SLOTS - 1, steps)):
        for copy in copies(jnp.int32(ahead)):
            copy.start()
    if before is not None:
        before()

    def step(number, carry):
        @pl.when(number + SLOTS - 1 < steps)
        def _():
            for copy in copies(number + SLOTS - 1):
                copy.start()

        for copy in copies(number):
            copy.wait()
        total = jnp.dot(
            buffer[lax.rem(number, SLOTS)], turned[...], preferred_element_type=jnp.float32
        )
        rows = pl.ds(pl.multiple_of(jnp.minimum(number * block, many - block), 4), block)
        for part in range(total_ref.shape[0]):
            total_ref[part, rows, :] = total[:, part * LANES : (part + 1) * LANES]
        return carry

    lax.fori_loop(0, steps, step, 0)


def turn_pieces(edges, pieces, gathered, sems, turned, lanes):
    rows = pieces[0].shape[0]
    slots = gathered.shape[0] // rows
    copies = []
    for number, (edge, piece) in enumerate(zip(edges, pieces)):
        target = gathered.at[
            pl.ds(number % slots * rows, rows), pl.ds(edge, piece.shape[1])
        ]
        copies.append(pltpu.make_async_copy(piece, target, sems.at[number]))
    for copy in copies:
        copy.start()
    for copy in copies:
        copy.wait()
    for at in range(0, turned.shape[0], LANES):
        turned[at : at + LANES, lanes : lanes + slots * rows] = gathered[:, at : at + LANES].T


def near_kernel(edges, *refs):
    *pieces, turned, gathered, sems = refs
    turn_pieces(edges, pieces, gathered, sems, turned, 0)


def lead_kernel(edges, columns, span, rep_ref, near, *refs):
    pieces, refs = refs[: len(edges)], refs[len(edges) :]
    coupling_ref, edge_ref, total, turned, send, gathered, sems, buffer, buffer_sems = refs

    def before():
        lanes = near.shape[1]
        turned[:, :lanes] = near[...]
        turn_pieces(edges, pieces, gathered, sems, turned, lanes)

    multiply(coupling_ref, edge_ref, buffer, buffer_sems, turned, total, columns, before)
    first_send(span, rep_ref, total, send)


def some_kernel(columns, turned, coupling_ref, edge_ref, total, buffer, sems):
    multiply(coupling_ref, edge_ref, buffer, sems, turned, total, columns)


def rest_kernel(columns, span, rep_ref, turned, begun, coupling_ref, edge_ref, *refs):
    total, send, buffer, sems = refs
    done = begun.shape[1]

    def before():
        total[:, :done, :] = begun[...]

    low, many = columns
    multiply(
        coupling_ref,
        edge_ref,
        buffer,
        sems,
        turned,
        total.at[:, done : done + many, :],
        columns,
        before,
    )
    first_send(span, rep_ref, total, send)


def column_rows(total_ref, width, part, j, offset, bp):
    rows = pl.ds(offset + part * width + j, bp, stride=NOCC)
    return jnp.concatenate([total_ref[h, rows, :] for h in range(total_ref.shape[0])], axis=1)


def first_send(span, rep_ref, total_ref, out_ref):
    offset, count, width = span
    low = rep_ref[0] % 2

    def step(j, carry):
        for high in range(2):
            rows = column_rows(total_ref, width, 2 * high + 1 - low, j, offset, out_ref.shape[2])
            out_ref[high, j] = to_code(encode(rows, count))
        return carry

    lax.fori_loop(0, width, step, 0)


def second_send_kernel(span, rep_ref, total_ref, got_ref, out_ref):
    offset, count, width = span
    low, high = rep_ref[0] % 2, 1 - rep_ref[0] // 2

    def step(j, carry):
        rows = column_rows(total_ref, width, 2 * high + low, j, offset, out_ref.shape[1])
        rows = rows + decode(from_code(got_ref[high, j]), count)
        out_ref[j] = to_code(encode(rows, count))
        return carry

    lax.fori_loop(0, width, step, 0)


def keep_kernel(span, rep_ref, total_ref, got_ref, out_ref):
    offset, count, width = span
    low, high = rep_ref[0] % 2, rep_ref[0] // 2

    def step(j, carry):
        rows = column_rows(total_ref, width, 2 * high + low, j, offset, out_ref.shape[1])
        out_ref[j] = rows + decode(from_code(got_ref[high, j]), count)
        return carry

    lax.fori_loop(0, width, step, 0)


def pack_rows(count, rows_dev, kept_ref, got_ref, stage):
    pack = LANES // rows_dev
    groups = stage.shape[1]
    size, _, slab = kept_ref.shape

    def step(jj, carry):
        coded = []
        for jq in range(pack):
            j = jnp.minimum(jq * groups + jj, size - 1)
            coded.append(encode(kept_ref[j] + decode(from_code(got_ref[j]), count), count))
        for g in range(slab // rows_dev):
            own = [block[:, g * rows_dev : (g + 1) * rows_dev] for block in coded]
            stage[g, jj] = to_code(jnp.concatenate(own, axis=1))
        return carry

    lax.fori_loop(0, groups, step, 0)


def third_send_kernel(count, rows_dev, kept_ref, got_ref, stage):
    pack_rows(count, rows_dev, kept_ref, got_ref, stage)


def last_send_kernel(count, rows_dev, parts, kept_ref, got_ref, *refs):
    earlier, targets, stage = refs[: parts - 1], refs[parts - 1 : -1], refs[-1]
    pack_rows(count, rows_dev, kept_ref, got_ref, stage)
    for number, target in enumerate(targets):
        at = 0
        for source in (*earlier, stage):
            bp = source.shape[2]
            target[:, at : at + bp, :] = source[number]
            at += bp


def update_kernel(counts, bps, width, rows_dev, order, me_ref, occ_energy_ref, occ_irrep_ref, *refs):
    (
        integrals_ref,
        row_energy_ref,
        vir_energy_ref,
        row_irrep_ref,
        vir_irrep_ref,
        out_ref,
        blocks,
        stage,
    ) = refs[-8:]
    arrived = refs[:-8]
    grid_size = len(arrived)
    place = walk_place(me_ref[0], grid_size)
    for offset, got_ref in zip(order, arrived):
        source = walk_index(lax.rem(place - offset + grid_size, grid_size), grid_size)
        blocks[source] = got_ref[...]
    pack = LANES // rows_dev
    for jj in range(blocks.shape[1]):
        at = 0
        for g in range(len(arrived)):
            row = 0
            for count, bp in zip(counts, bps):
                block = decode(from_code(blocks[g, jj, row : row + bp, :]), count)
                stage[at : at + count, :] = block[:count]
                at += count
                row += bp
        turned = stage[...].T
        for jq in range(pack):
            j = jq * blocks.shape[1] + jj
            if j >= width:
                continue
            cycle = turned[jq * rows_dev : (jq + 1) * rows_dev]
            denominator = row_energy_ref[...] + occ_energy_ref[j] - vir_energy_ref[...]
            labels = row_irrep_ref[...] ^ occ_irrep_ref[j] ^ vir_irrep_ref[...]
            out_ref[j] = jnp.where(
                labels == 0, (integrals_ref[j] + cycle) / denominator, jnp.float32(0.0)
            )


def local_call(kernel, out_shape, specs, args, scratch=(), aliases={}, cost=(10**7, 4 * 10**6), room=0):
    spaces = {"s": pltpu.SMEM, "v": pltpu.VMEM, "a": pl.ANY}
    return pl.pallas_call(
        kernel,
        out_shape=out_shape,
        in_specs=[pl.BlockSpec(memory_space=spaces[letter]) for letter in specs],
        out_specs=jax.tree.map(lambda _: pl.BlockSpec(memory_space=pltpu.VMEM), out_shape),
        scratch_shapes=list(scratch),
        input_output_aliases=aliases,
        compiler_params=pltpu.CompilerParams(vmem_limit_bytes=8 * MIB + room),
        cost_estimate=pl.CostEstimate(
            flops=cost[0], bytes_accessed=cost[1], transcendentals=0
        ),
        name=kernel.func.__name__,
    )(*args)


def body(
    amplitudes,
    coupling,
    integrals,
    row_energy,
    occ_energy,
    vir_energy,
    row_irrep,
    occ_irrep,
    vir_irrep,
):
    grid_size = lax.axis_size("grid")
    me = lax.axis_index("grid").astype(jnp.int32).reshape(1)
    rep = lax.axis_index("rep").astype(jnp.int32).reshape(1)
    rows_dev, depth = amplitudes.shape
    coupling = coupling.T
    columns = coupling.shape[0]
    count = columns // NOCC
    ragged = ceil_to(columns, 16) - columns
    if ragged:
        coupling = jnp.pad(coupling, ((0, ragged), (0, 0)))
        columns += ragged
    edge = depth % LANES
    edge = jnp.pad(coupling[:, depth - edge :], ((0, 0), (0, LANES - edge)))
    slab = rows_dev * grid_size
    width = NOCC // lax.axis_size("rep")

    walk = [*range(0, grid_size, 2), *range(1, grid_size, 2)[::-1]]
    onward = [(walk[i], walk[(i + 1) % grid_size]) for i in range(grid_size)]
    back = [(b, a) for a, b in onward]

    longer = grid_size // 2
    order = [0]
    for hop in range(1, longer):
        order += [-hop, hop]
    order.append(longer)
    near, far, near_edges, far_edges = [], [], [], []
    for number, at in enumerate(range(0, depth, K_BLOCK)):
        own = amplitudes[:, at : at + K_BLOCK]
        size = own.shape[1]
        own = jnp.pad(own, ((0, 0), (0, ceil_to(size, LANES) - size)))
        ahead = behind = own
        pieces = [own]
        for hop in range(1, longer + 1):
            if hop == longer:
                ahead, behind = lax.optimization_barrier((ahead, behind))
            if hop < longer or number % 2 == 0:
                ahead = lax.ppermute(ahead, "grid", onward)
                pieces.append(ahead)
            if hop < longer or number % 2 == 1:
                behind = lax.ppermute(behind, "grid", back)
                pieces.append(behind)
        near += pieces[:longer]
        far += pieces[longer:]
        near_edges += [at] * longer
        far_edges += [at] * longer

    counts = [FIRST_PART, count - FIRST_PART] if count > FIRST_PART else [count]
    firsts = [0, FIRST_PART][: len(counts)]
    bps = [ceil_to(number + 1, 16) for number in counts]
    lows = [first * NOCC // 16 * 16 for first in firsts]
    highs = [
        min(columns, ceil_to((first + number) * NOCC, 16)) for first, number in zip(firsts, counts)
    ]
    parts = [(low, high - low) for low, high in zip(lows, highs)]
    spans = [
        (first * NOCC - low, number, width) for first, low, number in zip(firsts, lows, counts)
    ]
    total_shapes = [
        jax.ShapeDtypeStruct((slab // LANES, max(span[0] + bp * NOCC, part[1]), LANES), jnp.float32)
        for span, part, bp in zip(spans, parts, bps)
    ]
    send_shapes = [jax.ShapeDtypeStruct((2, width, bp, slab), jnp.int16) for bp in bps]
    deep = ceil_to(depth, LANES)
    low_pairs = [(i, i ^ 1) for i in range(lax.axis_size("rep"))]
    high_pairs = [(i, i ^ 2) for i in range(lax.axis_size("rep"))]

    half = slab // 2
    turn_scratch = [
        pltpu.VMEM((half, deep), jnp.bfloat16),
        pltpu.SemaphoreType.DMA((len(near),)),
    ]
    near = local_call(
        functools.partial(near_kernel, tuple(near_edges)),
        jax.ShapeDtypeStruct((deep, half), jnp.bfloat16),
        "a" * len(near),
        near,
        turn_scratch,
        cost=(10**8, 4 * half * deep),
        room=2 * half * deep + (2 * half * deep if slab > 2 * LANES else 0),
    )
    totals, sends, got = [], [], []
    def buffers(many, steps):
        block = min(C_BLOCK, ceil_to(-(-many // steps), 16))
        scratch = [
            pltpu.VMEM((SLOTS, block, deep), jnp.bfloat16),
            pltpu.SemaphoreType.DMA((SLOTS, COPIES + 1)),
        ]
        return scratch, 2 * SLOTS * block * deep

    def work(many):
        return 2 * many * deep * slab, 2 * many * deep

    for part, (cols, span, bp) in enumerate(zip(parts, spans, bps)):
        low, many = cols
        if part == 0:
            scratch, room = buffers(many, 3)
            room += slab * deep
            if slab > 2 * LANES:
                room += 3 * slab * deep + 4 * slab * total_shapes[part].shape[1]
            total, turned, send = local_call(
                functools.partial(lead_kernel, tuple(far_edges), cols, span),
                (
                    total_shapes[0],
                    jax.ShapeDtypeStruct((deep, slab), jnp.bfloat16),
                    send_shapes[0],
                ),
                "sv" + "a" * (len(far) + 2),
                (rep, near, *far, coupling, edge),
                [*turn_scratch, *scratch],
                cost=work(many),
                room=room,
            )
            if len(parts) > 1:
                first, other = parts[1]
                begun_columns = other * 9 // 40 // 16 * 16
                scratch, room = buffers(begun_columns, 1)
                begun = local_call(
                    functools.partial(some_kernel, (first, begun_columns)),
                    jax.ShapeDtypeStruct((slab // LANES, begun_columns, LANES), jnp.float32),
                    "vaa",
                    (turned, coupling, edge),
                    scratch,
                    cost=work(begun_columns),
                    room=room,
                )
        else:
            turned, _ = lax.optimization_barrier((turned, sends[0]))
            rest_columns = (low + begun_columns, many - begun_columns)
            scratch, room = buffers(rest_columns[1], 3)
            total, send = local_call(
                functools.partial(rest_kernel, rest_columns, span),
                (total_shapes[part], send_shapes[part]),
                "svvaa",
                (rep, turned, begun, coupling, edge),
                scratch,
                cost=work(rest_columns[1]),
                room=room,
            )

        arrived = lax.ppermute(send, "rep", low_pairs)
        if part == 0 and len(parts) > 1:
            arrived, begun = lax.optimization_barrier((arrived, begun))
        totals.append(total)
        got.append(arrived)
        sends.append(
            local_call(
                functools.partial(second_send_kernel, span),
                jax.ShapeDtypeStruct((width, bp, slab), jnp.int16),
                "svv",
                (rep, total, arrived),
            )
        )
    kept = [
        local_call(
            functools.partial(keep_kernel, span),
            jax.ShapeDtypeStruct((width, bp, slab), jnp.float32),
            "svv",
            (rep, total, arrived),
        )
        for span, bp, total, arrived in zip(spans, bps, totals, got)
    ]
    got = [lax.ppermute(send, "rep", high_pairs) for send in sends]

    groups = -(-width // (LANES // rows_dev))
    staged = []
    for part, span in enumerate(spans[:-1]):
        mine, _ = lax.optimization_barrier((kept[part], sends[-1]))
        staged.append(
            local_call(
                functools.partial(third_send_kernel, span[1], rows_dev),
                jax.ShapeDtypeStruct((grid_size, groups, bps[part], LANES), jnp.int16),
                "vv",
                (mine, got[part]),
            )
        )
    targets = local_call(
        functools.partial(last_send_kernel, counts[-1], rows_dev, len(counts)),
        (jax.ShapeDtypeStruct((groups, sum(bps), LANES), jnp.int16),) * grid_size,
        "vv" + "v" * len(staged),
        (kept[-1], got[-1], *staged),
        [pltpu.VMEM((grid_size, groups, bps[-1], LANES), jnp.int16)],
    )
    arrived = list(targets)
    for number in range(1, grid_size)[::-1]:
        arrived[number] = lax.ppermute(
            targets[number],
            "grid",
            [(walk[i], walk[(i + order[number]) % grid_size]) for i in range(grid_size)],
        )

    updated = local_call(
        functools.partial(update_kernel, counts, bps, width, rows_dev, order),
        jax.ShapeDtypeStruct((width, rows_dev, count * grid_size), jnp.float32),
        "sss" + "v" * (len(arrived) + 5),
        (
            me,
            occ_energy,
            occ_irrep,
            *arrived,
            jnp.transpose(integrals, (1, 0, 2)),
            row_energy[:, None],
            vir_energy[None, :],
            row_irrep[:, None],
            vir_irrep[None, :],
        ),
        [
            pltpu.VMEM((grid_size, groups, sum(bps), LANES), jnp.int16),
            pltpu.VMEM((count * grid_size, LANES), jnp.float32),
        ],
    )
    return jnp.transpose(updated, (1, 0, 2))


def solution(mesh):
    return jax.shard_map(
        body,
        mesh=mesh,
        in_specs=(
            P("grid", "rep"),
            P("rep", "grid"),
            P("grid", "rep", None),
            P("grid"),
            P("rep"),
            P(),
            P("grid"),
            P("rep"),
            P(),
        ),
        out_specs=P("grid", "rep", None),
        check_vma=False,
    )
```
